32 devices in a mesh: sub: 8 (over y, x, core), alt: 4 (over z).
Axes of the slice: x: 2, y: 2, z: 4, core: 2. Of those that a mesh axis runs over, the one named last changes fastest.
Arguments:
- cotangent: bfloat16 [4096, 1024], P('alt', 'sub'), may hold values from -180 to 180, as said below
- amplitude: bfloat16 [1024, 1024], P('alt', 'sub'), may hold values from 0.19921875 to 1
- phase: float32 [1024, 1024], P('alt', 'sub'), may hold values from -6 to 6
- position: float32 [2, 1024], P(None, 'sub'), may hold values from -1 to 1
- profile: float32 [8], P('alt'), may hold values from 0.35 to 15, as said below
- alt_weight: float32 [8], P('alt'), may hold values from 0.3 to 3
Outputs:
- phase_grad: float32 [1024, 1024], P('alt', 'sub')
- profile_grad: float32 [8], P('alt')
The draws below stay inside these ranges and needn't reach their ends.
Inputs may be any that keep to these rules, and one draw needn't show every extreme that they name: `cotangent`: cotangent values of varying scale per subaperture. `profile`: positive sodium densities.
All inputs are finite; a program needn't handle non-finite values.
Results may differ from the reference program's by a relative error of at most 0.0003.
Values may be sent and summed in bfloat16 or wider, within the bound.
No kernel may reach another device: no remote copies, remote signals or barrier semaphores. Data moves between devices by JAX's collectives and lax.ppermute only.
A program may use at most 64 MiB of HBM per device.

```python
import math
import jax
import jax.numpy as jnp
from jax import lax

P_SIZE = 32
FIELD = 64
NSUB = 1024
NBINS = 8


def draw_cotangent(key, part):
    key_a = jax.random.fold_in(key, 11)
    key_b = jax.random.fold_in(key, 12)
    ramp = jnp.arange(NSUB, dtype=jnp.float32) / (NSUB - 1)
    spread = jnp.exp(jax.random.uniform(key_b, (NSUB,), jnp.float32) * jnp.log(10.0))
    base = jnp.clip(jax.random.normal(key_a, (FIELD * FIELD, NSUB), jnp.float32), -6.0, 6.0)
    values = base * (3.0 ** ramp * spread)[None, :]
    return values.astype(jnp.bfloat16)


def draw_profile(key, part):
    key_a = jax.random.fold_in(key, 21)
    ramp = jnp.arange(NBINS, dtype=jnp.float32) / (NBINS - 1)
    values = 3.0 ** ramp * jnp.exp(jax.random.uniform(key_a, (NBINS,), jnp.float32, -1.0, 1.0))
    return values


def level_of(own_key, shape, cuts, smallest, top_value):
    def one(dim, parts):
        heights = jax.random.uniform(jax.random.fold_in(jax.random.fold_in(own_key, 6), dim), (parts,), jnp.float32, smallest / len(cuts), top_value / len(cuts))
        return jnp.repeat(jnp.exp(heights), shape[dim] // parts).reshape((-1,) + (1,) * (len(shape) - dim - 1))

    level = one(*cuts[0])
    for cut in cuts[1:]:
        level = level * one(*cut)
    return level


def bell_draw(rng, dims, deviation, most, split=(), kind=jnp.bfloat16):
    values = jax.random.normal(rng, dims, jnp.float32) * deviation
    if len(split) > 0:
        values = level_of(rng, dims, split, -0.22, 0.18) * values
    return jnp.clip(values, min=-most, max=most).astype(kind)


def setup_inputs(seed: int = 0) -> dict:
    key_list = jax.random.split(jax.random.key(seed), 7)
    cotangent = draw_cotangent(jax.random.fold_in(key_list[6], 71), 0)
    amplitude = jnp.clip(0.19921875 + 0.80078125 * jax.random.uniform(key_list[1], (P_SIZE * P_SIZE, NSUB), jnp.float32) ** level_of(key_list[1], (P_SIZE * P_SIZE, NSUB), ((0, 4), (1, 8)), -0.2, 0.2), 0.19921875, 1.0).astype(jnp.bfloat16)
    phase = bell_draw(key_list[2], (P_SIZE * P_SIZE, NSUB), 1.0, 6.0, ((0, 4), (1, 8)), jnp.float32)
    position = jnp.clip(jax.random.uniform(key_list[3], (2, NSUB), jnp.float32, -1.0, 1.0) * level_of(key_list[3], (2, NSUB), ((1, 8),), -0.4, 0.0), -1.0, 1.0)
    profile = draw_profile(jax.random.fold_in(key_list[6], 71), 0)
    alt_weight = jnp.clip(jnp.exp(math.log(3.0) - 2.3025851 * jax.random.uniform(key_list[5], (NBINS,), jnp.float32) ** level_of(key_list[5], (NBINS,), ((0, 4),), -0.2, 0.2)), 0.3, 3.0)
    return dict(cotangent=cotangent, amplitude=amplitude, phase=phase, position=position, profile=profile, alt_weight=alt_weight)


ELONG = 0.75

def dft_tables(size_pupil, size_field):
    rows = jnp.arange(size_field, dtype=jnp.int32)[:, None]
    cols = jnp.arange(size_pupil, dtype=jnp.int32)[None, :]
    angle = 2.0 * jnp.pi / size_field * (rows * cols % size_field).astype(jnp.float32)
    return (jnp.cos(angle), -jnp.sin(angle))

def spot_image(psi, ampl, table_re, table_im, size_pupil):
    high = lax.Precision.HIGHEST
    field_re = ampl * jnp.cos(psi)
    field_im = ampl * jnp.sin(psi)
    first_re = jnp.einsum('kj,ajs->aks', table_re, field_re, precision=high) - jnp.einsum('kj,ajs->aks', table_im, field_im, precision=high)
    first_im = jnp.einsum('kj,ajs->aks', table_re, field_im, precision=high) + jnp.einsum('kj,ajs->aks', table_im, field_re, precision=high)
    final_re = jnp.einsum('ka,ams->kms', table_re, first_re, precision=high) - jnp.einsum('ka,ams->kms', table_im, first_im, precision=high)
    final_im = jnp.einsum('ka,ams->kms', table_re, first_im, precision=high) + jnp.einsum('ka,ams->kms', table_im, first_re, precision=high)
    return (final_re * final_re + final_im * final_im) / (size_pupil * size_pupil)

def reference(cotangent, amplitude, phase, position, profile, alt_weight):
    nsub_all = phase.shape[1]
    nbins_all = profile.shape[0]
    grad_img = cotangent.astype(jnp.float32).reshape(FIELD, FIELD, nsub_all)
    ampl = amplitude.astype(jnp.float32).reshape(P_SIZE, P_SIZE, nsub_all)
    phases = phase.reshape(P_SIZE, P_SIZE, nsub_all)
    table_re, table_im = dft_tables(P_SIZE, FIELD)
    coord = jnp.arange(P_SIZE, dtype=jnp.float32) - (P_SIZE - 1) / 2.0
    tilt = coord[None, :, None] * position[0][None, None, :] + coord[:, None, None] * position[1][None, None, :]
    total = jnp.sum(profile)

    def step(accum, index):
        kappa = ELONG * (2.0 * index.astype(jnp.float32) / (nbins_all - 1) - 1.0)
        psi = phases + kappa * tilt
        intensity, pull = jax.vjp(lambda value: spot_image(value, ampl, table_re, table_im, P_SIZE), psi)
        dpsi, = pull(profile[index] * alt_weight[index] * grad_img)
        stat = jnp.sum(grad_img * intensity)
        return (accum + dpsi, stat)
    accum, stats = lax.scan(step, jnp.zeros((P_SIZE, P_SIZE, nsub_all), jnp.float32), jnp.arange(nbins_all, dtype=jnp.int32))
    phase_grad = (accum / total).reshape(P_SIZE * P_SIZE, nsub_all)
    centre = jnp.sum(profile * alt_weight * stats)
    profile_grad = (alt_weight * stats / total - centre / (total * total)) / nsub_all
    return (phase_grad, profile_grad)
```

```python
import functools
import math

import jax
import jax.numpy as jnp
import ml_dtypes
import numpy as np
from jax import lax
from jax.experimental import pallas as pl
from jax.experimental.pallas import tpu as pltpu
from jax.sharding import PartitionSpec as P

ELONG = 0.75
LANES = 128
VMEM_LIMIT = 48 * 1024 * 1024
F32 = jnp.float32
BF16 = jnp.bfloat16


def dft_matrix(pupil, field):
    angle = 2.0 * np.pi / field * (np.outer(np.arange(field), np.arange(pupil)) % field)
    c, s = np.cos(angle), np.sin(angle)
    return np.block([[c, s], [-s, c]])


def table_three(matrix):
    hi = matrix.astype(np.float32).astype(ml_dtypes.bfloat16)
    lo = (matrix - hi.astype(np.float64)).astype(np.float32).astype(ml_dtypes.bfloat16)
    return np.concatenate([hi, lo, hi], axis=1)


def split_three(x):
    hi = x.astype(BF16)
    lo = (x - hi.astype(F32)).astype(BF16)
    return jnp.concatenate([hi, hi, lo], axis=0)


def dot(a, b):
    return jnp.dot(a, b, preferred_element_type=F32)


def lane_group(shape, width):
    return lax.broadcasted_iota(jnp.int32, shape, len(shape) - 1) // width


def roll(x, shift):
    return pltpu.roll(x, shift % LANES, x.ndim - 1)


def swap_groups(blocks, width):
    n = len(blocks)
    blocks = list(blocks)
    group = lane_group(blocks[0].shape, width)
    step = 1
    while step < n:
        low = (group & step) == 0
        for i in range(n):
            if i & step:
                continue
            j = i + step
            a, b = blocks[i], blocks[j]
            blocks[i] = jnp.where(low, a, roll(b, step * width))
            blocks[j] = jnp.where(low, roll(a, -step * width), b)
        step *= 2
    return blocks


def spread_groups(x, n, width):
    group = lane_group(x.shape, width)
    out = [x]
    step = n // 2
    while step >= 1:
        low = (group & step) == 0
        made = []
        for y in out:
            up, down = roll(y, step * width), roll(y, -step * width)
            made.append(jnp.where(low, y, up))
            made.append(jnp.where(low, down, y))
        out = made
        step //= 2
    return out


def pack_kernel(n, nb, profile_ref, weight_ref, cot_ref, amp_ref, phase_ref, early_ref, late_ref):
    width = LANES // n
    qp = phase_ref.shape[0] // n
    qc = cot_ref.shape[0] // n
    blocks = swap_groups([phase_ref[a * qp : (a + 1) * qp, :] for a in range(n)], width)
    for d in range(n):
        hi = blocks[d].astype(BF16)
        early_ref[d, 0:qp, :] = hi
        early_ref[d, qp : 2 * qp, :] = (blocks[d] - hi.astype(F32)).astype(BF16)
    blocks = swap_groups([amp_ref[a * qp : (a + 1) * qp, :].astype(F32) for a in range(n)], width)
    for d in range(n):
        early_ref[d, 2 * qp : 3 * qp, :] = blocks[d].astype(BF16)
    rows = early_ref.shape[1] - 3 * qp
    row = lax.broadcasted_iota(jnp.int32, (rows, LANES), 0)
    extra = jnp.zeros((rows, LANES), F32)
    for j in range(nb):
        for k, ref in enumerate((profile_ref, weight_ref)):
            value = jnp.full((rows, LANES), ref[j], F32)
            for part in range(3):
                piece = value.astype(BF16).astype(F32)
                extra = jnp.where(row == (2 * j + k) * 3 + part, piece, extra)
                value = value - piece
    for d in range(n):
        early_ref[d, 3 * qp :, :] = extra.astype(BF16)

    def step(i, carry):
        at = pl.multiple_of(i * 16, 16)
        parts = [cot_ref[pl.ds(a * qc + at, 16), :].astype(F32) for a in range(n)]
        for d, block in enumerate(swap_groups(parts, width)):
            late_ref[d, pl.ds(at, 16), :] = block.astype(BF16)
        return carry

    lax.fori_loop(0, qc // 16, step, 0, unroll=2)


def sincos(x):
    turns = jnp.round(x * (2.0 / math.pi))
    r = x - turns * 1.5703125
    r = r - turns * 4.838267948966e-4
    r2 = r * r
    s = r + r * r2 * (-1.6666654611e-1 + r2 * (8.3321608736e-3 + r2 * -1.9515295891e-4))
    c = (1.0 - 0.5 * r2) + r2 * r2 * (
        4.166664568298827e-2 + r2 * (-1.388731625493765e-3 + r2 * 2.443315711809948e-5)
    )
    quad = turns.astype(jnp.int32)
    odd = (quad & 1) != 0
    sin_v = jnp.where(odd, c, s)
    cos_v = jnp.where(odd, s, c)
    sin_v = jnp.where((quad & 2) != 0, -sin_v, sin_v)
    cos_v = jnp.where(((quad + 1) & 2) != 0, -cos_v, cos_v)
    return sin_v, cos_v


def main_kernel(
    n,
    nb,
    pupil,
    field,
    me_ref,
    pos_ref,
    early_ref,
    late_ref,
    fwd_ref,
    bwd_ref,
    grad_ref,
    aux_ref,
    phase_s,
    amp_s,
    e_s,
    f_s,
    g_s,
    pg_s,
):
    width = LANES // n
    nbins = n * nb
    qp = pupil * pupil // (n * n)
    qc = field * field // (n * n)
    group1 = lane_group((1, LANES), width)

    pos = pos_ref[...]
    me = me_ref[0]
    near = jnp.zeros_like(pos)
    for d in range(n):
        near = jnp.where(me == d, spread_groups(pos, n, width)[d], near)

    prof, wgt = [], []
    for t in range(nb):
        p_row, w_row = jnp.zeros((1, LANES), F32), jnp.zeros((1, LANES), F32)
        for d in range(n):
            extra = early_ref[d, 3 * qp :, :].astype(F32)
            p_d = sum(extra[(2 * t) * 3 + part : (2 * t) * 3 + part + 1, :] for part in (0, 1, 2))
            w_d = sum(
                extra[(2 * t + 1) * 3 + part : (2 * t + 1) * 3 + part + 1, :] for part in (0, 1, 2)
            )
            p_row = jnp.where(group1 == d, p_d, p_row)
            w_row = jnp.where(group1 == d, w_d, w_row)
        prof.append(p_row)
        wgt.append(w_row)
    total = sum(prof)
    step = n // 2
    while step >= 1:
        total = total + roll(total, step * width)
        step //= 2
    coef = [2.0 / (pupil * pupil) * prof[t] * wgt[t] / total for t in range(nb)]
    kappa = [
        ELONG * (2.0 * (group1 * nb + t).astype(F32) / (nbins - 1) - 1.0) for t in range(nb)
    ]
    tilt_x = [kappa[t] * near[0:1, :] for t in range(nb)]
    tilt_y = [kappa[t] * near[1:2, :] for t in range(nb)]

    def unpack(d, carry):
        for q in range(0, qp, 16):
            hi = early_ref[d, q : q + 16, :].astype(F32)
            lo = early_ref[d, qp + q : qp + q + 16, :].astype(F32)
            am = early_ref[d, 2 * qp + q : 2 * qp + q + 16, :].astype(F32)
            for a, (one, two) in enumerate(
                zip(spread_groups(hi + lo, n, width), spread_groups(am, n, width))
            ):
                at = pl.multiple_of((d * n + a) * qp + q, 16)
                phase_s[pl.ds(at, 16), :] = one
                amp_s[pl.ds(at, 16), :] = two
        return carry

    lax.fori_loop(0, n, unpack, 0)

    v_rows = lax.broadcasted_iota(jnp.int32, (pupil, LANES), 0).astype(F32) - (pupil - 1) / 2.0
    swing = [v_rows * tilt_y[t] for t in range(nb)]
    fwd = fwd_ref[...]
    bwd = bwd_ref[...]

    def first(i, carry):
        for k in range(4):
            c = i * 4 + k
            u = c.astype(F32) - (pupil - 1) / 2.0
            ph = phase_s[pl.ds(c, pupil, stride=pupil), :]
            am = amp_s[pl.ds(c, pupil, stride=pupil), :]
            fields = []
            for t in range(nb):
                sin_v, cos_v = sincos(ph + (u * tilt_x[t] + swing[t]))
                e = jnp.concatenate([am * cos_v, am * sin_v], axis=0)
                e_s[t, pl.ds(pl.multiple_of(c * 2 * pupil, 2 * pupil), 2 * pupil), :] = e
                fields.append(split_three(e))
            out = dot(fwd, jnp.concatenate(fields, axis=1))
            for t in range(nb):
                f_s[t, pl.ds(pl.multiple_of(c * 2 * field, 2 * field), 2 * field), :] = out[
                    :, t * LANES : (t + 1) * LANES
                ]
        return carry

    lax.fori_loop(0, pupil // 4, first, 0)

    per = qc // field

    def middle(i, carry):
        d, j = i // per, i % per
        raw = late_ref[d, pl.ds(pl.multiple_of(j * field, field), field), :].astype(F32)
        for a, cot in enumerate(spread_groups(raw, n, width)):
            k1 = (d * n + a) * per + j
            parts = []
            for t in range(nb):
                re = f_s[t, pl.ds(k1, pupil, stride=2 * field), :]
                im = f_s[t, pl.ds(k1 + field, pupil, stride=2 * field), :]
                parts.append(split_three(jnp.concatenate([re, im], axis=0)))
            image = dot(fwd, jnp.concatenate(parts, axis=1))
            both = jnp.concatenate([cot, cot], axis=0)
            parts = [
                split_three(image[:, t * LANES : (t + 1) * LANES] * both) for t in range(nb)
            ]
            back = dot(bwd, jnp.concatenate(parts, axis=1))
            for t in range(nb):
                g_s[t, pl.ds(pl.multiple_of(k1 * 2 * pupil, 2 * pupil), 2 * pupil), :] = back[
                    :, t * LANES : (t + 1) * LANES
                ]
        return carry

    lax.fori_loop(0, n * per, middle, 0)

    def last(i, stats):
        stats = list(stats)
        for k in range(4):
            c = i * 4 + k
            parts = []
            for t in range(nb):
                re = g_s[t, pl.ds(c, field, stride=2 * pupil), :]
                im = g_s[t, pl.ds(c + pupil, field, stride=2 * pupil), :]
                parts.append(split_three(jnp.concatenate([re, im], axis=0)))
            out = dot(bwd, jnp.concatenate(parts, axis=1))
            grad = jnp.zeros((pupil, LANES), F32)
            for t in range(nb):
                g = out[:, t * LANES : (t + 1) * LANES]
                e = e_s[t, pl.ds(pl.multiple_of(c * 2 * pupil, 2 * pupil), 2 * pupil), :]
                g_re, g_im = g[:pupil], g[pupil:]
                e_re, e_im = e[:pupil], e[pupil:]
                stats[t] = stats[t] + (e_re * g_re + e_im * g_im)
                grad = grad + coef[t] * (e_re * g_im - e_im * g_re)
            step = n // 2
            while step >= 1:
                grad = grad + roll(grad, step * width)
                step //= 2
            pg_s[pl.ds(c, pupil, stride=pupil), :] = grad
        return tuple(stats)

    stats = lax.fori_loop(
        0, pupil // 4, last, tuple(jnp.zeros((pupil, LANES), F32) for _ in range(nb))
    )

    aux = jnp.zeros(aux_ref.shape, F32)
    row = lax.broadcasted_iota(jnp.int32, aux_ref.shape, 0)
    for t in range(nb):
        stat = jnp.sum(stats[t], axis=0, keepdims=True) * (1.0 / (pupil * pupil))
        aux = jnp.where(row == t, stat, aux)
        aux = jnp.where(row == nb + t, prof[t], aux)
        aux = jnp.where(row == 2 * nb + t, wgt[t], aux)
    aux_ref[...] = jnp.where(row == 3 * nb, total, aux)

    def repack(d, carry):
        for q in range(0, qp, 8):
            out = jnp.zeros((8, LANES), F32)
            group = lane_group((8, LANES), width)
            for a in range(n):
                at = pl.multiple_of((d * n + a) * qp + q, 8)
                out = jnp.where(group == a, pg_s[pl.ds(at, 8), :], out)
            grad_ref[d, q : q + 8, :] = out
        return carry

    lax.fori_loop(0, n, repack, 0)


def final_kernel(n, nb, nsub_all, me_ref, grad_ref, stat_ref, aux_ref, out_ref, prof_ref):
    width = LANES // n
    qp = grad_ref.shape[1]
    for a, block in enumerate(swap_groups([grad_ref[d] for d in range(n)], width)):
        out_ref[a * qp : (a + 1) * qp, :] = block
    group = lane_group((1, LANES), width)
    mine = group == me_ref[0]
    stat = stat_ref[...]
    aux = aux_ref[...]
    total = jnp.max(aux[3 * nb : 3 * nb + 1, :])
    centre = jnp.float32(0.0)
    for t in range(nb):
        centre += jnp.sum(
            stat[t : t + 1] * aux[nb + t : nb + t + 1] * aux[2 * nb + t : 2 * nb + t + 1]
        )
    for t in range(nb):
        own = jnp.sum(
            jnp.where(mine, stat[t : t + 1] * aux[2 * nb + t : 2 * nb + t + 1], 0.0)
        )
        prof_ref[t] = (own / total - centre / (total * total)) / nsub_all


def local(cotangent, amplitude, phase, position, profile, alt_weight):
    n = lax.axis_size("alt")
    count = phase.shape[1]
    nsub_all = lax.axis_size("sub") * count
    nb = profile.shape[0]
    pupil = math.isqrt(n * phase.shape[0])
    field = math.isqrt(n * cotangent.shape[0])
    qp = phase.shape[0] // n
    qc = cotangent.shape[0] // n
    extra = -(-6 * nb // 16) * 16
    me = lax.axis_index("alt").astype(jnp.int32).reshape(1)
    smem = pl.BlockSpec(memory_space=pltpu.SMEM)
    vmem = pl.BlockSpec(memory_space=pltpu.VMEM)
    params = pltpu.CompilerParams(vmem_limit_bytes=VMEM_LIMIT)

    early, late = pl.pallas_call(
        functools.partial(pack_kernel, n, nb),
        out_shape=(
            jax.ShapeDtypeStruct((n, 3 * qp + extra, LANES), BF16),
            jax.ShapeDtypeStruct((n, qc, LANES), BF16),
        ),
        in_specs=[smem, smem, vmem, vmem, vmem],
        out_specs=(vmem, vmem),
        compiler_params=params,
        name="pack",
    )(profile, alt_weight, cotangent, amplitude, phase)
    early = lax.all_to_all(early, "alt", 0, 0)
    late = lax.all_to_all(late, "alt", 0, 0)

    base = dft_matrix(pupil, field)
    fwd = jnp.asarray(table_three(base))
    bwd = jnp.asarray(table_three(base.T))
    aux_rows = -(-(3 * nb + 1) // 8) * 8
    grad, aux = pl.pallas_call(
        functools.partial(main_kernel, n, nb, pupil, field),
        out_shape=(
            jax.ShapeDtypeStruct((n, qp, LANES), F32),
            jax.ShapeDtypeStruct((aux_rows, LANES), F32),
        ),
        in_specs=[smem, vmem, vmem, vmem, vmem, vmem],
        out_specs=(vmem, vmem),
        scratch_shapes=[
            pltpu.VMEM((pupil * pupil, LANES), F32),
            pltpu.VMEM((pupil * pupil, LANES), F32),
            pltpu.VMEM((nb, 2 * pupil * pupil, LANES), F32),
            pltpu.VMEM((nb, 2 * pupil * field, LANES), F32),
            pltpu.VMEM((nb, 2 * pupil * field, LANES), F32),
            pltpu.VMEM((pupil * pupil, LANES), F32),
        ],
        compiler_params=params,
        name="spots",
    )(me, position, early, late, fwd, bwd)
    grad = lax.all_to_all(grad, "alt", 0, 0)
    stat = lax.psum(aux[:nb], ("sub", "alt"))
    phase_grad, profile_grad = pl.pallas_call(
        functools.partial(final_kernel, n, nb, nsub_all),
        out_shape=(
            jax.ShapeDtypeStruct(phase.shape, F32),
            jax.ShapeDtypeStruct(profile.shape, F32),
        ),
        in_specs=[smem, vmem, vmem, vmem],
        out_specs=(vmem, smem),
        compiler_params=params,
        name="unpack",
    )(me, grad, stat, aux)
    return phase_grad, profile_grad


def solution(mesh):
    placed = (P("alt", "sub"), P("alt", "sub"), P("alt", "sub"), P(None, "sub"), P("alt"), P("alt"))
    return jax.shard_map(
        local, mesh=mesh, in_specs=placed, out_specs=(P("alt", "sub"), P("alt")), check_vma=False
    )
```

```python
import functools
import math

import jax
import jax.numpy as jnp
import ml_dtypes
import numpy as np
from jax import lax
from jax.experimental import pallas as pl
from jax.experimental.pallas import tpu as pltpu
from jax.sharding import PartitionSpec as P

ELONG = 0.75
LANES = 128
VMEM_LIMIT = 24 * 1024 * 1024
F32 = jnp.float32
BF16 = jnp.bfloat16


def dft_matrix(pupil, field):
    angle = 2.0 * np.pi / field * (np.outer(np.arange(field), np.arange(pupil)) % field)
    c, s = np.cos(angle), np.sin(angle)
    return np.block([[c, s], [-s, c]])


def table_three(matrix):
    hi = matrix.astype(np.float32).astype(ml_dtypes.bfloat16)
    lo = (matrix - hi.astype(np.float64)).astype(np.float32).astype(ml_dtypes.bfloat16)
    return np.concatenate([hi, lo, hi], axis=1)


def split_three(x):
    hi = x.astype(BF16)
    lo = (x - hi.astype(F32)).astype(BF16)
    return jnp.concatenate([hi, hi, lo], axis=0)


def dot(a, b):
    return jnp.dot(a, b, preferred_element_type=F32)


def lane_group(shape, width):
    return lax.broadcasted_iota(jnp.int32, shape, len(shape) - 1) // width


def roll(x, shift):
    return pltpu.roll(x, shift % LANES, x.ndim - 1)


def swap_groups(blocks, width):
    n = len(blocks)
    blocks = list(blocks)
    group = lane_group(blocks[0].shape, width)
    step = 1
    while step < n:
        low = (group & step) == 0
        for i in range(n):
            if i & step:
                continue
            j = i + step
            a, b = blocks[i], blocks[j]
            blocks[i] = jnp.where(low, a, roll(b, step * width))
            blocks[j] = jnp.where(low, roll(a, -step * width), b)
        step *= 2
    return blocks


def spread_groups(x, n, width):
    group = lane_group(x.shape, width)
    out = [x]
    step = n // 2
    while step >= 1:
        low = (group & step) == 0
        made = []
        for y in out:
            up, down = roll(y, step * width), roll(y, -step * width)
            made.append(jnp.where(low, y, up))
            made.append(jnp.where(low, down, y))
        out = made
        step //= 2
    return out


def pack_kernel(n, nb, me_ref, profile_ref, weight_ref, cot_hbm, amp_hbm, phase_hbm, *refs):
    early_refs, late_ref = refs[:n], refs[n]
    cot_ref, amp_ref, phase_ref, sems = refs[n + 1 :]
    copies = [
        pltpu.make_async_copy(src, dst, sems.at[i])
        for i, (src, dst) in enumerate(
            ((phase_hbm, phase_ref), (amp_hbm, amp_ref), (cot_hbm, cot_ref))
        )
    ]
    for copy in copies:
        copy.start()
    width = LANES // n
    qp = phase_ref.shape[0] // n
    qc = cot_ref.shape[0] // n
    me = me_ref[0]
    turn = lax.rem(n - me, n) * width
    rows = early_refs[0].shape[0] - 3 * qp
    row = lax.broadcasted_iota(jnp.int32, (rows, LANES), 0)
    extra = jnp.zeros((rows, LANES), F32)
    for j in range(nb):
        for k, ref in enumerate((profile_ref, weight_ref)):
            value = jnp.full((rows, LANES), ref[j], F32)
            for part in range(3):
                piece = value.astype(BF16).astype(F32)
                extra = jnp.where(row == (2 * j + k) * 3 + part, piece, extra)
                value = value - piece
    for j in range(n):
        early_refs[j][3 * qp :, :] = extra.astype(BF16)
    copies[0].wait()
    for q in range(0, qp, 16):
        parts = [pltpu.roll(phase_ref[a * qp + q : a * qp + q + 16, :], turn, 1) for a in range(n)]
        for j, block in enumerate(swap_groups(parts, width)):
            hi = block.astype(BF16)
            early_refs[j][q : q + 16, :] = hi
            early_refs[j][qp + q : qp + q + 16, :] = (block - hi.astype(F32)).astype(BF16)
    copies[1].wait()
    for q in range(0, qp, 16):
        parts = [
            pltpu.roll(amp_ref[a * qp + q : a * qp + q + 16, :].astype(F32), turn, 1)
            for a in range(n)
        ]
        for j, block in enumerate(swap_groups(parts, width)):
            early_refs[j][2 * qp + q : 2 * qp + q + 16, :] = block.astype(BF16)
    copies[2].wait()

    def step(i, carry):
        at = pl.multiple_of(i * 16, 16)
        parts = [cot_ref[pl.ds(a * qc + at, 16), :].astype(F32) for a in range(n)]
        for d, block in enumerate(swap_groups(parts, width)):
            late_ref[d, pl.ds(at, 16), :] = block.astype(BF16)
        return carry

    lax.fori_loop(0, qc // 16, step, 0, unroll=4)


def sincos(x):
    turns = jnp.round(x * (2.0 / math.pi))
    r = x - turns * 1.5703125
    r = r - turns * 4.838267948966e-4
    r2 = r * r
    s = r + r * r2 * (-1.6666654611e-1 + r2 * (8.3321608736e-3 + r2 * -1.9515295891e-4))
    c = (1.0 - 0.5 * r2) + r2 * r2 * (
        4.166664568298827e-2 + r2 * (-1.388731625493765e-3 + r2 * 2.443315711809948e-5)
    )
    quad = turns.astype(jnp.int32)
    odd = (quad & 1) != 0
    sin_v = jnp.where(odd, c, s)
    cos_v = jnp.where(odd, s, c)
    sin_v = jnp.where((quad & 2) != 0, -sin_v, sin_v)
    cos_v = jnp.where(((quad + 1) & 2) != 0, -cos_v, cos_v)
    return sin_v, cos_v


def first_kernel(n, nb, pupil, field, me_ref, pos_ref, *refs):
    early_refs = refs[:n]
    fwd_ref, e_s, f_s, aux_ref, phase_s, amp_s = refs[n:]
    width = LANES // n
    nbins = n * nb
    qp = pupil * pupil // (n * n)
    group1 = lane_group((1, LANES), width)

    pos = pos_ref[...]
    me = me_ref[0]
    near = jnp.zeros_like(pos)
    for d in range(n):
        near = jnp.where(me == d, spread_groups(pos, n, width)[d], near)

    prof, wgt = [], []
    for t in range(nb):
        p_row, w_row = jnp.zeros((1, LANES), F32), jnp.zeros((1, LANES), F32)
        for j in range(n):
            d = lax.rem(me + n - j, n)
            extra = early_refs[j][3 * qp :, :].astype(F32)
            p_d = sum(extra[(2 * t) * 3 + part : (2 * t) * 3 + part + 1, :] for part in (0, 1, 2))
            w_d = sum(
                extra[(2 * t + 1) * 3 + part : (2 * t + 1) * 3 + part + 1, :] for part in (0, 1, 2)
            )
            p_row = jnp.where(group1 == d, p_d, p_row)
            w_row = jnp.where(group1 == d, w_d, w_row)
        prof.append(p_row)
        wgt.append(w_row)
    total = sum(prof)
    step = n // 2
    while step >= 1:
        total = total + roll(total, step * width)
        step //= 2
    aux = jnp.zeros(aux_ref.shape, F32)
    row = lax.broadcasted_iota(jnp.int32, aux_ref.shape, 0)
    for t in range(nb):
        aux = jnp.where(row == t, 2.0 / (pupil * pupil) * prof[t] * wgt[t] / total, aux)
        aux = jnp.where(row == nb + t, prof[t], aux)
        aux = jnp.where(row == 2 * nb + t, wgt[t], aux)
    aux_ref[...] = jnp.where(row == 3 * nb, total, aux)
    kappa = [
        ELONG * (2.0 * (group1 * nb + t).astype(F32) / (nbins - 1) - 1.0) for t in range(nb)
    ]
    tilt_x = [kappa[t] * near[0:1, :] for t in range(nb)]
    tilt_y = [kappa[t] * near[1:2, :] for t in range(nb)]

    for j in range(n):
        d = lax.rem(me + n - j, n)
        for q in range(0, qp, 16):
            hi = early_refs[j][q : q + 16, :].astype(F32)
            lo = early_refs[j][qp + q : qp + q + 16, :].astype(F32)
            am = early_refs[j][2 * qp + q : 2 * qp + q + 16, :].astype(F32)
            for a, (one, two) in enumerate(
                zip(spread_groups(hi + lo, n, width), spread_groups(am, n, width))
            ):
                at = pl.multiple_of((d * n + a) * qp + q, 16)
                phase_s[pl.ds(at, 16), :] = one
                amp_s[pl.ds(at, 16), :] = two

    v_rows = lax.broadcasted_iota(jnp.int32, (pupil, LANES), 0).astype(F32) - (pupil - 1) / 2.0
    swing = [v_rows * tilt_y[t] for t in range(nb)]
    fwd = fwd_ref[...]

    def first(i, carry):
        for k in range(4):
            c = i * 4 + k
            u = c.astype(F32) - (pupil - 1) / 2.0
            ph = phase_s[pl.ds(c, pupil, stride=pupil), :]
            am = amp_s[pl.ds(c, pupil, stride=pupil), :]
            fields = []
            for t in range(nb):
                sin_v, cos_v = sincos(ph + (u * tilt_x[t] + swing[t]))
                e = jnp.concatenate([am * cos_v, am * sin_v], axis=0)
                e_s[t, pl.ds(pl.multiple_of(c * 2 * pupil, 2 * pupil), 2 * pupil), :] = e
                fields.append(split_three(e))
            out = dot(fwd, jnp.concatenate(fields, axis=1))
            for t in range(nb):
                f_s[t, pl.ds(pl.multiple_of(c * 2 * field, 2 * field), 2 * field), :] = out[
                    :, t * LANES : (t + 1) * LANES
                ]
        return carry

    lax.fori_loop(0, pupil // 4, first, 0)


def second_kernel(
    n, nb, pupil, field, e_s, f_s, aux_in, late_ref, fwd_ref, bwd_ref, grad_ref, stat_ref, g_s, pg_s
):
    width = LANES // n
    qp = pupil * pupil // (n * n)
    qc = field * field // (n * n)
    fwd = fwd_ref[...]
    bwd = bwd_ref[...]
    coef = [aux_in[t : t + 1, :] for t in range(nb)]

    per = qc // field

    def middle(i, carry):
        d, j = i // per, i % per
        raw = late_ref[d, pl.ds(pl.multiple_of(j * field, field), field), :].astype(F32)
        for a, cot in enumerate(spread_groups(raw, n, width)):
            k1 = (d * n + a) * per + j
            parts = []
            for t in range(nb):
                re = f_s[t, pl.ds(k1, pupil, stride=2 * field), :]
                im = f_s[t, pl.ds(k1 + field, pupil, stride=2 * field), :]
                parts.append(split_three(jnp.concatenate([re, im], axis=0)))
            image = dot(fwd, jnp.concatenate(parts, axis=1))
            both = jnp.concatenate([cot, cot], axis=0)
            parts = [
                split_three(image[:, t * LANES : (t + 1) * LANES] * both) for t in range(nb)
            ]
            back = dot(bwd, jnp.concatenate(parts, axis=1))
            for t in range(nb):
                g_s[t, pl.ds(pl.multiple_of(k1 * 2 * pupil, 2 * pupil), 2 * pupil), :] = back[
                    :, t * LANES : (t + 1) * LANES
                ]
        return carry

    lax.fori_loop(0, n * per, middle, 0)

    def last(i, stats):
        stats = list(stats)
        for k in range(4):
            c = i * 4 + k
            parts = []
            for t in range(nb):
                re = g_s[t, pl.ds(c, field, stride=2 * pupil), :]
                im = g_s[t, pl.ds(c + pupil, field, stride=2 * pupil), :]
                parts.append(split_three(jnp.concatenate([re, im], axis=0)))
            out = dot(bwd, jnp.concatenate(parts, axis=1))
            grad = jnp.zeros((pupil, LANES), F32)
            for t in range(nb):
                g = out[:, t * LANES : (t + 1) * LANES]
                e = e_s[t, pl.ds(pl.multiple_of(c * 2 * pupil, 2 * pupil), 2 * pupil), :]
                g_re, g_im = g[:pupil], g[pupil:]
                e_re, e_im = e[:pupil], e[pupil:]
                stats[t] = stats[t] + (e_re * g_re + e_im * g_im)
                grad = grad + coef[t] * (e_re * g_im - e_im * g_re)
            step = n // 2
            while step >= 1:
                grad = grad + roll(grad, step * width)
                step //= 2
            pg_s[pl.ds(c, pupil, stride=pupil), :] = grad
        return tuple(stats)

    stats = lax.fori_loop(
        0, pupil // 4, last, tuple(jnp.zeros((pupil, LANES), F32) for _ in range(nb))
    )

    lane = lax.broadcasted_iota(jnp.int32, (1, LANES), 1)
    sums = jnp.zeros((1, LANES), F32)
    for t in range(nb):
        stat = jnp.sum(stats[t], axis=0, keepdims=True) * (1.0 / (pupil * pupil))
        step = 1
        while step < width:
            stat = stat + roll(stat, step)
            step *= 2
        sums = jnp.where(lane % width == width - 1 - t, roll(stat, -t), sums)
    for i in range(stat_ref.shape[0]):
        stat_ref[i] = sums

    def repack(d, carry):
        for q in range(0, qp, 8):
            out = jnp.zeros((8, LANES), F32)
            group = lane_group((8, LANES), width)
            for a in range(n):
                at = pl.multiple_of((d * n + a) * qp + q, 8)
                out = jnp.where(group == a, pg_s[pl.ds(at, 8), :], out)
            grad_ref[d, q : q + 8, :] = out
        return carry

    lax.fori_loop(0, n, repack, 0)


def final_kernel(n, nb, nsub_all, me_ref, grad_ref, stat_ref, aux_ref, out_ref, prof_ref):
    width = LANES // n
    qp = grad_ref.shape[1]
    for a, block in enumerate(swap_groups([grad_ref[d] for d in range(n)], width)):
        out_ref[a * qp : (a + 1) * qp, :] = block
    lane = lax.broadcasted_iota(jnp.int32, (1, LANES), 1)
    stat = jnp.sum(stat_ref[...], axis=0)
    aux = aux_ref[...]
    total = jnp.max(aux[3 * nb : 3 * nb + 1, :])
    centre = jnp.zeros((1, LANES), F32)
    own = []
    for t in range(nb):
        prof, wgt = aux[nb + t : nb + t + 1], aux[2 * nb + t : 2 * nb + t + 1]
        term = stat * wgt
        centre += jnp.where(lane % width == width - 1 - t, term * prof, 0.0)
        own.append(jnp.sum(jnp.where(lane == (me_ref[0] + 1) * width - 1 - t, term, 0.0)))
    centre = jnp.sum(centre)
    for t in range(nb):
        prof_ref[t] = (own[t] / total - centre / (total * total)) / nsub_all


def local(cotangent, amplitude, phase, position, profile, alt_weight):
    n = lax.axis_size("alt")
    count = phase.shape[1]
    nsub_all = lax.axis_size("sub") * count
    nb = profile.shape[0]
    pupil = math.isqrt(n * phase.shape[0])
    field = math.isqrt(n * cotangent.shape[0])
    qp = phase.shape[0] // n
    qc = cotangent.shape[0] // n
    extra = -(-6 * nb // 16) * 16
    me = lax.axis_index("alt").astype(jnp.int32).reshape(1)
    smem = pl.BlockSpec(memory_space=pltpu.SMEM)
    vmem = pl.BlockSpec(memory_space=pltpu.VMEM)
    params = pltpu.CompilerParams(vmem_limit_bytes=VMEM_LIMIT)

    any_space = pl.BlockSpec(memory_space=pl.ANY)
    early_shape = (3 * qp + extra, LANES)
    *early, late = pl.pallas_call(
        functools.partial(pack_kernel, n, nb),
        out_shape=[jax.ShapeDtypeStruct(early_shape, BF16)] * n
        + [jax.ShapeDtypeStruct((n, qc, LANES), BF16)],
        in_specs=[smem, smem, smem, any_space, any_space, any_space],
        out_specs=[vmem] * (n + 1),
        scratch_shapes=[
            pltpu.VMEM(cotangent.shape, BF16),
            pltpu.VMEM(amplitude.shape, BF16),
            pltpu.VMEM(phase.shape, F32),
            pltpu.SemaphoreType.DMA((3,)),
        ],
        compiler_params=params,
        name="pack",
    )(me, profile, alt_weight, cotangent, amplitude, phase)
    early = early[:1] + [
        lax.ppermute(early[j], "alt", [(i, (i + j) % n) for i in range(n)]) for j in range(1, n)
    ]
    late = lax.all_to_all(late, "alt", 0, 0)

    base = dft_matrix(pupil, field)
    fwd = jnp.asarray(table_three(base))
    bwd = jnp.asarray(table_three(base.T))
    aux_rows = -(-(3 * nb + 1) // 8) * 8
    e, f, aux = pl.pallas_call(
        functools.partial(first_kernel, n, nb, pupil, field),
        out_shape=(
            jax.ShapeDtypeStruct((nb, 2 * pupil * pupil, LANES), F32),
            jax.ShapeDtypeStruct((nb, 2 * pupil * field, LANES), F32),
            jax.ShapeDtypeStruct((aux_rows, LANES), F32),
        ),
        in_specs=[smem, vmem] + [vmem] * n + [vmem],
        out_specs=(vmem, vmem, vmem),
        scratch_shapes=[
            pltpu.VMEM((pupil * pupil, LANES), F32),
            pltpu.VMEM((pupil * pupil, LANES), F32),
        ],
        compiler_params=params,
        name="fields",
    )(me, position, *early, fwd)
    devices = lax.axis_size("sub") * n
    grad, stat = pl.pallas_call(
        functools.partial(second_kernel, n, nb, pupil, field),
        out_shape=(
            jax.ShapeDtypeStruct((n, qp, LANES), F32),
            jax.ShapeDtypeStruct((devices, 1, LANES), F32),
        ),
        in_specs=[vmem] * 6,
        out_specs=(vmem, vmem),
        scratch_shapes=[
            pltpu.VMEM((nb, 2 * pupil * field, LANES), F32),
            pltpu.VMEM((pupil * pupil, LANES), F32),
        ],
        compiler_params=params,
        name="images",
    )(e, f, aux, late, fwd, bwd)
    grad = lax.all_to_all(grad, "alt", 0, 0)
    stat = lax.all_to_all(stat, ("sub", "alt"), 0, 0)
    phase_grad, profile_grad = pl.pallas_call(
        functools.partial(final_kernel, n, nb, nsub_all),
        out_shape=(
            jax.ShapeDtypeStruct(phase.shape, F32),
            jax.ShapeDtypeStruct(profile.shape, F32),
        ),
        in_specs=[smem, vmem, vmem, vmem],
        out_specs=(vmem, smem),
        compiler_params=params,
        name="unpack",
    )(me, grad, stat, aux)
    return phase_grad, profile_grad


def solution(mesh):
    placed = (P("alt", "sub"), P("alt", "sub"), P("alt", "sub"), P(None, "sub"), P("alt"), P("alt"))
    return jax.shard_map(
        local, mesh=mesh, in_specs=placed, out_specs=(P("alt", "sub"), P("alt")), check_vma=False
    )
```

```python
import functools
import math

import jax
import jax.numpy as jnp
import ml_dtypes
import numpy as np
from jax import lax
from jax.experimental import pallas as pl
from jax.experimental.pallas import tpu as pltpu
from jax.sharding import PartitionSpec as P

ELONG = 0.75
LANES = 128
VMEM_LIMIT = 24 * 1024 * 1024
F32 = jnp.float32
BF16 = jnp.bfloat16


def dft_matrix(pupil, field):
    angle = 2.0 * np.pi / field * (np.outer(np.arange(field), np.arange(pupil)) % field)
    c, s = np.cos(angle), np.sin(angle)
    return np.block([[c, s], [-s, c]])


def table_three(matrix):
    hi = matrix.astype(np.float32).astype(ml_dtypes.bfloat16)
    lo = (matrix - hi.astype(np.float64)).astype(np.float32).astype(ml_dtypes.bfloat16)
    return np.concatenate([hi, lo, hi], axis=1)


def split_three(x):
    hi = x.astype(BF16)
    lo = (x - hi.astype(F32)).astype(BF16)
    return jnp.concatenate([hi, hi, lo], axis=0)


def dot(a, b):
    return jnp.dot(a, b, preferred_element_type=F32)


def lane_group(shape, width):
    return lax.broadcasted_iota(jnp.int32, shape, len(shape) - 1) // width


def roll(x, shift):
    return pltpu.roll(x, shift % LANES, x.ndim - 1)


def swap_groups(blocks, width):
    n = len(blocks)
    blocks = list(blocks)
    group = lane_group(blocks[0].shape, width)
    step = 1
    while step < n:
        low = (group & step) == 0
        for i in range(n):
            if i & step:
                continue
            j = i + step
            a, b = blocks[i], blocks[j]
            blocks[i] = jnp.where(low, a, roll(b, step * width))
            blocks[j] = jnp.where(low, roll(a, -step * width), b)
        step *= 2
    return blocks


def spread_groups(x, n, width):
    group = lane_group(x.shape, width)
    out = [x]
    step = n // 2
    while step >= 1:
        low = (group & step) == 0
        made = []
        for y in out:
            up, down = roll(y, step * width), roll(y, -step * width)
            made.append(jnp.where(low, y, up))
            made.append(jnp.where(low, down, y))
        out = made
        step //= 2
    return out


def pack_early_kernel(n, nb, me_ref, profile_hbm, weight_hbm, amp_hbm, phase_hbm, *refs):
    early_refs = refs[:n]
    profile_ref, weight_ref, amp_ref, phase_ref, sems = refs[n:]
    pairs = (
        (phase_hbm, phase_ref),
        (amp_hbm, amp_ref),
        (profile_hbm, profile_ref),
        (weight_hbm, weight_ref),
    )
    copies = [pltpu.make_async_copy(src, dst, sems.at[i]) for i, (src, dst) in enumerate(pairs)]
    for copy in copies:
        copy.start()
    width = LANES // n
    qp = phase_ref.shape[0] // n
    turn = lax.rem(n - me_ref[0], n) * width
    copies[0].wait()
    for q in range(0, qp, 16):
        parts = [pltpu.roll(phase_ref[a * qp + q : a * qp + q + 16, :], turn, 1) for a in range(n)]
        for j, block in enumerate(swap_groups(parts, width)):
            hi = block.astype(BF16)
            early_refs[j][q : q + 16, :] = hi
            early_refs[j][qp + q : qp + q + 16, :] = (block - hi.astype(F32)).astype(BF16)
    copies[1].wait()
    for q in range(0, qp, 16):
        parts = [
            pltpu.roll(amp_ref[a * qp + q : a * qp + q + 16, :].astype(F32), turn, 1)
            for a in range(n)
        ]
        for j, block in enumerate(swap_groups(parts, width)):
            early_refs[j][2 * qp + q : 2 * qp + q + 16, :] = block.astype(BF16)
    copies[2].wait()
    copies[3].wait()
    rows = early_refs[0].shape[0] - 3 * qp
    row = lax.broadcasted_iota(jnp.int32, (rows, LANES), 0)
    extra = jnp.zeros((rows, LANES), F32)
    for j in range(nb):
        for k, ref in enumerate((profile_ref, weight_ref)):
            value = jnp.full((rows, LANES), ref[j], F32)
            for part in range(3):
                piece = value.astype(BF16).astype(F32)
                extra = jnp.where(row == (2 * j + k) * 3 + part, piece, extra)
                value = value - piece
    for j in range(n):
        early_refs[j][3 * qp :, :] = extra.astype(BF16)


def pack_late_kernel(n, me_ref, cot_hbm, *refs):
    late_refs = refs[:n]
    cot_ref, sem = refs[n:]
    copy = pltpu.make_async_copy(cot_hbm, cot_ref, sem)
    copy.start()
    width = LANES // n
    qc = cot_ref.shape[0] // n
    turn = lax.rem(n - me_ref[0], n) * width
    copy.wait()

    def step(i, carry):
        at = pl.multiple_of(i * 16, 16)
        parts = [
            pltpu.roll(cot_ref[pl.ds(a * qc + at, 16), :].astype(F32), turn, 1) for a in range(n)
        ]
        for j, block in enumerate(swap_groups(parts, width)):
            late_refs[j][pl.ds(at, 16), :] = block.astype(BF16)
        return carry

    lax.fori_loop(0, qc // 16, step, 0, unroll=4)


def sincos(x):
    turns = jnp.round(x * (2.0 / math.pi))
    r = x - turns * 1.5703125
    r = r - turns * 4.838267948966e-4
    r2 = r * r
    s = r + r * r2 * (-1.6666654611e-1 + r2 * (8.3321608736e-3 + r2 * -1.9515295891e-4))
    c = (1.0 - 0.5 * r2) + r2 * r2 * (
        4.166664568298827e-2 + r2 * (-1.388731625493765e-3 + r2 * 2.443315711809948e-5)
    )
    quad = turns.astype(jnp.int32)
    odd = (quad & 1) != 0
    sin_v = jnp.where(odd, c, s)
    cos_v = jnp.where(odd, s, c)
    sin_v = jnp.where((quad & 2) != 0, -sin_v, sin_v)
    cos_v = jnp.where(((quad + 1) & 2) != 0, -cos_v, cos_v)
    return sin_v, cos_v


def first_kernel(n, nb, pupil, field, me_ref, pos_hbm, fwd_hbm, *refs):
    early_refs = refs[:n]
    e_s, f_s, aux_ref, phase_s, amp_s, pos_ref, fwd_ref, sems = refs[n:]
    copies = [
        pltpu.make_async_copy(pos_hbm, pos_ref, sems.at[0]),
        pltpu.make_async_copy(fwd_hbm, fwd_ref, sems.at[1]),
    ]
    for copy in copies:
        copy.start()
    width = LANES // n
    nbins = n * nb
    qp = pupil * pupil // (n * n)
    group1 = lane_group((1, LANES), width)

    me = me_ref[0]

    for j in range(n):
        d = lax.rem(me + n - j, n)
        for q in range(0, qp, 16):
            hi = early_refs[j][q : q + 16, :].astype(F32)
            lo = early_refs[j][qp + q : qp + q + 16, :].astype(F32)
            am = early_refs[j][2 * qp + q : 2 * qp + q + 16, :].astype(F32)
            for a, (one, two) in enumerate(
                zip(spread_groups(hi + lo, n, width), spread_groups(am, n, width))
            ):
                at = pl.multiple_of((d * n + a) * qp + q, 16)
                phase_s[pl.ds(at, 16), :] = one
                amp_s[pl.ds(at, 16), :] = two

    for copy in copies:
        copy.wait()
    pos = pos_ref[...]
    near = jnp.zeros_like(pos)
    for d in range(n):
        near = jnp.where(me == d, spread_groups(pos, n, width)[d], near)

    prof, wgt = [], []
    for t in range(nb):
        p_row, w_row = jnp.zeros((1, LANES), F32), jnp.zeros((1, LANES), F32)
        for j in range(n):
            d = lax.rem(me + n - j, n)
            extra = early_refs[j][3 * qp :, :].astype(F32)
            p_d = sum(extra[(2 * t) * 3 + part : (2 * t) * 3 + part + 1, :] for part in (0, 1, 2))
            w_d = sum(
                extra[(2 * t + 1) * 3 + part : (2 * t + 1) * 3 + part + 1, :] for part in (0, 1, 2)
            )
            p_row = jnp.where(group1 == d, p_d, p_row)
            w_row = jnp.where(group1 == d, w_d, w_row)
        prof.append(p_row)
        wgt.append(w_row)
    total = sum(prof)
    step = n // 2
    while step >= 1:
        total = total + roll(total, step * width)
        step //= 2
    aux = jnp.zeros(aux_ref.shape, F32)
    row = lax.broadcasted_iota(jnp.int32, aux_ref.shape, 0)
    for t in range(nb):
        aux = jnp.where(row == t, 2.0 / (pupil * pupil) * prof[t] * wgt[t] / total, aux)
        aux = jnp.where(row == nb + t, prof[t], aux)
        aux = jnp.where(row == 2 * nb + t, wgt[t], aux)
    aux_ref[...] = jnp.where(row == 3 * nb, total, aux)
    kappa = [
        ELONG * (2.0 * (group1 * nb + t).astype(F32) / (nbins - 1) - 1.0) for t in range(nb)
    ]
    tilt_x = [kappa[t] * near[0:1, :] for t in range(nb)]
    tilt_y = [kappa[t] * near[1:2, :] for t in range(nb)]

    v_rows = lax.broadcasted_iota(jnp.int32, (pupil, LANES), 0).astype(F32) - (pupil - 1) / 2.0
    swing = [v_rows * tilt_y[t] for t in range(nb)]
    fwd = fwd_ref[...]

    def first(i, carry):
        for k in range(4):
            c = i * 4 + k
            u = c.astype(F32) - (pupil - 1) / 2.0
            ph = phase_s[pl.ds(c, pupil, stride=pupil), :]
            am = amp_s[pl.ds(c, pupil, stride=pupil), :]
            fields = []
            for t in range(nb):
                sin_v, cos_v = sincos(ph + (u * tilt_x[t] + swing[t]))
                e = jnp.concatenate([am * cos_v, am * sin_v], axis=0)
                e_s[t, pl.ds(pl.multiple_of(c * 2 * pupil, 2 * pupil), 2 * pupil), :] = e
                fields.append(split_three(e))
            out = dot(fwd, jnp.concatenate(fields, axis=1))
            for t in range(nb):
                f_s[t, pl.ds(pl.multiple_of(c * 2 * field, 2 * field), 2 * field), :] = out[
                    :, t * LANES : (t + 1) * LANES
                ]
        return carry

    lax.fori_loop(0, pupil // 4, first, 0)


def second_kernel(n, nb, pupil, field, me_ref, fwd_hbm, bwd_hbm, e_s, f_s, aux_in, *refs):
    late_refs, grad_refs = refs[:n], refs[n : 2 * n]
    g_s, pg_s, fwd_ref, bwd_ref, sems = refs[2 * n :]
    copies = [
        pltpu.make_async_copy(fwd_hbm, fwd_ref, sems.at[0]),
        pltpu.make_async_copy(bwd_hbm, bwd_ref, sems.at[1]),
    ]
    for copy in copies:
        copy.start()
    me = me_ref[0]
    for copy in copies:
        copy.wait()
    width = LANES // n
    qp = pupil * pupil // (n * n)
    qc = field * field // (n * n)
    fwd = fwd_ref[...]
    bwd = bwd_ref[...]
    coef = [aux_in[t : t + 1, :] for t in range(nb)]

    per = qc // field

    def middle(ref, d, j):
        raw = ref[pl.ds(pl.multiple_of(j * field, field), field), :].astype(F32)
        for a, cot in enumerate(spread_groups(raw, n, width)):
            k1 = (d * n + a) * per + j
            parts = []
            for t in range(nb):
                re = f_s[t, pl.ds(k1, pupil, stride=2 * field), :]
                im = f_s[t, pl.ds(k1 + field, pupil, stride=2 * field), :]
                parts.append(split_three(jnp.concatenate([re, im], axis=0)))
            image = dot(fwd, jnp.concatenate(parts, axis=1))
            both = jnp.concatenate([cot, cot], axis=0)
            parts = [
                split_three(image[:, t * LANES : (t + 1) * LANES] * both) for t in range(nb)
            ]
            back = dot(bwd, jnp.concatenate(parts, axis=1))
            for t in range(nb):
                g_s[t, pl.ds(pl.multiple_of(k1 * 2 * pupil, 2 * pupil), 2 * pupil), :] = back[
                    :, t * LANES : (t + 1) * LANES
                ]

    for k, ref in enumerate(late_refs):
        d = lax.rem(me + n - k, n)
        if per == 1:
            middle(ref, d, 0)
        else:
            lax.fori_loop(0, per, lambda j, carry: middle(ref, d, j) or carry, 0)

    def last(i, stats):
        stats = list(stats)
        for k in range(4):
            c = i * 4 + k
            parts = []
            for t in range(nb):
                re = g_s[t, pl.ds(c, field, stride=2 * pupil), :]
                im = g_s[t, pl.ds(c + pupil, field, stride=2 * pupil), :]
                parts.append(split_three(jnp.concatenate([re, im], axis=0)))
            out = dot(bwd, jnp.concatenate(parts, axis=1))
            grad = jnp.zeros((pupil, LANES), F32)
            for t in range(nb):
                g = out[:, t * LANES : (t + 1) * LANES]
                e = e_s[t, pl.ds(pl.multiple_of(c * 2 * pupil, 2 * pupil), 2 * pupil), :]
                g_re, g_im = g[:pupil], g[pupil:]
                e_re, e_im = e[:pupil], e[pupil:]
                stats[t] = stats[t] + (e_re * g_re + e_im * g_im)
                grad = grad + coef[t] * (e_re * g_im - e_im * g_re)
            step = n // 2
            while step >= 1:
                grad = grad + roll(grad, step * width)
                step //= 2
            pg_s[pl.ds(c, pupil, stride=pupil), :] = grad
        return tuple(stats)

    stats = lax.fori_loop(
        0, pupil // 4, last, tuple(jnp.zeros((pupil, LANES), F32) for _ in range(nb))
    )

    lane = lax.broadcasted_iota(jnp.int32, (1, LANES), 1)
    sums = jnp.zeros((1, LANES), F32)
    for t in range(nb):
        stat = jnp.sum(stats[t], axis=0, keepdims=True) * (1.0 / (pupil * pupil))
        step = 1
        while step < width:
            stat = stat + roll(stat, step)
            step *= 2
        sums = jnp.where(lane % width == width - 1 - t, roll(stat, -t), sums)
    group = lane_group((8, LANES), width)
    for k, ref in enumerate(grad_refs):
        d = lax.rem(me + k, n)
        for q in range(0, qp, 8):
            out = jnp.zeros((8, LANES), F32)
            for a in range(n):
                at = pl.multiple_of((d * n + a) * qp + q, 8)
                out = jnp.where(group == a, pg_s[pl.ds(at, 8), :], out)
            ref[q : q + 8, :] = out
        ref[qp : qp + 8, :] = jnp.broadcast_to(sums, (8, LANES))


def sum_kernel(n, *refs):
    refs[n][...] = sum(refs[k][...] for k in range(n))


def grad_kernel(n, me_ref, *refs):
    width = LANES // n
    out_ref = refs[n]
    qp = out_ref.shape[0] // n
    turn = me_ref[0] * width
    for q in range(0, qp, 8):
        parts = [refs[(n - i) % n][q : q + 8, :] for i in range(n)]
        for a, block in enumerate(swap_groups(parts, width)):
            out_ref[a * qp + q : a * qp + q + 8, :] = pltpu.roll(block, turn, 1)


def profile_kernel(n, nb, nsub_all, me_ref, aux_ref, *refs):
    width = LANES // n
    prof_ref = refs[-1]
    lane = lax.broadcasted_iota(jnp.int32, (1, LANES), 1)
    stat = sum(ref[...] for ref in refs[:-1])[0:1, :]
    aux = aux_ref[...]
    total = jnp.max(aux[3 * nb : 3 * nb + 1, :])
    centre = jnp.zeros((1, LANES), F32)
    own = []
    for t in range(nb):
        prof, wgt = aux[nb + t : nb + t + 1], aux[2 * nb + t : 2 * nb + t + 1]
        term = stat * wgt
        centre += jnp.where(lane % width == width - 1 - t, term * prof, 0.0)
        own.append(jnp.sum(jnp.where(lane == (me_ref[0] + 1) * width - 1 - t, term, 0.0)))
    centre = jnp.sum(centre)
    for t in range(nb):
        prof_ref[t] = (own[t] / total - centre / (total * total)) / nsub_all


def local(cotangent, amplitude, phase, position, profile, alt_weight):
    n = lax.axis_size("alt")
    count = phase.shape[1]
    nsub_all = lax.axis_size("sub") * count
    nb = profile.shape[0]
    pupil = math.isqrt(n * phase.shape[0])
    field = math.isqrt(n * cotangent.shape[0])
    qp = phase.shape[0] // n
    qc = cotangent.shape[0] // n
    extra = -(-6 * nb // 16) * 16
    me = lax.axis_index("alt").astype(jnp.int32).reshape(1)
    smem = pl.BlockSpec(memory_space=pltpu.SMEM)
    vmem = pl.BlockSpec(memory_space=pltpu.VMEM)
    params = pltpu.CompilerParams(vmem_limit_bytes=VMEM_LIMIT)

    hbm = pl.BlockSpec(memory_space=pltpu.HBM)
    early_shape = (3 * qp + extra, LANES)
    n_sub = lax.axis_size("sub")

    def exchange(blocks, axis, size):
        return [blocks[0]] + [
            lax.ppermute(blocks[j], axis, [(i, (i + j) % size) for i in range(size)])
            for j in range(1, size)
        ]

    early = pl.pallas_call(
        functools.partial(pack_early_kernel, n, nb),
        out_shape=[jax.ShapeDtypeStruct(early_shape, BF16)] * n,
        in_specs=[smem, hbm, hbm, hbm, hbm],
        out_specs=[vmem] * n,
        scratch_shapes=[
            pltpu.SMEM(profile.shape, F32),
            pltpu.SMEM(alt_weight.shape, F32),
            pltpu.VMEM(amplitude.shape, BF16),
            pltpu.VMEM(phase.shape, F32),
            pltpu.SemaphoreType.DMA((4,)),
        ],
        compiler_params=params,
        name="pack_early",
    )(me, profile, alt_weight, amplitude, phase)
    early = exchange(early, "alt", n)
    late = pl.pallas_call(
        functools.partial(pack_late_kernel, n),
        out_shape=[jax.ShapeDtypeStruct((qc, LANES), BF16)] * n,
        in_specs=[smem, hbm],
        out_specs=[vmem] * n,
        scratch_shapes=[pltpu.VMEM(cotangent.shape, BF16), pltpu.SemaphoreType.DMA],
        compiler_params=params,
        name="pack_late",
    )(me, cotangent)
    late = exchange(late, "alt", n)

    base = dft_matrix(pupil, field)
    fwd = jnp.asarray(table_three(base))
    bwd = jnp.asarray(table_three(base.T))
    aux_rows = -(-(3 * nb + 1) // 8) * 8
    e, f, aux = pl.pallas_call(
        functools.partial(first_kernel, n, nb, pupil, field),
        out_shape=(
            jax.ShapeDtypeStruct((nb, 2 * pupil * pupil, LANES), F32),
            jax.ShapeDtypeStruct((nb, 2 * pupil * field, LANES), F32),
            jax.ShapeDtypeStruct((aux_rows, LANES), F32),
        ),
        in_specs=[smem, hbm, hbm] + [vmem] * n,
        out_specs=(vmem, vmem, vmem),
        scratch_shapes=[
            pltpu.VMEM((pupil * pupil, LANES), F32),
            pltpu.VMEM((pupil * pupil, LANES), F32),
            pltpu.VMEM(position.shape, F32),
            pltpu.VMEM(fwd.shape, BF16),
            pltpu.SemaphoreType.DMA((2,)),
        ],
        compiler_params=params,
        name="fields",
    )(me, position, fwd, *early)
    grads = pl.pallas_call(
        functools.partial(second_kernel, n, nb, pupil, field),
        out_shape=[jax.ShapeDtypeStruct((qp + 8, LANES), F32)] * n,
        in_specs=[smem, hbm, hbm] + [vmem] * (3 + n),
        out_specs=[vmem] * n,
        scratch_shapes=[
            pltpu.VMEM((nb, 2 * pupil * field, LANES), F32),
            pltpu.VMEM((pupil * pupil, LANES), F32),
            pltpu.VMEM(fwd.shape, BF16),
            pltpu.VMEM(bwd.shape, BF16),
            pltpu.SemaphoreType.DMA((2,)),
        ],
        compiler_params=params,
        name="images",
    )(me, fwd, bwd, e, f, aux, *late)
    grads = exchange(grads, "alt", n)
    stat = pl.pallas_call(
        functools.partial(sum_kernel, n),
        out_shape=jax.ShapeDtypeStruct((8, LANES), F32),
        grid=(1,),
        in_specs=[pl.BlockSpec((8, LANES), lambda i: (qp // 8, 0))] * n,
        out_specs=pl.BlockSpec((8, LANES), lambda i: (0, 0)),
        compiler_params=params,
        name="group_sum",
    )(*grads)
    stats = exchange([stat] * n_sub, "sub", n_sub)
    phase_grad = pl.pallas_call(
        functools.partial(grad_kernel, n),
        out_shape=jax.ShapeDtypeStruct(phase.shape, F32),
        in_specs=[smem] + [vmem] * n,
        out_specs=vmem,
        compiler_params=params,
        name="gradient",
    )(me, *grads)
    profile_grad = pl.pallas_call(
        functools.partial(profile_kernel, n, nb, nsub_all),
        out_shape=jax.ShapeDtypeStruct(profile.shape, F32),
        in_specs=[smem] + [vmem] * (1 + n_sub),
        out_specs=smem,
        compiler_params=params,
        name="profile",
    )(me, aux, *stats)
    return phase_grad, profile_grad


def solution(mesh):
    placed = (P("alt", "sub"), P("alt", "sub"), P("alt", "sub"), P(None, "sub"), P("alt"), P("alt"))
    return jax.shard_map(
        local, mesh=mesh, in_specs=placed, out_specs=(P("alt", "sub"), P("alt")), check_vma=False
    )
```

```python
import functools
import math

import jax
import jax.numpy as jnp
import ml_dtypes
import numpy as np
from jax import lax
from jax.experimental import pallas as pl
from jax.experimental.pallas import tpu as pltpu
from jax.sharding import PartitionSpec as P

ELONG = 0.75
LANES = 128
VMEM_LIMIT = 44 * 1024 * 1024
F32 = jnp.float32
BF16 = jnp.bfloat16


CHUNK = 512


def halves(pupil, field, fun):
    freq = np.arange(field // 2) + 0.5
    place = (pupil - 1) / 2.0 - np.arange(pupil // 2)
    return fun(2.0 * np.pi / field * np.outer(freq, place))


def hi_lo(matrix):
    hi = matrix.astype(np.float32).astype(ml_dtypes.bfloat16)
    lo = (matrix - hi.astype(np.float64)).astype(np.float32).astype(ml_dtypes.bfloat16)
    return np.concatenate([hi, lo], axis=1)


def tables(pupil, field):
    fun = (np.cos, np.sin)
    fwd, bwd = [], []
    for b in range(2):
        for a in range(2):
            t = np.kron(halves(pupil, field, fun[a]), halves(pupil, field, fun[b]))
            fwd.append(hi_lo(t))
            rows = min(CHUNK, t.shape[0])
            bwd.append(
                np.stack([hi_lo(t[m : m + rows].T) for m in range(0, t.shape[0], rows)])
            )
    return np.stack(fwd), np.stack(bwd)


def split(x):
    hi = x.astype(BF16)
    return hi, (x - hi.astype(F32)).astype(BF16)


def dot_three(table, depth, hi, lo):
    wide = jnp.concatenate([table, table[:, :depth]], axis=1)
    return jnp.dot(wide, jnp.concatenate([hi, hi, lo], axis=0), preferred_element_type=F32)


def lane_group(shape, width):
    return lax.broadcasted_iota(jnp.int32, shape, len(shape) - 1) // width


def roll(x, shift):
    return pltpu.roll(x, shift % LANES, x.ndim - 1)


def swap_groups(blocks, width):
    n = len(blocks)
    blocks = list(blocks)
    group = lane_group(blocks[0].shape, width)
    step = 1
    while step < n:
        low = (group & step) == 0
        for i in range(n):
            if i & step:
                continue
            j = i + step
            a, b = blocks[i], blocks[j]
            blocks[i] = jnp.where(low, a, roll(b, step * width))
            blocks[j] = jnp.where(low, roll(a, -step * width), b)
        step *= 2
    return blocks


def spread_groups(x, n, width):
    group = lane_group(x.shape, width)
    out = [x]
    step = n // 2
    while step >= 1:
        low = (group & step) == 0
        made = []
        for y in out:
            up, down = roll(y, step * width), roll(y, -step * width)
            made.append(jnp.where(low, y, up))
            made.append(jnp.where(low, down, y))
        out = made
        step //= 2
    return out


def reverse_rows(x):
    row = lax.broadcasted_iota(jnp.int32, (8, LANES), 0)
    parts = []
    for i in range(x.shape[0] - 8, -1, -8):
        y = pltpu.roll(x[i : i + 8], 4, 0)
        y = jnp.where((row & 2) == 0, pltpu.roll(y, 6, 0), pltpu.roll(y, 2, 0))
        y = jnp.where((row & 1) == 0, pltpu.roll(y, 7, 0), pltpu.roll(y, 1, 0))
        parts.append(y)
    return jnp.concatenate(parts, axis=0)


def pack_kernel(n, nb, me_ref, profile_hbm, weight_hbm, amp_hbm, phase_hbm, cot_hbm, *refs):
    out_refs = refs[:n]
    profile_ref, weight_ref, amp_ref, phase_ref, cot_ref, sems = refs[n:]
    pairs = (
        (phase_hbm, phase_ref),
        (amp_hbm, amp_ref),
        (profile_hbm, profile_ref),
        (weight_hbm, weight_ref),
        (cot_hbm, cot_ref),
    )
    copies = [pltpu.make_async_copy(src, dst, sems.at[i]) for i, (src, dst) in enumerate(pairs)]
    for copy in copies:
        copy.start()
    width = LANES // n
    qp = phase_ref.shape[0] // n
    qc = cot_ref.shape[0] // n
    turn = lax.rem(n - me_ref[0], n) * width
    for copy in copies:
        copy.wait()
    for q in range(0, qp, 16):
        parts = [pltpu.roll(phase_ref[a * qp + q : a * qp + q + 16, :], turn, 1) for a in range(n)]
        for j, block in enumerate(swap_groups(parts, width)):
            hi, lo = split(block)
            out_refs[j][q : q + 16, :] = hi
            out_refs[j][qp + q : qp + q + 16, :] = lo
    for q in range(0, qp, 16):
        parts = [
            pltpu.roll(amp_ref[a * qp + q : a * qp + q + 16, :].astype(F32), turn, 1)
            for a in range(n)
        ]
        for j, block in enumerate(swap_groups(parts, width)):
            out_refs[j][2 * qp + q : 2 * qp + q + 16, :] = block.astype(BF16)

    def step(i, carry):
        at = pl.multiple_of(i * 16, 16)
        parts = [
            pltpu.roll(cot_ref[pl.ds(a * qc + at, 16), :].astype(F32), turn, 1) for a in range(n)
        ]
        for j, block in enumerate(swap_groups(parts, width)):
            out_refs[j][pl.ds(3 * qp + at, 16), :] = block.astype(BF16)
        return carry

    lax.fori_loop(0, qc // 16, step, 0, unroll=4)
    base = 3 * qp + qc
    rows = out_refs[0].shape[0] - base
    row = lax.broadcasted_iota(jnp.int32, (rows, LANES), 0)
    extra = jnp.zeros((rows, LANES), F32)
    for j in range(nb):
        for k, ref in enumerate((profile_ref, weight_ref)):
            value = jnp.full((rows, LANES), ref[j], F32)
            for part in range(3):
                piece = value.astype(BF16).astype(F32)
                extra = jnp.where(row == (2 * j + k) * 3 + part, piece, extra)
                value = value - piece
    for j in range(n):
        out_refs[j][base:, :] = extra.astype(BF16)


def sincos(x):
    turns = jnp.round(x * (2.0 / math.pi))
    r = x - turns * 1.5703125
    r = r - turns * 4.838267948966e-4
    r2 = r * r
    s = r + r * r2 * (-1.6666654611e-1 + r2 * (8.3321608736e-3 + r2 * -1.9515295891e-4))
    c = (1.0 - 0.5 * r2) + r2 * r2 * (
        4.166664568298827e-2 + r2 * (-1.388731625493765e-3 + r2 * 2.443315711809948e-5)
    )
    quad = turns.astype(jnp.int32)
    odd = (quad & 1) != 0
    sin_v = jnp.where(odd, c, s)
    cos_v = jnp.where(odd, s, c)
    sin_v = jnp.where((quad & 2) != 0, -sin_v, sin_v)
    cos_v = jnp.where(((quad + 1) & 2) != 0, -cos_v, cos_v)
    return sin_v, cos_v


def spots_kernel(n, nb, pupil, field, me_ref, pos_hbm, fwd_hbm, bwd_hbm, *refs):
    in_refs, grad_refs, aux_ref = refs[:n], refs[n : 2 * n], refs[2 * n]
    (
        phase_s, amp_s, cot_s, e_s, x_s, p_s, y_s, g_s, pg_s, pos_ref, fwd_ref, bwd_ref, sems
    ) = refs[2 * n + 1 :]
    copies = [
        pltpu.make_async_copy(pos_hbm, pos_ref, sems.at[0]),
        pltpu.make_async_copy(fwd_hbm, fwd_ref, sems.at[1]),
        pltpu.make_async_copy(bwd_hbm, bwd_ref, sems.at[2]),
    ]
    for copy in copies:
        copy.start()
    width = LANES // n
    nbins = n * nb
    qp = pupil * pupil // (n * n)
    qc = field * field // (n * n)
    half, fhalf = pupil // 2, field // 2
    wide = nb * LANES
    me = me_ref[0]
    group1 = lane_group((1, LANES), width)
    owner = [lax.rem(me + n - j, n) for j in range(n)]

    for j in range(n):
        for q in range(0, qp, 16):
            hi = in_refs[j][q : q + 16, :].astype(F32)
            lo = in_refs[j][qp + q : qp + q + 16, :].astype(F32)
            am = in_refs[j][2 * qp + q : 2 * qp + q + 16, :].astype(F32)
            turned = [(a * qp + q) % pupil >= half for a in range(n)]
            for src, dst in ((hi + lo, phase_s), (am, amp_s)):
                ways = {
                    way: spread_groups(reverse_rows(src) if way else src, n, width)
                    for way in set(turned)
                }
                for a in range(n):
                    line = (a * qp + q) // pupil * pupil + (half if turned[a] else 0)
                    part = (a * qp + q) % half
                    part = half - 16 - part if turned[a] else part
                    at = pl.multiple_of(owner[j] * (n * qp) + line + part, 16)
                    dst[pl.ds(at, 16), :] = ways[turned[a]][a]

    per = qc // field
    for j in range(n):
        low = owner[j] < n // 2
        sign = jnp.where(low, 0, 1)

        def place(i, carry):
            for q in range(0, field, 16):
                at = pl.multiple_of(3 * qp + i * field + q, 16)
                raw = in_refs[j][pl.ds(at, 16), :].astype(F32)
                raw = reverse_rows(raw) if q >= fhalf else raw
                col = field - 16 - q if q >= fhalf else q
                for a, cot in enumerate(spread_groups(raw, n, width)):
                    k1 = (owner[j] * n + a) * per + i
                    line = jnp.where(low, k1, field - 1 - k1)
                    at = pl.multiple_of(line * fhalf + col, 16)
                    cot_s[sign, int(q >= fhalf), pl.ds(at, 16), :] = cot
            return carry

        lax.fori_loop(0, per, place, 0)

    prof, wgt = [], []
    for t in range(nb):
        p_row, w_row = jnp.zeros((1, LANES), F32), jnp.zeros((1, LANES), F32)
        for j in range(n):
            extra = in_refs[j][3 * qp + qc :, :].astype(F32)
            rows = [extra[6 * t + i : 6 * t + i + 1, :] for i in range(6)]
            p_row = jnp.where(group1 == owner[j], rows[0] + rows[1] + rows[2], p_row)
            w_row = jnp.where(group1 == owner[j], rows[3] + rows[4] + rows[5], w_row)
        prof.append(p_row)
        wgt.append(w_row)
    total = sum(prof)
    step = n // 2
    while step >= 1:
        total = total + roll(total, step * width)
        step //= 2
    coef = [2.0 / (pupil * pupil) * prof[t] * wgt[t] / total for t in range(nb)]
    aux = jnp.zeros(aux_ref.shape, F32)
    row = lax.broadcasted_iota(jnp.int32, aux_ref.shape, 0)
    for t in range(nb):
        aux = jnp.where(row == nb + t, prof[t], aux)
        aux = jnp.where(row == 2 * nb + t, wgt[t], aux)
    aux_ref[...] = jnp.where(row == 3 * nb, total, aux)

    copies[0].wait()
    pos = pos_ref[...]
    near = jnp.zeros_like(pos)
    for d, one in enumerate(spread_groups(pos, n, width)):
        near = jnp.where(me == d, one, near)
    shift = math.pi / field
    tilt_x, tilt_y = [], []
    for t in range(nb):
        kappa = ELONG * (2.0 * (group1 * nb + t).astype(F32) / (nbins - 1) - 1.0)
        tilt_x.append(kappa * near[0:1, :] + shift)
        tilt_y.append(kappa * near[1:2, :] + shift)

    row = lax.broadcasted_iota(jnp.int32, (pupil, LANES), 0)
    u_rows = jnp.where(row < half, row, pupil + half - 1 - row).astype(F32) - (pupil - 1) / 2.0
    lean = [u_rows * tilt_x[t] for t in range(nb)]

    def fields(i, carry):
        at16 = pl.multiple_of(i * half, half)
        for t in range(nb):
            found = []
            for r in (i, pupil - 1 - i):
                at = pl.multiple_of(r * pupil, pupil)
                v = r.astype(F32) - (pupil - 1) / 2.0
                am = amp_s[pl.ds(at, pupil), :]
                sin_v, cos_v = sincos(phase_s[pl.ds(at, pupil), :] + (lean[t] + v * tilt_y[t]))
                one = (am * cos_v, am * sin_v)
                for k in range(2):
                    e_s[t, k, pl.ds(at, pupil), :] = one[k]
                found.append(one)
            for k in range(2):
                even, odd = found[1][k] + found[0][k], found[1][k] - found[0][k]
                classes = (
                    even[half:] + even[:half],
                    odd[half:] + odd[:half],
                    even[half:] - even[:half],
                    odd[half:] - odd[:half],
                )
                lanes = pl.ds(k * wide + t * LANES, LANES)
                for c, x in enumerate(classes):
                    hi, lo = split(x)
                    x_s[c, 0, pl.ds(at16, half), lanes] = hi
                    x_s[c, 1, pl.ds(at16, half), lanes] = lo
        return carry

    lax.fori_loop(0, half, fields, 0)

    depth = half * half
    rows_all = fhalf * fhalf
    chunk = min(CHUNK, rows_all)
    copies[1].wait()
    copies[2].wait()

    def images(m, first):
        base = m * chunk
        for c in range(4):
            table = fwd_ref[c, pl.ds(pl.multiple_of(base, chunk), chunk), :]
            for k in range(2):
                lanes = pl.ds(k * wide, wide)
                p_s[c, k] = dot_three(table, depth, x_s[c, 0, :, lanes], x_s[c, 1, :, lanes])

        def weigh(i, carry):
            at = pl.multiple_of(i * 16, 16)
            there = pl.multiple_of(base + i * 16, 16)
            cot = [cot_s[a, b, pl.ds(there, 16), :] for a in range(2) for b in range(2)]
            for t in range(nb):
                lanes = pl.ds(t * LANES, LANES)
                re = [p_s[c, 0, pl.ds(at, 16), lanes] for c in range(4)]
                im = [p_s[c, 1, pl.ds(at, 16), lanes] for c in range(4)]
                s0, s1, s2, s3 = re[0] + im[1], re[0] - im[1], im[2] - re[3], im[2] + re[3]
                y = [cot[0] * (s0 + s2), cot[1] * (s0 - s2), cot[2] * (s1 + s3), cot[3] * (s1 - s3)]
                s0, s1, s2, s3 = im[0] - re[1], im[0] + re[1], re[2] + im[3], re[2] - im[3]
                z = [cot[0] * (s0 - s2), cot[1] * (s0 + s2), cot[2] * (s1 - s3), cot[3] * (s1 + s3)]
                yp, ym, yd, ye = y[0] + y[1], y[2] + y[3], y[0] - y[1], y[2] - y[3]
                zp, zm, zd, ze = z[0] + z[1], z[2] + z[3], z[0] - z[1], z[2] - z[3]
                back = (
                    (yp + ym, zp + zm),
                    (zm - zp, yp - ym),
                    (-ze - zd, yd + ye),
                    (ye - yd, ze - zd),
                )
                for c in range(4):
                    for k in range(2):
                        hi, lo = split(back[c][k])
                        lanes = pl.ds(k * wide + t * LANES, LANES)
                        y_s[c, 0, pl.ds(at, 16), lanes] = hi
                        y_s[c, 1, pl.ds(at, 16), lanes] = lo
            return carry

        lax.fori_loop(0, chunk // 16, weigh, 0, unroll=2)
        for c in range(4):
            table = bwd_ref[c, m]
            for k in range(2):
                lanes = pl.ds(k * wide, wide)
                out = dot_three(table, chunk, y_s[c, 0, :, lanes], y_s[c, 1, :, lanes])
                g_s[c, k] = out if first else g_s[c, k] + out

    images(0, True)
    if rows_all > chunk:
        lax.fori_loop(1, rows_all // chunk, lambda m, carry: images(m, False) or carry, 0)

    def products(i, stats):
        stats = list(stats)
        at16 = pl.multiple_of(i * half, half)
        grads = [jnp.zeros((pupil, LANES), F32) for _ in range(2)]
        spots = [pl.multiple_of(r * pupil, pupil) for r in (i, pupil - 1 - i)]
        for t in range(nb):
            found = []
            for k in range(2):
                g = [g_s[c, k, pl.ds(at16, half), pl.ds(t * LANES, LANES)] for c in range(4)]
                even = jnp.concatenate([g[0] - g[2], g[0] + g[2]], axis=0)
                odd = jnp.concatenate([g[1] - g[3], g[1] + g[3]], axis=0)
                found.append((even - odd, even + odd))
            for which in range(2):
                e_re = e_s[t, 0, pl.ds(spots[which], pupil), :]
                e_im = e_s[t, 1, pl.ds(spots[which], pupil), :]
                g_re, g_im = found[0][which], found[1][which]
                stats[t] = stats[t] + (e_re * g_re + e_im * g_im)
                grads[which] = grads[which] + coef[t] * (e_re * g_im - e_im * g_re)
        for which in range(2):
            grad = grads[which]
            step = n // 2
            while step >= 1:
                grad = grad + roll(grad, step * width)
                step //= 2
            grad = jnp.concatenate([grad[:half], reverse_rows(grad[half:])], axis=0)
            pg_s[pl.ds(spots[which], pupil), :] = grad
        return tuple(stats)

    stats = lax.fori_loop(0, half, products, tuple(jnp.zeros((pupil, LANES), F32) for _ in range(nb)))

    lane = lax.broadcasted_iota(jnp.int32, (1, LANES), 1)
    sums = jnp.zeros((1, LANES), F32)
    for t in range(nb):
        stat = jnp.sum(stats[t], axis=0, keepdims=True) * (1.0 / (pupil * pupil))
        step = 1
        while step < width:
            stat = stat + roll(stat, step)
            step *= 2
        sums = jnp.where(lane % width == width - 1 - t, roll(stat, -t), sums)
    group = lane_group((8, LANES), width)
    for k, ref in enumerate(grad_refs):
        d = lax.rem(me + k, n)
        for q in range(0, qp, 8):
            out = jnp.zeros((8, LANES), F32)
            for a in range(n):
                at = pl.multiple_of((d * n + a) * qp + q, 8)
                out = jnp.where(group == a, pg_s[pl.ds(at, 8), :], out)
            ref[q : q + 8, :] = out
        ref[qp : qp + 8, :] = jnp.broadcast_to(sums, (8, LANES))


def sum_kernel(n, *refs):
    refs[n][...] = jnp.broadcast_to(sum(refs[k][...] for k in range(n))[None], refs[n].shape)


def grad_kernel(n, me_ref, *refs):
    width = LANES // n
    out_ref = refs[n]
    qp = out_ref.shape[0] // n
    turn = me_ref[0] * width
    for q in range(0, qp, 8):
        parts = [refs[(n - i) % n][q : q + 8, :] for i in range(n)]
        for a, block in enumerate(swap_groups(parts, width)):
            out_ref[a * qp + q : a * qp + q + 8, :] = pltpu.roll(block, turn, 1)


def profile_kernel(n, nb, nsub_all, me_ref, aux_ref, stat_ref, prof_ref):
    width = LANES // n
    lane = lax.broadcasted_iota(jnp.int32, (1, LANES), 1)
    stat = jnp.sum(stat_ref[...], axis=0)[0:1, :]
    aux = aux_ref[...]
    total = jnp.max(aux[3 * nb : 3 * nb + 1, :])
    centre = jnp.zeros((1, LANES), F32)
    own = []
    for t in range(nb):
        prof, wgt = aux[nb + t : nb + t + 1], aux[2 * nb + t : 2 * nb + t + 1]
        term = stat * wgt
        centre += jnp.where(lane % width == width - 1 - t, term * prof, 0.0)
        own.append(jnp.sum(jnp.where(lane == (me_ref[0] + 1) * width - 1 - t, term, 0.0)))
    centre = jnp.sum(centre)
    for t in range(nb):
        prof_ref[t] = (own[t] / total - centre / (total * total)) / nsub_all


def local(cotangent, amplitude, phase, position, profile, alt_weight):
    n = lax.axis_size("alt")
    n_sub = lax.axis_size("sub")
    nsub_all = n_sub * phase.shape[1]
    nb = profile.shape[0]
    pupil = math.isqrt(n * phase.shape[0])
    field = math.isqrt(n * cotangent.shape[0])
    qp = phase.shape[0] // n
    qc = cotangent.shape[0] // n
    extra = -(-6 * nb // 16) * 16
    me = lax.axis_index("alt").astype(jnp.int32).reshape(1)
    smem = pl.BlockSpec(memory_space=pltpu.SMEM)
    vmem = pl.BlockSpec(memory_space=pltpu.VMEM)
    hbm = pl.BlockSpec(memory_space=pltpu.HBM)
    params = pltpu.CompilerParams(vmem_limit_bytes=VMEM_LIMIT)

    def keep(*arrays):
        return [pltpu.with_memory_space_constraint(x, pltpu.HBM) for x in arrays]

    def exchange(blocks):
        return [blocks[0]] + [
            lax.ppermute(blocks[j], "alt", [(i, (i + j) % n) for i in range(n)])
            for j in range(1, n)
        ]

    blocks = pl.pallas_call(
        functools.partial(pack_kernel, n, nb),
        out_shape=[jax.ShapeDtypeStruct((3 * qp + qc + extra, LANES), BF16)] * n,
        in_specs=[smem] + [hbm] * 5,
        out_specs=[vmem] * n,
        scratch_shapes=[
            pltpu.SMEM(profile.shape, F32),
            pltpu.SMEM(alt_weight.shape, F32),
            pltpu.VMEM(amplitude.shape, BF16),
            pltpu.VMEM(phase.shape, F32),
            pltpu.VMEM(cotangent.shape, BF16),
            pltpu.SemaphoreType.DMA((5,)),
        ],
        compiler_params=params,
        name="pack",
    )(me, *keep(profile, alt_weight, amplitude, phase, cotangent))
    blocks = exchange(blocks)

    fwd, bwd = (jnp.asarray(x) for x in tables(pupil, field))
    depth = pupil * pupil // 4
    rows_all = field * field // 4
    chunk = min(CHUNK, rows_all)
    wide = nb * LANES
    aux_rows = -(-(3 * nb + 1) // 8) * 8
    *grads, aux = pl.pallas_call(
        functools.partial(spots_kernel, n, nb, pupil, field),
        out_shape=[jax.ShapeDtypeStruct((qp + 8, LANES), F32)] * n
        + [jax.ShapeDtypeStruct((aux_rows, LANES), F32)],
        in_specs=[smem] + [hbm] * 3 + [vmem] * n,
        out_specs=[vmem] * (n + 1),
        scratch_shapes=[
            pltpu.VMEM((pupil * pupil, LANES), F32),
            pltpu.VMEM((pupil * pupil, LANES), F32),
            pltpu.VMEM((2, 2, rows_all, LANES), F32),
            pltpu.VMEM((nb, 2, pupil * pupil, LANES), F32),
            pltpu.VMEM((4, 2, depth, 2 * wide), BF16),
            pltpu.VMEM((4, 2, chunk, wide), F32),
            pltpu.VMEM((4, 2, chunk, 2 * wide), BF16),
            pltpu.VMEM((4, 2, depth, wide), F32),
            pltpu.VMEM((pupil * pupil, LANES), F32),
            pltpu.VMEM(position.shape, F32),
            pltpu.VMEM(fwd.shape, BF16),
            pltpu.VMEM(bwd.shape, BF16),
            pltpu.SemaphoreType.DMA((3,)),
        ],
        compiler_params=params,
        name="spots",
    )(me, *keep(position, fwd, bwd), *blocks)
    grads = exchange(grads)
    stat = pl.pallas_call(
        functools.partial(sum_kernel, n),
        out_shape=jax.ShapeDtypeStruct((n_sub, 8, LANES), F32),
        grid=(1,),
        in_specs=[pl.BlockSpec((8, LANES), lambda i: (qp // 8, 0))] * n,
        out_specs=pl.BlockSpec((n_sub, 8, LANES), lambda i: (0, 0, 0)),
        compiler_params=params,
        name="group_sum",
    )(*grads)
    stat = lax.all_to_all(stat, "sub", 0, 0)
    phase_grad = pl.pallas_call(
        functools.partial(grad_kernel, n),
        out_shape=jax.ShapeDtypeStruct(phase.shape, F32),
        in_specs=[smem] + [vmem] * n,
        out_specs=vmem,
        compiler_params=params,
        name="gradient",
    )(me, *grads)
    profile_grad = pl.pallas_call(
        functools.partial(profile_kernel, n, nb, nsub_all),
        out_shape=jax.ShapeDtypeStruct(profile.shape, F32),
        in_specs=[smem, vmem, vmem],
        out_specs=smem,
        compiler_params=params,
        name="profile",
    )(me, aux, stat)
    return phase_grad, profile_grad


def solution(mesh):
    placed = (P("alt", "sub"), P("alt", "sub"), P("alt", "sub"), P(None, "sub"), P("alt"), P("alt"))
    return jax.shard_map(
        local, mesh=mesh, in_specs=placed, out_specs=(P("alt", "sub"), P("alt")), check_vma=False
    )
```

```python
import functools
import math

import jax
import jax.numpy as jnp
import ml_dtypes
import numpy as np
from jax import lax
from jax.experimental import pallas as pl
from jax.experimental.pallas import tpu as pltpu
from jax.sharding import PartitionSpec as P

ELONG = 0.75
LANES = 128
VMEM_LIMIT = 44 * 1024 * 1024
F32 = jnp.float32
BF16 = jnp.bfloat16


CHUNK = 1024


def halves(pupil, field, fun):
    freq = np.arange(field // 2) + 0.5
    place = (pupil - 1) / 2.0 - np.arange(pupil // 2)
    return fun(2.0 * np.pi / field * np.outer(freq, place))


def hi_lo(matrix):
    hi = matrix.astype(np.float32).astype(ml_dtypes.bfloat16)
    lo = (matrix - hi.astype(np.float64)).astype(np.float32).astype(ml_dtypes.bfloat16)
    return np.concatenate([hi, lo], axis=1)


def tables(pupil, field):
    fun = (np.cos, np.sin)
    fwd, bwd = [], []
    for b in range(2):
        for a in range(2):
            t = np.kron(halves(pupil, field, fun[a]), halves(pupil, field, fun[b]))
            fwd.append(hi_lo(t))
            rows = min(CHUNK, t.shape[0])
            bwd.append(
                np.stack([hi_lo(t[m : m + rows].T) for m in range(0, t.shape[0], rows)])
            )
    return np.stack(fwd), np.stack(bwd)


def split(x):
    hi = x.astype(BF16)
    return hi, (x - hi.astype(F32)).astype(BF16)


def dot_three(table, depth, hi, lo):
    wide = jnp.concatenate([table, table[:, :depth]], axis=1)
    return jnp.dot(wide, jnp.concatenate([hi, hi, lo], axis=0), preferred_element_type=F32)


def lane_group(shape, width):
    return lax.broadcasted_iota(jnp.int32, shape, len(shape) - 1) // width


def roll(x, shift):
    return pltpu.roll(x, shift % LANES, x.ndim - 1)


def swap_groups(blocks, width):
    n = len(blocks)
    blocks = list(blocks)
    group = lane_group(blocks[0].shape, width)
    step = 1
    while step < n:
        low = (group & step) == 0
        for i in range(n):
            if i & step:
                continue
            j = i + step
            a, b = blocks[i], blocks[j]
            blocks[i] = jnp.where(low, a, roll(b, step * width))
            blocks[j] = jnp.where(low, roll(a, -step * width), b)
        step *= 2
    return blocks


def spread_groups(x, n, width):
    group = lane_group(x.shape, width)
    out = [x]
    step = n // 2
    while step >= 1:
        low = (group & step) == 0
        made = []
        for y in out:
            up, down = roll(y, step * width), roll(y, -step * width)
            made.append(jnp.where(low, y, up))
            made.append(jnp.where(low, down, y))
        out = made
        step //= 2
    return out


def reverse_rows(x):
    row = lax.broadcasted_iota(jnp.int32, (8, LANES), 0)
    parts = []
    for i in range(x.shape[0] - 8, -1, -8):
        y = pltpu.roll(x[i : i + 8], 4, 0)
        y = jnp.where((row & 2) == 0, pltpu.roll(y, 6, 0), pltpu.roll(y, 2, 0))
        y = jnp.where((row & 1) == 0, pltpu.roll(y, 7, 0), pltpu.roll(y, 1, 0))
        parts.append(y)
    return jnp.concatenate(parts, axis=0)


def pack_kernel(n, nb, me_ref, profile_hbm, weight_hbm, amp_hbm, phase_hbm, cot_hbm, *refs):
    out_refs = refs[:n]
    profile_ref, weight_ref, amp_ref, phase_ref, cot_ref, sems = refs[n:]
    pairs = (
        (phase_hbm, phase_ref),
        (amp_hbm, amp_ref),
        (profile_hbm, profile_ref),
        (weight_hbm, weight_ref),
        (cot_hbm, cot_ref),
    )
    copies = [pltpu.make_async_copy(src, dst, sems.at[i]) for i, (src, dst) in enumerate(pairs)]
    for copy in copies:
        copy.start()
    width = LANES // n
    qp = phase_ref.shape[0] // n
    qc = cot_ref.shape[0] // n
    turn = lax.rem(n - me_ref[0], n) * width
    for copy in copies:
        copy.wait()
    for q in range(0, qp, 16):
        parts = [pltpu.roll(phase_ref[a * qp + q : a * qp + q + 16, :], turn, 1) for a in range(n)]
        for j, block in enumerate(swap_groups(parts, width)):
            hi, lo = split(block)
            out_refs[j][q : q + 16, :] = hi
            out_refs[j][qp + q : qp + q + 16, :] = lo
    for q in range(0, qp, 16):
        parts = [
            pltpu.roll(amp_ref[a * qp + q : a * qp + q + 16, :].astype(F32), turn, 1)
            for a in range(n)
        ]
        for j, block in enumerate(swap_groups(parts, width)):
            out_refs[j][2 * qp + q : 2 * qp + q + 16, :] = block.astype(BF16)

    def step(i, carry):
        at = pl.multiple_of(i * 16, 16)
        parts = [
            pltpu.roll(cot_ref[pl.ds(a * qc + at, 16), :].astype(F32), turn, 1) for a in range(n)
        ]
        for j, block in enumerate(swap_groups(parts, width)):
            out_refs[j][pl.ds(3 * qp + at, 16), :] = block.astype(BF16)
        return carry

    lax.fori_loop(0, qc // 16, step, 0, unroll=4)
    base = 3 * qp + qc
    rows = out_refs[0].shape[0] - base
    row = lax.broadcasted_iota(jnp.int32, (rows, LANES), 0)
    extra = jnp.zeros((rows, LANES), F32)
    for j in range(nb):
        for k, ref in enumerate((profile_ref, weight_ref)):
            value = jnp.full((rows, LANES), ref[j], F32)
            for part in range(3):
                piece = value.astype(BF16).astype(F32)
                extra = jnp.where(row == (2 * j + k) * 3 + part, piece, extra)
                value = value - piece
    for j in range(n):
        out_refs[j][base:, :] = extra.astype(BF16)


def sincos(x):
    turns = jnp.round(x * (2.0 / math.pi))
    r = x - turns * 1.5703125
    r = r - turns * 4.838267948966e-4
    r2 = r * r
    s = r + r * r2 * (-1.6666654611e-1 + r2 * (8.3321608736e-3 + r2 * -1.9515295891e-4))
    c = (1.0 - 0.5 * r2) + r2 * r2 * (
        4.166664568298827e-2 + r2 * (-1.388731625493765e-3 + r2 * 2.443315711809948e-5)
    )
    quad = turns.astype(jnp.int32)
    odd = (quad & 1) != 0
    sin_v = jnp.where(odd, c, s)
    cos_v = jnp.where(odd, s, c)
    sin_v = jnp.where((quad & 2) != 0, -sin_v, sin_v)
    cos_v = jnp.where(((quad + 1) & 2) != 0, -cos_v, cos_v)
    return sin_v, cos_v


def spots_kernel(n, nb, pupil, field, me_ref, pos_hbm, fwd_hbm, bwd_hbm, *refs):
    in_refs, grad_refs, aux_ref, stat_ref = refs[:n], refs[n : 2 * n], refs[2 * n], refs[2 * n + 1]
    (
        phase_s, amp_s, cot_s, e_s, x_s, p_s, y_s, g_s, pg_s, pos_ref, fwd_ref, bwd_ref, sems
    ) = refs[2 * n + 2 :]
    copies = [
        pltpu.make_async_copy(pos_hbm, pos_ref, sems.at[0]),
        pltpu.make_async_copy(fwd_hbm, fwd_ref, sems.at[1]),
        pltpu.make_async_copy(bwd_hbm, bwd_ref, sems.at[2]),
    ]
    for copy in copies:
        copy.start()
    width = LANES // n
    nbins = n * nb
    qp = pupil * pupil // (n * n)
    qc = field * field // (n * n)
    half, fhalf = pupil // 2, field // 2
    wide = nb * LANES
    me = me_ref[0]
    group1 = lane_group((1, LANES), width)
    owner = [lax.rem(me + n - j, n) for j in range(n)]

    for j in range(n):
        for q in range(0, qp, 16):
            hi = in_refs[j][q : q + 16, :].astype(F32)
            lo = in_refs[j][qp + q : qp + q + 16, :].astype(F32)
            am = in_refs[j][2 * qp + q : 2 * qp + q + 16, :].astype(F32)
            turned = [(a * qp + q) % pupil >= half for a in range(n)]
            for src, dst in ((hi + lo, phase_s), (am, amp_s)):
                ways = {
                    way: spread_groups(reverse_rows(src) if way else src, n, width)
                    for way in set(turned)
                }
                for a in range(n):
                    line = (a * qp + q) // pupil * pupil + (half if turned[a] else 0)
                    part = (a * qp + q) % half
                    part = half - 16 - part if turned[a] else part
                    at = pl.multiple_of(owner[j] * (n * qp) + line + part, 16)
                    dst[pl.ds(at, 16), :] = ways[turned[a]][a]

    per = qc // field
    for j in range(n):
        low = owner[j] < n // 2
        sign = jnp.where(low, 0, 1)

        def place(i, carry):
            for q in range(0, field, 16):
                at = pl.multiple_of(3 * qp + i * field + q, 16)
                raw = in_refs[j][pl.ds(at, 16), :].astype(F32)
                raw = reverse_rows(raw) if q >= fhalf else raw
                col = field - 16 - q if q >= fhalf else q
                for a, cot in enumerate(spread_groups(raw, n, width)):
                    k1 = (owner[j] * n + a) * per + i
                    line = jnp.where(low, k1, field - 1 - k1)
                    at = pl.multiple_of(line * fhalf + col, 16)
                    cot_s[sign, int(q >= fhalf), pl.ds(at, 16), :] = cot
            return carry

        lax.fori_loop(0, per, place, 0)

    prof, wgt = [], []
    for t in range(nb):
        p_row, w_row = jnp.zeros((1, LANES), F32), jnp.zeros((1, LANES), F32)
        for j in range(n):
            extra = in_refs[j][3 * qp + qc :, :].astype(F32)
            rows = [extra[6 * t + i : 6 * t + i + 1, :] for i in range(6)]
            p_row = jnp.where(group1 == owner[j], rows[0] + rows[1] + rows[2], p_row)
            w_row = jnp.where(group1 == owner[j], rows[3] + rows[4] + rows[5], w_row)
        prof.append(p_row)
        wgt.append(w_row)
    total = sum(prof)
    step = n // 2
    while step >= 1:
        total = total + roll(total, step * width)
        step //= 2
    coef = [2.0 / (pupil * pupil) * prof[t] * wgt[t] / total for t in range(nb)]
    aux = jnp.zeros(aux_ref.shape, F32)
    row = lax.broadcasted_iota(jnp.int32, aux_ref.shape, 0)
    for t in range(nb):
        aux = jnp.where(row == nb + t, prof[t], aux)
        aux = jnp.where(row == 2 * nb + t, wgt[t], aux)
    aux_ref[...] = jnp.where(row == 3 * nb, total, aux)

    copies[0].wait()
    pos = pos_ref[...]
    near = jnp.zeros_like(pos)
    for d, one in enumerate(spread_groups(pos, n, width)):
        near = jnp.where(me == d, one, near)
    shift = math.pi / field
    tilt_x, tilt_y = [], []
    for t in range(nb):
        kappa = ELONG * (2.0 * (group1 * nb + t).astype(F32) / (nbins - 1) - 1.0)
        tilt_x.append(kappa * near[0:1, :] + shift)
        tilt_y.append(kappa * near[1:2, :] + shift)

    row = lax.broadcasted_iota(jnp.int32, (pupil, LANES), 0)
    u_rows = jnp.where(row < half, row, pupil + half - 1 - row).astype(F32) - (pupil - 1) / 2.0
    lean = [u_rows * tilt_x[t] for t in range(nb)]

    def fields(i, carry):
        at16 = pl.multiple_of(i * half, half)
        for t in range(nb):
            found = []
            for r in (i, pupil - 1 - i):
                at = pl.multiple_of(r * pupil, pupil)
                v = r.astype(F32) - (pupil - 1) / 2.0
                am = amp_s[pl.ds(at, pupil), :]
                sin_v, cos_v = sincos(phase_s[pl.ds(at, pupil), :] + (lean[t] + v * tilt_y[t]))
                one = (am * cos_v, am * sin_v)
                for k in range(2):
                    e_s[t, k, pl.ds(at, pupil), :] = one[k]
                found.append(one)
            for k in range(2):
                even, odd = found[1][k] + found[0][k], found[1][k] - found[0][k]
                classes = (
                    even[half:] + even[:half],
                    odd[half:] + odd[:half],
                    even[half:] - even[:half],
                    odd[half:] - odd[:half],
                )
                lanes = pl.ds(k * wide + t * LANES, LANES)
                for c, x in enumerate(classes):
                    hi, lo = split(x)
                    x_s[c, 0, pl.ds(at16, half), lanes] = hi
                    x_s[c, 1, pl.ds(at16, half), lanes] = lo
        return carry

    lax.fori_loop(0, half, fields, 0)

    depth = half * half
    rows_all = fhalf * fhalf
    chunk = min(CHUNK, rows_all)
    copies[1].wait()
    copies[2].wait()

    def images(m, first):
        base = m * chunk
        for c in range(4):
            table = fwd_ref[c, pl.ds(pl.multiple_of(base, chunk), chunk), :]
            for k in range(2):
                lanes = pl.ds(k * wide, wide)
                p_s[c, k] = dot_three(table, depth, x_s[c, 0, :, lanes], x_s[c, 1, :, lanes])

        def weigh(i, carry):
            at = pl.multiple_of(i * 16, 16)
            there = pl.multiple_of(base + i * 16, 16)
            cot = [cot_s[a, b, pl.ds(there, 16), :] for a in range(2) for b in range(2)]
            for t in range(nb):
                lanes = pl.ds(t * LANES, LANES)
                re = [p_s[c, 0, pl.ds(at, 16), lanes] for c in range(4)]
                im = [p_s[c, 1, pl.ds(at, 16), lanes] for c in range(4)]
                s0, s1, s2, s3 = re[0] + im[1], re[0] - im[1], im[2] - re[3], im[2] + re[3]
                y = [cot[0] * (s0 + s2), cot[1] * (s0 - s2), cot[2] * (s1 + s3), cot[3] * (s1 - s3)]
                s0, s1, s2, s3 = im[0] - re[1], im[0] + re[1], re[2] + im[3], re[2] - im[3]
                z = [cot[0] * (s0 - s2), cot[1] * (s0 + s2), cot[2] * (s1 - s3), cot[3] * (s1 + s3)]
                yp, ym, yd, ye = y[0] + y[1], y[2] + y[3], y[0] - y[1], y[2] - y[3]
                zp, zm, zd, ze = z[0] + z[1], z[2] + z[3], z[0] - z[1], z[2] - z[3]
                back = (
                    (yp + ym, zp + zm),
                    (zm - zp, yp - ym),
                    (-ze - zd, yd + ye),
                    (ye - yd, ze - zd),
                )
                for c in range(4):
                    for k in range(2):
                        hi, lo = split(back[c][k])
                        lanes = pl.ds(k * wide + t * LANES, LANES)
                        y_s[c, 0, pl.ds(at, 16), lanes] = hi
                        y_s[c, 1, pl.ds(at, 16), lanes] = lo
            return carry

        lax.fori_loop(0, chunk // 16, weigh, 0, unroll=2)
        for c in range(4):
            table = bwd_ref[c, m]
            for k in range(2):
                lanes = pl.ds(k * wide, wide)
                out = dot_three(table, chunk, y_s[c, 0, :, lanes], y_s[c, 1, :, lanes])
                g_s[c, k] = out if first else g_s[c, k] + out

    images(0, True)
    if rows_all > chunk:
        lax.fori_loop(1, rows_all // chunk, lambda m, carry: images(m, False) or carry, 0)

    def products(i, stats):
        stats = list(stats)
        at16 = pl.multiple_of(i * half, half)
        grads = [jnp.zeros((pupil, LANES), F32) for _ in range(2)]
        spots = [pl.multiple_of(r * pupil, pupil) for r in (i, pupil - 1 - i)]
        for t in range(nb):
            found = []
            for k in range(2):
                g = [g_s[c, k, pl.ds(at16, half), pl.ds(t * LANES, LANES)] for c in range(4)]
                even = jnp.concatenate([g[0] - g[2], g[0] + g[2]], axis=0)
                odd = jnp.concatenate([g[1] - g[3], g[1] + g[3]], axis=0)
                found.append((even - odd, even + odd))
            for which in range(2):
                e_re = e_s[t, 0, pl.ds(spots[which], pupil), :]
                e_im = e_s[t, 1, pl.ds(spots[which], pupil), :]
                g_re, g_im = found[0][which], found[1][which]
                stats[t] = stats[t] + (e_re * g_re + e_im * g_im)
                grads[which] = grads[which] + coef[t] * (e_re * g_im - e_im * g_re)
        for which in range(2):
            grad = grads[which]
            step = n // 2
            while step >= 1:
                grad = grad + roll(grad, step * width)
                step //= 2
            grad = jnp.concatenate([grad[:half], reverse_rows(grad[half:])], axis=0)
            pg_s[pl.ds(spots[which], pupil), :] = grad
        return tuple(stats)

    stats = lax.fori_loop(0, half, products, tuple(jnp.zeros((pupil, LANES), F32) for _ in range(nb)))

    lane = lax.broadcasted_iota(jnp.int32, (1, LANES), 1)
    sums = jnp.zeros((1, LANES), F32)
    for t in range(nb):
        stat = jnp.sum(stats[t], axis=0, keepdims=True) * (1.0 / (pupil * pupil))
        step = 1
        while step < width:
            stat = stat + roll(stat, step)
            step *= 2
        sums = jnp.where(lane % width == width - 1 - t, roll(stat, -t), sums)
    stat_ref[...] = jnp.broadcast_to(sums, stat_ref.shape)
    group = lane_group((8, LANES), width)
    for k, ref in enumerate(grad_refs):
        d = lax.rem(me + k, n)
        for q in range(0, qp, 8):
            out = jnp.zeros((8, LANES), F32)
            for a in range(n):
                at = pl.multiple_of((d * n + a) * qp + q, 8)
                out = jnp.where(group == a, pg_s[pl.ds(at, 8), :], out)
            ref[q : q + 8, :] = out


def final_kernel(n, nb, nsub_all, me_ref, aux_ref, stat_ref, *refs):
    width = LANES // n
    out_ref, prof_ref = refs[n:]
    qp = out_ref.shape[0] // n
    turn = me_ref[0] * width
    for q in range(0, qp, 8):
        parts = [refs[(n - i) % n][q : q + 8, :] for i in range(n)]
        for a, block in enumerate(swap_groups(parts, width)):
            out_ref[a * qp + q : a * qp + q + 8, :] = pltpu.roll(block, turn, 1)
    lane = lax.broadcasted_iota(jnp.int32, (1, LANES), 1)
    stat = jnp.sum(stat_ref[...], axis=0, keepdims=True)
    aux = aux_ref[...]
    total = jnp.max(aux[3 * nb : 3 * nb + 1, :])
    centre = jnp.zeros((1, LANES), F32)
    own = []
    for t in range(nb):
        prof, wgt = aux[nb + t : nb + t + 1], aux[2 * nb + t : 2 * nb + t + 1]
        term = stat * wgt
        centre += jnp.where(lane % width == width - 1 - t, term * prof, 0.0)
        own.append(jnp.sum(jnp.where(lane == (me_ref[0] + 1) * width - 1 - t, term, 0.0)))
    centre = jnp.sum(centre)
    for t in range(nb):
        prof_ref[t] = (own[t] / total - centre / (total * total)) / nsub_all


def local(cotangent, amplitude, phase, position, profile, alt_weight):
    n = lax.axis_size("alt")
    n_sub = lax.axis_size("sub")
    nsub_all = n_sub * phase.shape[1]
    nb = profile.shape[0]
    pupil = math.isqrt(n * phase.shape[0])
    field = math.isqrt(n * cotangent.shape[0])
    qp = phase.shape[0] // n
    qc = cotangent.shape[0] // n
    extra = -(-6 * nb // 16) * 16
    me = lax.axis_index("alt").astype(jnp.int32).reshape(1)
    smem = pl.BlockSpec(memory_space=pltpu.SMEM)
    vmem = pl.BlockSpec(memory_space=pltpu.VMEM)
    hbm = pl.BlockSpec(memory_space=pltpu.HBM)
    params = pltpu.CompilerParams(vmem_limit_bytes=VMEM_LIMIT)

    def keep(*arrays):
        return [pltpu.with_memory_space_constraint(x, pltpu.HBM) for x in arrays]

    def exchange(blocks):
        return [blocks[0]] + [
            lax.ppermute(blocks[j], "alt", [(i, (i + j) % n) for i in range(n)])
            for j in range(1, n)
        ]

    blocks = pl.pallas_call(
        functools.partial(pack_kernel, n, nb),
        out_shape=[jax.ShapeDtypeStruct((3 * qp + qc + extra, LANES), BF16)] * n,
        in_specs=[smem] + [hbm] * 5,
        out_specs=[vmem] * n,
        scratch_shapes=[
            pltpu.SMEM(profile.shape, F32),
            pltpu.SMEM(alt_weight.shape, F32),
            pltpu.VMEM(amplitude.shape, BF16),
            pltpu.VMEM(phase.shape, F32),
            pltpu.VMEM(cotangent.shape, BF16),
            pltpu.SemaphoreType.DMA((5,)),
        ],
        compiler_params=params,
        name="pack",
    )(me, *keep(profile, alt_weight, amplitude, phase, cotangent))
    blocks = exchange(blocks)

    fwd, bwd = (jnp.asarray(x) for x in tables(pupil, field))
    depth = pupil * pupil // 4
    rows_all = field * field // 4
    chunk = min(CHUNK, rows_all)
    wide = nb * LANES
    aux_rows = -(-(3 * nb + 1) // 8) * 8
    *grads, aux, stat = pl.pallas_call(
        functools.partial(spots_kernel, n, nb, pupil, field),
        out_shape=[jax.ShapeDtypeStruct((qp, LANES), F32)] * n
        + [jax.ShapeDtypeStruct((rows, LANES), F32) for rows in (aux_rows, n_sub * n)],
        in_specs=[smem] + [hbm] * 3 + [vmem] * n,
        out_specs=[vmem] * (n + 2),
        scratch_shapes=[
            pltpu.VMEM((pupil * pupil, LANES), F32),
            pltpu.VMEM((pupil * pupil, LANES), F32),
            pltpu.VMEM((2, 2, rows_all, LANES), F32),
            pltpu.VMEM((nb, 2, pupil * pupil, LANES), F32),
            pltpu.VMEM((4, 2, depth, 2 * wide), BF16),
            pltpu.VMEM((4, 2, chunk, wide), F32),
            pltpu.VMEM((4, 2, chunk, 2 * wide), BF16),
            pltpu.VMEM((4, 2, depth, wide), F32),
            pltpu.VMEM((pupil * pupil, LANES), F32),
            pltpu.VMEM(position.shape, F32),
            pltpu.VMEM(fwd.shape, BF16),
            pltpu.VMEM(bwd.shape, BF16),
            pltpu.SemaphoreType.DMA((3,)),
        ],
        compiler_params=params,
        name="spots",
    )(me, *keep(position, fwd, bwd), *blocks)
    stat = lax.all_to_all(stat, ("sub", "alt"), 0, 0, tiled=True)
    grads = exchange(grads)
    return pl.pallas_call(
        functools.partial(final_kernel, n, nb, nsub_all),
        out_shape=(
            jax.ShapeDtypeStruct(phase.shape, F32),
            jax.ShapeDtypeStruct(profile.shape, F32),
        ),
        in_specs=[smem, vmem, vmem] + [vmem] * n,
        out_specs=(vmem, smem),
        compiler_params=params,
        name="finish",
    )(me, aux, stat, *grads)


def solution(mesh):
    placed = (P("alt", "sub"), P("alt", "sub"), P("alt", "sub"), P(None, "sub"), P("alt"), P("alt"))
    return jax.shard_map(
        local, mesh=mesh, in_specs=placed, out_specs=(P("alt", "sub"), P("alt")), check_vma=False
    )
```

```python
import functools
import math

import jax
import jax.numpy as jnp
import ml_dtypes
import numpy as np
from jax import lax
from jax.experimental import pallas as pl
from jax.experimental.pallas import tpu as pltpu
from jax.sharding import PartitionSpec as P

ELONG = 0.75
LANES = 128
VMEM_LIMIT = 32 * 1024 * 1024
F32 = jnp.float32
BF16 = jnp.bfloat16


CHUNK = 256


def halves(pupil, field, fun):
    freq = np.arange(field // 2) + 0.5
    place = (pupil - 1) / 2.0 - np.arange(pupil // 2)
    return fun(2.0 * np.pi / field * np.outer(freq, place))


def hi_lo(matrix):
    hi = matrix.astype(np.float32).astype(ml_dtypes.bfloat16)
    lo = (matrix - hi.astype(np.float64)).astype(np.float32).astype(ml_dtypes.bfloat16)
    return np.concatenate([hi, lo], axis=1)


def tables(pupil, field):
    fun = (np.cos, np.sin)
    fwd, bwd = [], []
    for b in range(2):
        for a in range(2):
            t = np.kron(halves(pupil, field, fun[a]), halves(pupil, field, fun[b]))
            fwd.append(hi_lo(t))
            rows = min(CHUNK, t.shape[0])
            bwd.append(
                np.stack([hi_lo(t[m : m + rows].T) for m in range(0, t.shape[0], rows)])
            )
    return np.stack(fwd), np.stack(bwd)


def split(x):
    hi = x.astype(BF16)
    return hi, (x - hi.astype(F32)).astype(BF16)


def dot_three(table, depth, hi, lo):
    wide = jnp.concatenate([table, table[:, :depth]], axis=1)
    return jnp.dot(wide, jnp.concatenate([hi, hi, lo], axis=0), preferred_element_type=F32)


def lane_group(shape, width):
    return lax.broadcasted_iota(jnp.int32, shape, len(shape) - 1) // width


def roll(x, shift):
    return pltpu.roll(x, shift % LANES, x.ndim - 1)


def swap_groups(blocks, width):
    n = len(blocks)
    blocks = list(blocks)
    group = lane_group(blocks[0].shape, width)
    step = 1
    while step < n:
        low = (group & step) == 0
        for i in range(n):
            if i & step:
                continue
            j = i + step
            a, b = blocks[i], blocks[j]
            blocks[i] = jnp.where(low, a, roll(b, step * width))
            blocks[j] = jnp.where(low, roll(a, -step * width), b)
        step *= 2
    return blocks


def spread_groups(x, n, width):
    group = lane_group(x.shape, width)
    out = [x]
    step = n // 2
    while step >= 1:
        low = (group & step) == 0
        made = []
        for y in out:
            up, down = roll(y, step * width), roll(y, -step * width)
            made.append(jnp.where(low, y, up))
            made.append(jnp.where(low, down, y))
        out = made
        step //= 2
    return out


def reverse_rows(x):
    row = lax.broadcasted_iota(jnp.int32, (8, LANES), 0)
    parts = []
    for i in range(x.shape[0] - 8, -1, -8):
        y = pltpu.roll(x[i : i + 8], 4, 0)
        y = jnp.where((row & 2) == 0, pltpu.roll(y, 6, 0), pltpu.roll(y, 2, 0))
        y = jnp.where((row & 1) == 0, pltpu.roll(y, 7, 0), pltpu.roll(y, 1, 0))
        parts.append(y)
    return jnp.concatenate(parts, axis=0)


def pack_early_kernel(n, nb, me_ref, profile_hbm, weight_hbm, amp_hbm, phase_hbm, *refs):
    out_refs = refs[:n]
    profile_ref, weight_ref, amp_ref, phase_ref, sems = refs[n:]
    pairs = (
        (phase_hbm, phase_ref),
        (amp_hbm, amp_ref),
        (profile_hbm, profile_ref),
        (weight_hbm, weight_ref),
    )
    copies = [pltpu.make_async_copy(src, dst, sems.at[i]) for i, (src, dst) in enumerate(pairs)]
    for copy in copies:
        copy.start()
    width = LANES // n
    qp = phase_ref.shape[0] // n
    turn = lax.rem(n - me_ref[0], n) * width
    for copy in copies:
        copy.wait()
    for q in range(0, qp, 16):
        parts = [pltpu.roll(phase_ref[a * qp + q : a * qp + q + 16, :], turn, 1) for a in range(n)]
        for j, block in enumerate(swap_groups(parts, width)):
            hi, lo = split(block)
            out_refs[j][q : q + 16, :] = hi
            out_refs[j][qp + q : qp + q + 16, :] = lo
    for q in range(0, qp, 16):
        parts = [
            pltpu.roll(amp_ref[a * qp + q : a * qp + q + 16, :].astype(F32), turn, 1)
            for a in range(n)
        ]
        for j, block in enumerate(swap_groups(parts, width)):
            out_refs[j][2 * qp + q : 2 * qp + q + 16, :] = block.astype(BF16)

    base = 3 * qp
    rows = out_refs[0].shape[0] - base
    row = lax.broadcasted_iota(jnp.int32, (rows, LANES), 0)
    extra = jnp.zeros((rows, LANES), F32)
    for j in range(nb):
        for k, ref in enumerate((profile_ref, weight_ref)):
            value = jnp.full((rows, LANES), ref[j], F32)
            for part in range(3):
                piece = value.astype(BF16).astype(F32)
                extra = jnp.where(row == (2 * j + k) * 3 + part, piece, extra)
                value = value - piece
    for j in range(n):
        out_refs[j][base:, :] = extra.astype(BF16)


def pack_late_kernel(n, me_ref, cot_hbm, *refs):
    out_refs = refs[n - 1 : 2 * n - 1]
    cot_ref, sem = refs[2 * n - 1 :]
    copy = pltpu.make_async_copy(cot_hbm, cot_ref, sem)
    copy.start()
    width = LANES // n
    qc = cot_ref.shape[0] // n
    turn = lax.rem(n - me_ref[0], n) * width
    copy.wait()

    def step(i, carry):
        at = pl.multiple_of(i * 16, 16)
        parts = [
            pltpu.roll(cot_ref[pl.ds(a * qc + at, 16), :].astype(F32), turn, 1) for a in range(n)
        ]
        for j, block in enumerate(swap_groups(parts, width)):
            out_refs[j][pl.ds(at, 16), :] = block.astype(BF16)
        return carry

    lax.fori_loop(0, qc // 16, step, 0, unroll=4)

def sincos(x):
    turns = jnp.round(x * (2.0 / math.pi))
    r = x - turns * 1.5703125
    r = r - turns * 4.838267948966e-4
    r2 = r * r
    s = r + r * r2 * (-1.6666654611e-1 + r2 * (8.3321608736e-3 + r2 * -1.9515295891e-4))
    c = (1.0 - 0.5 * r2) + r2 * r2 * (
        4.166664568298827e-2 + r2 * (-1.388731625493765e-3 + r2 * 2.443315711809948e-5)
    )
    quad = turns.astype(jnp.int32)
    odd = (quad & 1) != 0
    sin_v = jnp.where(odd, c, s)
    cos_v = jnp.where(odd, s, c)
    sin_v = jnp.where((quad & 2) != 0, -sin_v, sin_v)
    cos_v = jnp.where(((quad + 1) & 2) != 0, -cos_v, cos_v)
    return sin_v, cos_v


def fields_kernel(n, nb, pupil, field, me_ref, pos_hbm, fwd_hbm, *refs):
    in_refs, (e_s, p_s, aux_ref) = refs[:n], refs[n : n + 3]
    phase_s, amp_s, x_s, pos_ref, fwd_ref, sems = refs[n + 3 :]
    copies = [
        pltpu.make_async_copy(pos_hbm, pos_ref, sems.at[0]),
        pltpu.make_async_copy(fwd_hbm, fwd_ref, sems.at[1]),
    ]
    for copy in copies:
        copy.start()
    width = LANES // n
    nbins = n * nb
    qp = pupil * pupil // (n * n)
    half = pupil // 2
    wide = nb * LANES
    me = me_ref[0]
    group1 = lane_group((1, LANES), width)
    owner = [lax.rem(me + n - j, n) for j in range(n)]

    for j in range(n):
        for q in range(0, qp, 16):
            hi = in_refs[j][q : q + 16, :].astype(F32)
            lo = in_refs[j][qp + q : qp + q + 16, :].astype(F32)
            am = in_refs[j][2 * qp + q : 2 * qp + q + 16, :].astype(F32)
            turned = [(a * qp + q) % pupil >= half for a in range(n)]
            for src, dst in ((hi + lo, phase_s), (am, amp_s)):
                ways = {
                    way: spread_groups(reverse_rows(src) if way else src, n, width)
                    for way in set(turned)
                }
                for a in range(n):
                    line = (a * qp + q) // pupil * pupil + (half if turned[a] else 0)
                    part = (a * qp + q) % half
                    part = half - 16 - part if turned[a] else part
                    at = pl.multiple_of(owner[j] * (n * qp) + line + part, 16)
                    dst[pl.ds(at, 16), :] = ways[turned[a]][a]

    prof, wgt = [], []
    for t in range(nb):
        p_row, w_row = jnp.zeros((1, LANES), F32), jnp.zeros((1, LANES), F32)
        for j in range(n):
            extra = in_refs[j][3 * qp :, :].astype(F32)
            rows = [extra[6 * t + i : 6 * t + i + 1, :] for i in range(6)]
            p_row = jnp.where(group1 == owner[j], rows[0] + rows[1] + rows[2], p_row)
            w_row = jnp.where(group1 == owner[j], rows[3] + rows[4] + rows[5], w_row)
        prof.append(p_row)
        wgt.append(w_row)
    total = sum(prof)
    step = n // 2
    while step >= 1:
        total = total + roll(total, step * width)
        step //= 2
    aux = jnp.zeros(aux_ref.shape, F32)
    row = lax.broadcasted_iota(jnp.int32, aux_ref.shape, 0)
    for t in range(nb):
        aux = jnp.where(row == t, 2.0 / (pupil * pupil) * prof[t] * wgt[t] / total, aux)
        aux = jnp.where(row == nb + t, prof[t], aux)
        aux = jnp.where(row == 2 * nb + t, wgt[t], aux)
    aux_ref[...] = jnp.where(row == 3 * nb, total, aux)

    copies[0].wait()
    pos = pos_ref[...]
    near = jnp.zeros_like(pos)
    for d, one in enumerate(spread_groups(pos, n, width)):
        near = jnp.where(me == d, one, near)
    shift = math.pi / field
    tilt_x, tilt_y = [], []
    for t in range(nb):
        kappa = ELONG * (2.0 * (group1 * nb + t).astype(F32) / (nbins - 1) - 1.0)
        tilt_x.append(kappa * near[0:1, :] + shift)
        tilt_y.append(kappa * near[1:2, :] + shift)

    row = lax.broadcasted_iota(jnp.int32, (pupil, LANES), 0)
    u_rows = jnp.where(row < half, row, pupil + half - 1 - row).astype(F32) - (pupil - 1) / 2.0
    lean = [u_rows * tilt_x[t] for t in range(nb)]

    def fields(i, carry):
        at16 = pl.multiple_of(i * half, half)
        for t in range(nb):
            found = []
            for r in (i, pupil - 1 - i):
                at = pl.multiple_of(r * pupil, pupil)
                v = r.astype(F32) - (pupil - 1) / 2.0
                am = amp_s[pl.ds(at, pupil), :]
                sin_v, cos_v = sincos(phase_s[pl.ds(at, pupil), :] + (lean[t] + v * tilt_y[t]))
                one = (am * cos_v, am * sin_v)
                for k in range(2):
                    e_s[t, k, pl.ds(at, pupil), :] = one[k]
                found.append(one)
            for k in range(2):
                even, odd = found[1][k] + found[0][k], found[1][k] - found[0][k]
                classes = (
                    even[half:] + even[:half],
                    odd[half:] + odd[:half],
                    even[half:] - even[:half],
                    odd[half:] - odd[:half],
                )
                lanes = pl.ds(k * wide + t * LANES, LANES)
                for c, x in enumerate(classes):
                    hi, lo = split(x)
                    x_s[c, 0, pl.ds(at16, half), lanes] = hi
                    x_s[c, 1, pl.ds(at16, half), lanes] = lo
        return carry

    lax.fori_loop(0, half, fields, 0)

    depth = half * half
    copies[1].wait()
    for c in range(4):
        for k in range(2):
            lanes = pl.ds(k * wide, wide)
            p_s[c, k] = dot_three(fwd_ref[c], depth, x_s[c, 0, :, lanes], x_s[c, 1, :, lanes])


def images_kernel(n, nb, pupil, field, me_ref, bwd_hbm, e_s, p_s, aux_in, *refs):
    in_refs, grad_refs, stat_ref = refs[:n], refs[n : 2 * n], refs[2 * n]
    cot_s, y_s, g_s, pg_s, bwd_ref, sem = refs[2 * n + 1 :]
    copy = pltpu.make_async_copy(bwd_hbm, bwd_ref, sem)
    copy.start()
    width = LANES // n
    qp = pupil * pupil // (n * n)
    qc = field * field // (n * n)
    half, fhalf = pupil // 2, field // 2
    wide = nb * LANES
    me = me_ref[0]
    owner = [lax.rem(me + n - j, n) for j in range(n)]
    coef = [aux_in[t : t + 1, :] for t in range(nb)]

    per = qc // field
    for j in range(n):
        low = owner[j] < n // 2
        sign = jnp.where(low, 0, 1)

        def place(i, carry):
            for q in range(0, field, 16):
                at = pl.multiple_of(i * field + q, 16)
                raw = in_refs[j][pl.ds(at, 16), :].astype(F32)
                raw = reverse_rows(raw) if q >= fhalf else raw
                col = field - 16 - q if q >= fhalf else q
                for a, cot in enumerate(spread_groups(raw, n, width)):
                    k1 = (owner[j] * n + a) * per + i
                    line = jnp.where(low, k1, field - 1 - k1)
                    at = pl.multiple_of(line * fhalf + col, 16)
                    cot_s[sign, int(q >= fhalf), pl.ds(at, 16), :] = cot
            return carry

        lax.fori_loop(0, per, place, 0)

    rows_all = fhalf * fhalf
    chunk = min(CHUNK, rows_all)
    copy.wait()

    def images(m, first):
        base = m * chunk

        def weigh(i, carry):
            at = pl.multiple_of(i * 16, 16)
            there = pl.multiple_of(base + i * 16, 16)
            cot = [cot_s[a, b, pl.ds(there, 16), :] for a in range(2) for b in range(2)]
            for t in range(nb):
                lanes = pl.ds(t * LANES, LANES)
                re = [p_s[c, 0, pl.ds(there, 16), lanes] for c in range(4)]
                im = [p_s[c, 1, pl.ds(there, 16), lanes] for c in range(4)]
                s0, s1, s2, s3 = re[0] + im[1], re[0] - im[1], im[2] - re[3], im[2] + re[3]
                y = [cot[0] * (s0 + s2), cot[1] * (s0 - s2), cot[2] * (s1 + s3), cot[3] * (s1 - s3)]
                s0, s1, s2, s3 = im[0] - re[1], im[0] + re[1], re[2] + im[3], re[2] - im[3]
                z = [cot[0] * (s0 - s2), cot[1] * (s0 + s2), cot[2] * (s1 - s3), cot[3] * (s1 + s3)]
                yp, ym, yd, ye = y[0] + y[1], y[2] + y[3], y[0] - y[1], y[2] - y[3]
                zp, zm, zd, ze = z[0] + z[1], z[2] + z[3], z[0] - z[1], z[2] - z[3]
                back = (
                    (yp + ym, zp + zm),
                    (zm - zp, yp - ym),
                    (-ze - zd, yd + ye),
                    (ye - yd, ze - zd),
                )
                for c in range(4):
                    for k in range(2):
                        hi, lo = split(back[c][k])
                        lanes = pl.ds(k * wide + t * LANES, LANES)
                        y_s[c, 0, pl.ds(at, 16), lanes] = hi
                        y_s[c, 1, pl.ds(at, 16), lanes] = lo
            return carry

        lax.fori_loop(0, chunk // 16, weigh, 0, unroll=2)
        for c in range(4):
            table = bwd_ref[c, m]
            for k in range(2):
                lanes = pl.ds(k * wide, wide)
                out = dot_three(table, chunk, y_s[c, 0, :, lanes], y_s[c, 1, :, lanes])
                g_s[c, k] = out if first else g_s[c, k] + out

    images(0, True)
    if rows_all > chunk:
        lax.fori_loop(1, rows_all // chunk, lambda m, carry: images(m, False) or carry, 0)

    def products(i, stats):
        stats = list(stats)
        at16 = pl.multiple_of(i * half, half)
        grads = [jnp.zeros((pupil, LANES), F32) for _ in range(2)]
        spots = [pl.multiple_of(r * pupil, pupil) for r in (i, pupil - 1 - i)]
        for t in range(nb):
            found = []
            for k in range(2):
                g = [g_s[c, k, pl.ds(at16, half), pl.ds(t * LANES, LANES)] for c in range(4)]
                even = jnp.concatenate([g[0] - g[2], g[0] + g[2]], axis=0)
                odd = jnp.concatenate([g[1] - g[3], g[1] + g[3]], axis=0)
                found.append((even - odd, even + odd))
            for which in range(2):
                e_re = e_s[t, 0, pl.ds(spots[which], pupil), :]
                e_im = e_s[t, 1, pl.ds(spots[which], pupil), :]
                g_re, g_im = found[0][which], found[1][which]
                stats[t] = stats[t] + (e_re * g_re + e_im * g_im)
                grads[which] = grads[which] + coef[t] * (e_re * g_im - e_im * g_re)
        for which in range(2):
            grad = grads[which]
            step = n // 2
            while step >= 1:
                grad = grad + roll(grad, step * width)
                step //= 2
            grad = jnp.concatenate([grad[:half], reverse_rows(grad[half:])], axis=0)
            pg_s[pl.ds(spots[which], pupil), :] = grad
        return tuple(stats)

    stats = lax.fori_loop(0, half, products, tuple(jnp.zeros((pupil, LANES), F32) for _ in range(nb)))

    lane = lax.broadcasted_iota(jnp.int32, (1, LANES), 1)
    sums = jnp.zeros((1, LANES), F32)
    for t in range(nb):
        stat = jnp.sum(stats[t], axis=0, keepdims=True) * (1.0 / (pupil * pupil))
        step = 1
        while step < width:
            stat = stat + roll(stat, step)
            step *= 2
        sums = jnp.where(lane % width == width - 1 - t, roll(stat, -t), sums)
    stat_ref[...] = jnp.broadcast_to(sums, stat_ref.shape)
    group = lane_group((8, LANES), width)
    for k, ref in enumerate(grad_refs):
        d = lax.rem(me + k, n)
        for q in range(0, qp, 8):
            out = jnp.zeros((8, LANES), F32)
            for a in range(n):
                at = pl.multiple_of((d * n + a) * qp + q, 8)
                out = jnp.where(group == a, pg_s[pl.ds(at, 8), :], out)
            ref[q : q + 8, :] = out


def final_kernel(n, nb, nsub_all, me_ref, aux_ref, stat_ref, *refs):
    width = LANES // n
    out_ref, prof_ref = refs[n:]
    qp = out_ref.shape[0] // n
    turn = me_ref[0] * width
    for q in range(0, qp, 8):
        parts = [refs[(n - i) % n][q : q + 8, :] for i in range(n)]
        for a, block in enumerate(swap_groups(parts, width)):
            out_ref[a * qp + q : a * qp + q + 8, :] = pltpu.roll(block, turn, 1)
    lane = lax.broadcasted_iota(jnp.int32, (1, LANES), 1)
    stat = jnp.sum(stat_ref[...], axis=0, keepdims=True)
    aux = aux_ref[...]
    total = jnp.max(aux[3 * nb : 3 * nb + 1, :])
    centre = jnp.zeros((1, LANES), F32)
    own = []
    for t in range(nb):
        prof, wgt = aux[nb + t : nb + t + 1], aux[2 * nb + t : 2 * nb + t + 1]
        term = stat * wgt
        centre += jnp.where(lane % width == width - 1 - t, term * prof, 0.0)
        own.append(jnp.sum(jnp.where(lane == (me_ref[0] + 1) * width - 1 - t, term, 0.0)))
    centre = jnp.sum(centre)
    for t in range(nb):
        prof_ref[t] = (own[t] / total - centre / (total * total)) / nsub_all


def local(cotangent, amplitude, phase, position, profile, alt_weight):
    n = lax.axis_size("alt")
    n_sub = lax.axis_size("sub")
    nsub_all = n_sub * phase.shape[1]
    nb = profile.shape[0]
    pupil = math.isqrt(n * phase.shape[0])
    field = math.isqrt(n * cotangent.shape[0])
    qp = phase.shape[0] // n
    qc = cotangent.shape[0] // n
    extra = -(-6 * nb // 16) * 16
    me = lax.axis_index("alt").astype(jnp.int32).reshape(1)
    smem = pl.BlockSpec(memory_space=pltpu.SMEM)
    vmem = pl.BlockSpec(memory_space=pltpu.VMEM)
    hbm = pl.BlockSpec(memory_space=pltpu.HBM)
    params = pltpu.CompilerParams(vmem_limit_bytes=VMEM_LIMIT)

    def keep(*arrays):
        return [pltpu.with_memory_space_constraint(x, pltpu.HBM) for x in arrays]

    def exchange(blocks):
        return [blocks[0]] + [
            lax.ppermute(blocks[j], "alt", [(i, (i + j) % n) for i in range(n)])
            for j in range(1, n)
        ]

    early = pl.pallas_call(
        functools.partial(pack_early_kernel, n, nb),
        out_shape=[jax.ShapeDtypeStruct((3 * qp + extra, LANES), BF16)] * n,
        in_specs=[smem] + [hbm] * 4,
        out_specs=[vmem] * n,
        scratch_shapes=[
            pltpu.SMEM(profile.shape, F32),
            pltpu.SMEM(alt_weight.shape, F32),
            pltpu.VMEM(amplitude.shape, BF16),
            pltpu.VMEM(phase.shape, F32),
            pltpu.SemaphoreType.DMA((4,)),
        ],
        compiler_params=params,
        name="pack_early",
    )(me, *keep(profile, alt_weight, amplitude, phase))
    early = exchange(early)
    late = pl.pallas_call(
        functools.partial(pack_late_kernel, n),
        out_shape=[jax.ShapeDtypeStruct((qc, LANES), BF16)] * n,
        in_specs=[smem, hbm] + [vmem] * (n - 1),
        out_specs=[vmem] * n,
        scratch_shapes=[pltpu.VMEM(cotangent.shape, BF16), pltpu.SemaphoreType.DMA],
        compiler_params=params,
        name="pack_late",
    )(me, *keep(cotangent), *early[1:])
    late = exchange(late)

    fwd, bwd = (jnp.asarray(x) for x in tables(pupil, field))
    depth = pupil * pupil // 4
    rows_all = field * field // 4
    chunk = min(CHUNK, rows_all)
    wide = nb * LANES
    aux_rows = -(-(3 * nb + 1) // 8) * 8
    e, p, aux = pl.pallas_call(
        functools.partial(fields_kernel, n, nb, pupil, field),
        out_shape=(
            jax.ShapeDtypeStruct((nb, 2, pupil * pupil, LANES), F32),
            jax.ShapeDtypeStruct((4, 2, rows_all, wide), F32),
            jax.ShapeDtypeStruct((aux_rows, LANES), F32),
        ),
        in_specs=[smem] + [hbm] * 2 + [vmem] * n,
        out_specs=(vmem, vmem, vmem),
        scratch_shapes=[
            pltpu.VMEM((pupil * pupil, LANES), F32),
            pltpu.VMEM((pupil * pupil, LANES), F32),
            pltpu.VMEM((4, 2, depth, 2 * wide), BF16),
            pltpu.VMEM(position.shape, F32),
            pltpu.VMEM(fwd.shape, BF16),
            pltpu.SemaphoreType.DMA((2,)),
        ],
        compiler_params=params,
        name="fields",
    )(me, *keep(position, fwd), *early)
    *grads, stat = pl.pallas_call(
        functools.partial(images_kernel, n, nb, pupil, field),
        out_shape=[jax.ShapeDtypeStruct((qp, LANES), F32)] * n
        + [jax.ShapeDtypeStruct((n_sub * n, LANES), F32)],
        in_specs=[smem, hbm] + [vmem] * (3 + n),
        out_specs=[vmem] * (n + 1),
        scratch_shapes=[
            pltpu.VMEM((2, 2, rows_all, LANES), F32),
            pltpu.VMEM((4, 2, chunk, 2 * wide), BF16),
            pltpu.VMEM((4, 2, depth, wide), F32),
            pltpu.VMEM((pupil * pupil, LANES), F32),
            pltpu.VMEM(bwd.shape, BF16),
            pltpu.SemaphoreType.DMA,
        ],
        compiler_params=params,
        name="images",
    )(me, *keep(bwd), e, p, aux, *late)
    stat = lax.all_to_all(stat, ("sub", "alt"), 0, 0, tiled=True)
    grads = exchange(grads)
    return pl.pallas_call(
        functools.partial(final_kernel, n, nb, nsub_all),
        out_shape=(
            jax.ShapeDtypeStruct(phase.shape, F32),
            jax.ShapeDtypeStruct(profile.shape, F32),
        ),
        in_specs=[smem, vmem, vmem] + [vmem] * n,
        out_specs=(vmem, smem),
        compiler_params=params,
        name="finish",
    )(me, aux, stat, *grads)


def solution(mesh):
    placed = (P("alt", "sub"), P("alt", "sub"), P("alt", "sub"), P(None, "sub"), P("alt"), P("alt"))
    return jax.shard_map(
        local, mesh=mesh, in_specs=placed, out_specs=(P("alt", "sub"), P("alt")), check_vma=False
    )
```

```python
import functools
import math

import jax
import jax.numpy as jnp
import ml_dtypes
import numpy as np
from jax import lax
from jax.experimental import pallas as pl
from jax.experimental.pallas import tpu as pltpu
from jax.sharding import PartitionSpec as P

ELONG = 0.75
LANES = 128
VMEM_LIMIT = 52 * 1024 * 1024
F32 = jnp.float32
BF16 = jnp.bfloat16


CHUNK = 512


def halves(pupil, field, fun):
    freq = np.arange(field // 2) + 0.5
    place = (pupil - 1) / 2.0 - np.arange(pupil // 2)
    return fun(2.0 * np.pi / field * np.outer(freq, place))


def hi_lo(matrix):
    hi = matrix.astype(np.float32).astype(ml_dtypes.bfloat16)
    lo = (matrix - hi.astype(np.float64)).astype(np.float32).astype(ml_dtypes.bfloat16)
    return np.concatenate([hi, lo], axis=1)


def tables(pupil, field):
    fun = (np.cos, np.sin)
    fwd, bwd = [], []
    for b in range(2):
        for a in range(2):
            t = np.kron(halves(pupil, field, fun[a]), halves(pupil, field, fun[b]))
            fwd.append(hi_lo(t))
            bwd.append(hi_lo(t.T))
    return np.stack(fwd), np.stack(bwd)


def split(x):
    hi = x.astype(BF16)
    return hi, (x - hi.astype(F32)).astype(BF16)


def dot_three(table, depth, hi, lo):
    wide = jnp.concatenate([table, table[:, :depth]], axis=1)
    return jnp.dot(wide, jnp.concatenate([hi, hi, lo], axis=0), preferred_element_type=F32)


def lane_group(shape, width):
    return lax.broadcasted_iota(jnp.int32, shape, len(shape) - 1) // width


def roll(x, shift):
    return pltpu.roll(x, shift % LANES, x.ndim - 1)


def swap_groups(blocks, width):
    n = len(blocks)
    blocks = list(blocks)
    group = lane_group(blocks[0].shape, width)
    step = 1
    while step < n:
        low = (group & step) == 0
        for i in range(n):
            if i & step:
                continue
            j = i + step
            a, b = blocks[i], blocks[j]
            blocks[i] = jnp.where(low, a, roll(b, step * width))
            blocks[j] = jnp.where(low, roll(a, -step * width), b)
        step *= 2
    return blocks


def spread_groups(x, n, width):
    group = lane_group(x.shape, width)
    out = [x]
    step = n // 2
    while step >= 1:
        low = (group & step) == 0
        made = []
        for y in out:
            up, down = roll(y, step * width), roll(y, -step * width)
            made.append(jnp.where(low, y, up))
            made.append(jnp.where(low, down, y))
        out = made
        step //= 2
    return out


def reverse_rows(x):
    row = lax.broadcasted_iota(jnp.int32, (8, LANES), 0)
    parts = []
    for i in range(x.shape[0] - 8, -1, -8):
        y = pltpu.roll(x[i : i + 8], 4, 0)
        y = jnp.where((row & 2) == 0, pltpu.roll(y, 6, 0), pltpu.roll(y, 2, 0))
        y = jnp.where((row & 1) == 0, pltpu.roll(y, 7, 0), pltpu.roll(y, 1, 0))
        parts.append(y)
    return jnp.concatenate(parts, axis=0)


def pack_kernel(n, nb, me_ref, profile_hbm, weight_hbm, amp_hbm, phase_hbm, cot_hbm, *refs):
    out_refs = refs[:n]
    profile_ref, weight_ref, amp_ref, phase_ref, cot_ref, sems = refs[n:]
    pairs = (
        (phase_hbm, phase_ref),
        (amp_hbm, amp_ref),
        (profile_hbm, profile_ref),
        (weight_hbm, weight_ref),
        (cot_hbm, cot_ref),
    )
    copies = [pltpu.make_async_copy(src, dst, sems.at[i]) for i, (src, dst) in enumerate(pairs)]
    for copy in copies:
        copy.start()
    width = LANES // n
    qp = phase_ref.shape[0] // n
    qc = cot_ref.shape[0] // n
    turn = lax.rem(n - me_ref[0], n) * width
    for copy in copies:
        copy.wait()
    for q in range(0, qp, 16):
        parts = [pltpu.roll(phase_ref[a * qp + q : a * qp + q + 16, :], turn, 1) for a in range(n)]
        for j, block in enumerate(swap_groups(parts, width)):
            hi, lo = split(block)
            out_refs[j][q : q + 16, :] = hi
            out_refs[j][qp + q : qp + q + 16, :] = lo
    for q in range(0, qp, 16):
        parts = [
            pltpu.roll(amp_ref[a * qp + q : a * qp + q + 16, :].astype(F32), turn, 1)
            for a in range(n)
        ]
        for j, block in enumerate(swap_groups(parts, width)):
            out_refs[j][2 * qp + q : 2 * qp + q + 16, :] = block.astype(BF16)

    def step(i, carry):
        at = pl.multiple_of(i * 16, 16)
        parts = [
            pltpu.roll(cot_ref[pl.ds(a * qc + at, 16), :].astype(F32), turn, 1) for a in range(n)
        ]
        for j, block in enumerate(swap_groups(parts, width)):
            out_refs[j][pl.ds(3 * qp + at, 16), :] = block.astype(BF16)
        return carry

    lax.fori_loop(0, qc // 16, step, 0, unroll=4)
    base = 3 * qp + qc
    rows = out_refs[0].shape[0] - base
    row = lax.broadcasted_iota(jnp.int32, (rows, LANES), 0)
    extra = jnp.zeros((rows, LANES), F32)
    for j in range(nb):
        for k, ref in enumerate((profile_ref, weight_ref)):
            value = jnp.full((rows, LANES), ref[j], F32)
            for part in range(3):
                piece = value.astype(BF16).astype(F32)
                extra = jnp.where(row == (2 * j + k) * 3 + part, piece, extra)
                value = value - piece
    for j in range(n):
        out_refs[j][base:, :] = extra.astype(BF16)


def sincos(x):
    turns = jnp.round(x * (2.0 / math.pi))
    r = x - turns * 1.5703125
    r = r - turns * 4.838267948966e-4
    r2 = r * r
    s = r + r * r2 * (-1.6666654611e-1 + r2 * (8.3321608736e-3 + r2 * -1.9515295891e-4))
    c = (1.0 - 0.5 * r2) + r2 * r2 * (
        4.166664568298827e-2 + r2 * (-1.388731625493765e-3 + r2 * 2.443315711809948e-5)
    )
    quad = turns.astype(jnp.int32)
    odd = (quad & 1) != 0
    sin_v = jnp.where(odd, c, s)
    cos_v = jnp.where(odd, s, c)
    sin_v = jnp.where((quad & 2) != 0, -sin_v, sin_v)
    cos_v = jnp.where(((quad + 1) & 2) != 0, -cos_v, cos_v)
    return sin_v, cos_v


def multiple(x, m):
    return x if isinstance(x, int) else pl.multiple_of(x, m)


def interleave(dots, pieces):
    for i, one in enumerate(dots):
        one()
        for piece in pieces[i * len(pieces) // len(dots) : (i + 1) * len(pieces) // len(dots)]:
            piece()


def spots_kernel(n, nb, pupil, field, me_ref, pos_hbm, fwd_hbm, bwd_hbm, *refs):
    in_refs, grad_refs, aux_ref, stat_ref = refs[:n], refs[n : 2 * n], refs[2 * n], refs[2 * n + 1]
    phase_s, amp_s, cot_s, pg_s, part_s, pos_ref, fwd_ref, bwd_ref, sems, *per_tile = refs[2 * n + 2 :]
    e_s, x_s, p_s, y_s, g_s = (per_tile[k * nb : (k + 1) * nb] for k in range(5))
    copies = [
        pltpu.make_async_copy(pos_hbm, pos_ref, sems.at[0]),
        pltpu.make_async_copy(fwd_hbm, fwd_ref, sems.at[1]),
        pltpu.make_async_copy(bwd_hbm, bwd_ref, sems.at[2]),
    ]
    for copy in copies:
        copy.start()
    width = LANES // n
    nbins = n * nb
    qp = pupil * pupil // (n * n)
    qc = field * field // (n * n)
    half, fhalf = pupil // 2, field // 2
    me = me_ref[0]
    group1 = lane_group((1, LANES), width)
    owner = [lax.rem(me + n - j, n) for j in range(n)]

    for j in range(n):
        for q in range(0, qp, 16):
            hi = in_refs[j][q : q + 16, :].astype(F32)
            lo = in_refs[j][qp + q : qp + q + 16, :].astype(F32)
            am = in_refs[j][2 * qp + q : 2 * qp + q + 16, :].astype(F32)
            turned = [(a * qp + q) % pupil >= half for a in range(n)]
            for src, dst in ((hi + lo, phase_s), (am, amp_s)):
                ways = {
                    way: spread_groups(reverse_rows(src) if way else src, n, width)
                    for way in set(turned)
                }
                for a in range(n):
                    line = (a * qp + q) // pupil * pupil + (half if turned[a] else 0)
                    part = (a * qp + q) % half
                    part = half - 16 - part if turned[a] else part
                    at = pl.multiple_of(owner[j] * (n * qp) + line + part, 16)
                    dst[pl.ds(at, 16), :] = ways[turned[a]][a]

    per = qc // field
    low = [owner[j] < n // 2 for j in range(n)]
    sign = [jnp.where(low[j], 0, 1) for j in range(n)]

    def place(j, i, q):
        at = 3 * qp + i * field + q
        raw = in_refs[j][at : at + 16, :].astype(F32)
        raw = reverse_rows(raw) if q >= fhalf else raw
        col = field - 16 - q if q >= fhalf else q
        for a, cot in enumerate(spread_groups(raw, n, width)):
            k1 = (owner[j] * n + a) * per + i
            line = jnp.where(low[j], k1, field - 1 - k1)
            at = pl.multiple_of(line * fhalf + col, 16)
            cot_s[sign[j], int(q >= fhalf), pl.ds(at, 16), :] = cot

    prof, wgt = [], []
    for t in range(nb):
        p_row, w_row = jnp.zeros((1, LANES), F32), jnp.zeros((1, LANES), F32)
        for j in range(n):
            extra = in_refs[j][3 * qp + qc :, :].astype(F32)
            rows = [extra[6 * t + i : 6 * t + i + 1, :] for i in range(6)]
            p_row = jnp.where(group1 == owner[j], rows[0] + rows[1] + rows[2], p_row)
            w_row = jnp.where(group1 == owner[j], rows[3] + rows[4] + rows[5], w_row)
        prof.append(p_row)
        wgt.append(w_row)
    total = sum(prof)
    step = n // 2
    while step >= 1:
        total = total + roll(total, step * width)
        step //= 2
    coef = [2.0 / (pupil * pupil) * prof[t] * wgt[t] / total for t in range(nb)]
    aux = jnp.zeros(aux_ref.shape, F32)
    row = lax.broadcasted_iota(jnp.int32, aux_ref.shape, 0)
    for t in range(nb):
        aux = jnp.where(row == nb + t, prof[t], aux)
        aux = jnp.where(row == 2 * nb + t, wgt[t], aux)
    aux_ref[...] = jnp.where(row == 3 * nb, total, aux)

    copies[0].wait()
    pos = pos_ref[...]
    near = jnp.zeros_like(pos)
    for d, one in enumerate(spread_groups(pos, n, width)):
        near = jnp.where(me == d, one, near)
    shift = math.pi / field
    tilt_x, tilt_y = [], []
    for t in range(nb):
        kappa = ELONG * (2.0 * (group1 * nb + t).astype(F32) / (nbins - 1) - 1.0)
        tilt_x.append(kappa * near[0:1, :] + shift)
        tilt_y.append(kappa * near[1:2, :] + shift)

    row = lax.broadcasted_iota(jnp.int32, (pupil, LANES), 0)
    u_rows = jnp.where(row < half, row, pupil + half - 1 - row).astype(F32) - (pupil - 1) / 2.0
    lean = [u_rows * tilt_x[t] for t in range(nb)]

    def fields(t, i):
        at16 = multiple(i * half, half)
        found = []
        for r in (i, pupil - 1 - i):
            at = multiple(r * pupil, pupil)
            v = (float(r) if isinstance(r, int) else r.astype(F32)) - (pupil - 1) / 2.0
            am = amp_s[pl.ds(at, pupil), :]
            sin_v, cos_v = sincos(phase_s[pl.ds(at, pupil), :] + (lean[t] + v * tilt_y[t]))
            one = (am * cos_v, am * sin_v)
            for k in range(2):
                e_s[t][k, pl.ds(at, pupil), :] = one[k]
            found.append(one)
        for k in range(2):
            even, odd = found[1][k] + found[0][k], found[1][k] - found[0][k]
            classes = (
                even[half:] + even[:half],
                odd[half:] + odd[:half],
                even[half:] - even[:half],
                odd[half:] - odd[:half],
            )
            lanes = pl.ds(k * LANES, LANES)
            for c, x in enumerate(classes):
                hi, lo = split(x)
                x_s[t][c, 0, pl.ds(at16, half), lanes] = hi
                x_s[t][c, 1, pl.ds(at16, half), lanes] = lo

    depth = half * half
    rows_all = fhalf * fhalf
    chunk = min(CHUNK, rows_all)

    def forward(t, c, m):
        rows = pl.ds(m * chunk, chunk)
        p_s[t][c, rows, :] = dot_three(fwd_ref[c, rows, :], depth, x_s[t][c, 0], x_s[t][c, 1])

    def weigh(t, i):
        rows = pl.ds(i * 16, 16)
        cot = [cot_s[a, b, rows, :] for a in range(2) for b in range(2)]
        re = [p_s[t][c, rows, pl.ds(0, LANES)] for c in range(4)]
        im = [p_s[t][c, rows, pl.ds(LANES, LANES)] for c in range(4)]
        s0, s1, s2, s3 = re[0] + im[1], re[0] - im[1], im[2] - re[3], im[2] + re[3]
        y = [cot[0] * (s0 + s2), cot[1] * (s0 - s2), cot[2] * (s1 + s3), cot[3] * (s1 - s3)]
        s0, s1, s2, s3 = im[0] - re[1], im[0] + re[1], re[2] + im[3], re[2] - im[3]
        z = [cot[0] * (s0 - s2), cot[1] * (s0 + s2), cot[2] * (s1 - s3), cot[3] * (s1 + s3)]
        yp, ym, yd, ye = y[0] + y[1], y[2] + y[3], y[0] - y[1], y[2] - y[3]
        zp, zm, zd, ze = z[0] + z[1], z[2] + z[3], z[0] - z[1], z[2] - z[3]
        back = (
            (yp + ym, zp + zm),
            (zm - zp, yp - ym),
            (-ze - zd, yd + ye),
            (ye - yd, ze - zd),
        )
        for c in range(4):
            for k in range(2):
                hi, lo = split(back[c][k])
                lanes = pl.ds(k * LANES, LANES)
                y_s[t][c, 0, rows, lanes] = hi
                y_s[t][c, 1, rows, lanes] = lo

    def backward(t, c):
        g_s[t][c] = dot_three(bwd_ref[c], rows_all, y_s[t][c, 0], y_s[t][c, 1])

    def products(t, i, stat):
        at16 = multiple(i * half, half)
        found = []
        for k in range(2):
            g = [g_s[t][c, pl.ds(at16, half), pl.ds(k * LANES, LANES)] for c in range(4)]
            even = jnp.concatenate([g[0] - g[2], g[0] + g[2]], axis=0)
            odd = jnp.concatenate([g[1] - g[3], g[1] + g[3]], axis=0)
            found.append((even - odd, even + odd))
        for which, r in enumerate((i, pupil - 1 - i)):
            rows = pl.ds(multiple(r * pupil, pupil), pupil)
            e_re, e_im = e_s[t][0, rows, :], e_s[t][1, rows, :]
            g_re, g_im = found[0][which], found[1][which]
            stat = stat + (e_re * g_re + e_im * g_im)
            grad = coef[t] * (e_re * g_im - e_im * g_re)
            if t:
                grad = grad + part_s[rows, :]
            if t < nb - 1:
                part_s[rows, :] = grad
                continue
            step = n // 2
            while step >= 1:
                grad = grad + roll(grad, step * width)
                step //= 2
            pg_s[rows, :] = jnp.concatenate([grad[:half], reverse_rows(grad[half:])], axis=0)
        return stat

    stats = [jnp.zeros((pupil, LANES), F32) for _ in range(nb)]

    def early_products(t, i):
        stats[t] = products(t, i, stats[t])

    work = functools.partial
    places = [
        work(place, j, i, q) for j in range(n) for i in range(per) for q in range(0, field, 16)
    ]
    lax.fori_loop(0, half, lambda i, carry: fields(0, i) or carry, 0)
    copies[1].wait()
    for t in range(nb):
        pieces = places if t == 0 else []
        if t < nb - 1:
            pieces = [work(fields, t + 1, i) for i in range(half)] + pieces
        elif nb > 1:
            pieces = [work(weigh, 0, i) for i in range(rows_all // 16)] + pieces
        interleave(
            [work(forward, t, c, m) for c in range(4) for m in range(rows_all // chunk)], pieces
        )
    if nb == 1:
        for i in range(rows_all // 16):
            weigh(0, i)
    copies[2].wait()
    for t in range(nb):
        if t < nb - 1:
            pieces = [work(weigh, t + 1, i) for i in range(rows_all // 16)]
        else:
            pieces = [work(early_products, b, i) for b in range(nb - 1) for i in range(half)]
        interleave([work(backward, t, c) for c in range(4)], pieces)
    stats[-1] = lax.fori_loop(0, half, lambda i, stat: products(nb - 1, i, stat), stats[-1])

    lane = lax.broadcasted_iota(jnp.int32, (1, LANES), 1)
    sums = jnp.zeros((1, LANES), F32)
    for t in range(nb):
        stat = jnp.sum(stats[t], axis=0, keepdims=True) * (1.0 / (pupil * pupil))
        step = 1
        while step < width:
            stat = stat + roll(stat, step)
            step *= 2
        sums = jnp.where(lane % width == width - 1 - t, roll(stat, -t), sums)
    stat_ref[...] = jnp.broadcast_to(sums, stat_ref.shape)
    group = lane_group((8, LANES), width)
    for k, ref in enumerate(grad_refs):
        d = lax.rem(me + k, n)
        for q in range(0, qp, 8):
            out = jnp.zeros((8, LANES), F32)
            for a in range(n):
                at = pl.multiple_of((d * n + a) * qp + q, 8)
                out = jnp.where(group == a, pg_s[pl.ds(at, 8), :], out)
            ref[q : q + 8, :] = out


def final_kernel(n, nb, nsub_all, me_ref, aux_ref, stat_ref, *refs):
    width = LANES // n
    out_ref, prof_ref = refs[n:]
    qp = out_ref.shape[0] // n
    turn = me_ref[0] * width
    for q in range(0, qp, 8):
        parts = [refs[(n - i) % n][q : q + 8, :] for i in range(n)]
        for a, block in enumerate(swap_groups(parts, width)):
            out_ref[a * qp + q : a * qp + q + 8, :] = pltpu.roll(block, turn, 1)
    lane = lax.broadcasted_iota(jnp.int32, (1, LANES), 1)
    stat = jnp.sum(stat_ref[...], axis=0, keepdims=True)
    aux = aux_ref[...]
    total = jnp.max(aux[3 * nb : 3 * nb + 1, :])
    centre = jnp.zeros((1, LANES), F32)
    own = []
    for t in range(nb):
        prof, wgt = aux[nb + t : nb + t + 1], aux[2 * nb + t : 2 * nb + t + 1]
        term = stat * wgt
        centre += jnp.where(lane % width == width - 1 - t, term * prof, 0.0)
        own.append(jnp.sum(jnp.where(lane == (me_ref[0] + 1) * width - 1 - t, term, 0.0)))
    centre = jnp.sum(centre)
    for t in range(nb):
        prof_ref[t] = (own[t] / total - centre / (total * total)) / nsub_all


def local(cotangent, amplitude, phase, position, profile, alt_weight):
    n = lax.axis_size("alt")
    n_sub = lax.axis_size("sub")
    nsub_all = n_sub * phase.shape[1]
    nb = profile.shape[0]
    pupil = math.isqrt(n * phase.shape[0])
    field = math.isqrt(n * cotangent.shape[0])
    qp = phase.shape[0] // n
    qc = cotangent.shape[0] // n
    extra = -(-6 * nb // 16) * 16
    me = lax.axis_index("alt").astype(jnp.int32).reshape(1)
    smem = pl.BlockSpec(memory_space=pltpu.SMEM)
    vmem = pl.BlockSpec(memory_space=pltpu.VMEM)
    hbm = pl.BlockSpec(memory_space=pltpu.HBM)
    params = pltpu.CompilerParams(vmem_limit_bytes=VMEM_LIMIT)

    def keep(*arrays):
        return [pltpu.with_memory_space_constraint(x, pltpu.HBM) for x in arrays]

    def exchange(blocks):
        return [blocks[0]] + [
            lax.ppermute(blocks[j], "alt", [(i, (i + j) % n) for i in range(n)])
            for j in range(1, n)
        ]

    blocks = pl.pallas_call(
        functools.partial(pack_kernel, n, nb),
        out_shape=[jax.ShapeDtypeStruct((3 * qp + qc + extra, LANES), BF16)] * n,
        in_specs=[smem] + [hbm] * 5,
        out_specs=[vmem] * n,
        scratch_shapes=[
            pltpu.SMEM(profile.shape, F32),
            pltpu.SMEM(alt_weight.shape, F32),
            pltpu.VMEM(amplitude.shape, BF16),
            pltpu.VMEM(phase.shape, F32),
            pltpu.VMEM(cotangent.shape, BF16),
            pltpu.SemaphoreType.DMA((5,)),
        ],
        compiler_params=params,
        name="pack",
    )(me, *keep(profile, alt_weight, amplitude, phase, cotangent))
    blocks = exchange(blocks)

    fwd, bwd = (jnp.asarray(x) for x in tables(pupil, field))
    depth = pupil * pupil // 4
    rows_all = field * field // 4
    aux_rows = -(-(3 * nb + 1) // 8) * 8
    *grads, aux, stat = pl.pallas_call(
        functools.partial(spots_kernel, n, nb, pupil, field),
        out_shape=[jax.ShapeDtypeStruct((qp, LANES), F32)] * n
        + [jax.ShapeDtypeStruct((rows, LANES), F32) for rows in (aux_rows, n_sub * n)],
        in_specs=[smem] + [hbm] * 3 + [vmem] * n,
        out_specs=[vmem] * (n + 2),
        scratch_shapes=[
            pltpu.VMEM((pupil * pupil, LANES), F32),
            pltpu.VMEM((pupil * pupil, LANES), F32),
            pltpu.VMEM((2, 2, rows_all, LANES), F32),
            pltpu.VMEM((pupil * pupil, LANES), F32),
            pltpu.VMEM((pupil * pupil, LANES), F32),
            pltpu.VMEM(position.shape, F32),
            pltpu.VMEM(fwd.shape, BF16),
            pltpu.VMEM(bwd.shape, BF16),
            pltpu.SemaphoreType.DMA((3,)),
        ]
        + [pltpu.VMEM((2, pupil * pupil, LANES), F32)] * nb
        + [pltpu.VMEM((4, 2, depth, 2 * LANES), BF16)] * nb
        + [pltpu.VMEM((4, rows_all, 2 * LANES), F32)] * nb
        + [pltpu.VMEM((4, 2, rows_all, 2 * LANES), BF16)] * nb
        + [pltpu.VMEM((4, depth, 2 * LANES), F32)] * nb,
        compiler_params=params,
        name="spots",
    )(me, *keep(position, fwd, bwd), *blocks)
    stat = lax.all_to_all(stat, ("sub", "alt"), 0, 0, tiled=True)
    grads = exchange(grads)
    return pl.pallas_call(
        functools.partial(final_kernel, n, nb, nsub_all),
        out_shape=(
            jax.ShapeDtypeStruct(phase.shape, F32),
            jax.ShapeDtypeStruct(profile.shape, F32),
        ),
        in_specs=[smem, vmem, vmem] + [vmem] * n,
        out_specs=(vmem, smem),
        compiler_params=params,
        name="finish",
    )(me, aux, stat, *grads)


def solution(mesh):
    placed = (P("alt", "sub"), P("alt", "sub"), P("alt", "sub"), P(None, "sub"), P("alt"), P("alt"))
    return jax.shard_map(
        local, mesh=mesh, in_specs=placed, out_specs=(P("alt", "sub"), P("alt")), check_vma=False
    )
```

```python
import functools
import math

import jax
import jax.numpy as jnp
import ml_dtypes
import numpy as np
from jax import lax
from jax.experimental import pallas as pl
from jax.experimental.pallas import tpu as pltpu
from jax.sharding import PartitionSpec as P

ELONG = 0.75
LANES = 128
VMEM_LIMIT = 52 * 1024 * 1024
F32 = jnp.float32
BF16 = jnp.bfloat16


CHUNK = 512


def halves(pupil, field, fun):
    freq = np.arange(field // 2) + 0.5
    place = (pupil - 1) / 2.0 - np.arange(pupil // 2)
    return fun(2.0 * np.pi / field * np.outer(freq, place))


def hi_lo(matrix):
    hi = matrix.astype(np.float32).astype(ml_dtypes.bfloat16)
    lo = (matrix - hi.astype(np.float64)).astype(np.float32).astype(ml_dtypes.bfloat16)
    return np.concatenate([hi, lo], axis=1)


def tables(pupil, field):
    fun = (np.cos, np.sin)
    fwd, bwd = [], []
    for b in range(2):
        for a in range(2):
            t = np.kron(halves(pupil, field, fun[a]), halves(pupil, field, fun[b]))
            fwd.append(hi_lo(t))
            bwd.append(np.concatenate(np.split(hi_lo(t.T), 2, axis=1), axis=0))
    return np.stack(fwd), np.stack(bwd)


def split(x):
    hi = x.astype(BF16)
    return hi, (x - hi.astype(F32)).astype(BF16)


def dot_three(table, depth, hi, lo):
    wide = jnp.concatenate([table, table[:, :depth]], axis=1)
    return jnp.dot(wide, jnp.concatenate([hi, hi, lo], axis=0), preferred_element_type=F32)


def lane_group(shape, width):
    return lax.broadcasted_iota(jnp.int32, shape, len(shape) - 1) // width


def roll(x, shift):
    return pltpu.roll(x, shift % LANES, x.ndim - 1)


def swap_groups(blocks, width):
    n = len(blocks)
    blocks = list(blocks)
    group = lane_group(blocks[0].shape, width)
    step = 1
    while step < n:
        low = (group & step) == 0
        for i in range(n):
            if i & step:
                continue
            j = i + step
            a, b = blocks[i], blocks[j]
            blocks[i] = jnp.where(low, a, roll(b, step * width))
            blocks[j] = jnp.where(low, roll(a, -step * width), b)
        step *= 2
    return blocks


def spread_groups(x, n, width):
    group = lane_group(x.shape, width)
    out = [x]
    step = n // 2
    while step >= 1:
        low = (group & step) == 0
        made = []
        for y in out:
            up, down = roll(y, step * width), roll(y, -step * width)
            made.append(jnp.where(low, y, up))
            made.append(jnp.where(low, down, y))
        out = made
        step //= 2
    return out


def reverse_rows(x):
    row = lax.broadcasted_iota(jnp.int32, (8, LANES), 0)
    parts = []
    for i in range(x.shape[0] - 8, -1, -8):
        y = pltpu.roll(x[i : i + 8], 4, 0)
        y = jnp.where((row & 2) == 0, pltpu.roll(y, 6, 0), pltpu.roll(y, 2, 0))
        y = jnp.where((row & 1) == 0, pltpu.roll(y, 7, 0), pltpu.roll(y, 1, 0))
        parts.append(y)
    return jnp.concatenate(parts, axis=0)


def pack_kernel(n, nb, me_ref, profile_hbm, weight_hbm, amp_hbm, phase_hbm, cot_hbm, *refs):
    out_refs = refs[:n]
    profile_ref, weight_ref, amp_ref, phase_ref, cot_ref, sems = refs[n:]
    pairs = (
        (phase_hbm, phase_ref),
        (amp_hbm, amp_ref),
        (profile_hbm, profile_ref),
        (weight_hbm, weight_ref),
        (cot_hbm, cot_ref),
    )
    copies = [pltpu.make_async_copy(src, dst, sems.at[i]) for i, (src, dst) in enumerate(pairs)]
    for copy in copies:
        copy.start()
    width = LANES // n
    qp = phase_ref.shape[0] // n
    qc = cot_ref.shape[0] // n
    turn = lax.rem(n - me_ref[0], n) * width
    for copy in copies:
        copy.wait()
    for q in range(0, qp, 16):
        parts = [pltpu.roll(phase_ref[a * qp + q : a * qp + q + 16, :], turn, 1) for a in range(n)]
        for j, block in enumerate(swap_groups(parts, width)):
            hi, lo = split(block)
            out_refs[j][q : q + 16, :] = hi
            out_refs[j][qp + q : qp + q + 16, :] = lo
    for q in range(0, qp, 16):
        parts = [
            pltpu.roll(amp_ref[a * qp + q : a * qp + q + 16, :].astype(F32), turn, 1)
            for a in range(n)
        ]
        for j, block in enumerate(swap_groups(parts, width)):
            out_refs[j][2 * qp + q : 2 * qp + q + 16, :] = block.astype(BF16)

    def step(i, carry):
        at = pl.multiple_of(i * 16, 16)
        parts = [
            pltpu.roll(cot_ref[pl.ds(a * qc + at, 16), :].astype(F32), turn, 1) for a in range(n)
        ]
        for j, block in enumerate(swap_groups(parts, width)):
            out_refs[j][pl.ds(3 * qp + at, 16), :] = block.astype(BF16)
        return carry

    lax.fori_loop(0, qc // 16, step, 0, unroll=4)
    base = 3 * qp + qc
    rows = out_refs[0].shape[0] - base
    row = lax.broadcasted_iota(jnp.int32, (rows, LANES), 0)
    extra = jnp.zeros((rows, LANES), F32)
    for j in range(nb):
        for k, ref in enumerate((profile_ref, weight_ref)):
            value = jnp.full((rows, LANES), ref[j], F32)
            for part in range(3):
                piece = value.astype(BF16).astype(F32)
                extra = jnp.where(row == (2 * j + k) * 3 + part, piece, extra)
                value = value - piece
    for j in range(n):
        out_refs[j][base:, :] = extra.astype(BF16)


def sincos(x):
    turns = jnp.round(x * (2.0 / math.pi))
    r = x - turns * 1.5703125
    r = r - turns * 4.838267948966e-4
    r2 = r * r
    s = r + r * r2 * (-1.6666654611e-1 + r2 * (8.3321608736e-3 + r2 * -1.9515295891e-4))
    c = (1.0 - 0.5 * r2) + r2 * r2 * (
        4.166664568298827e-2 + r2 * (-1.388731625493765e-3 + r2 * 2.443315711809948e-5)
    )
    quad = turns.astype(jnp.int32)
    odd = (quad & 1) != 0
    sin_v = jnp.where(odd, c, s)
    cos_v = jnp.where(odd, s, c)
    sin_v = jnp.where((quad & 2) != 0, -sin_v, sin_v)
    cos_v = jnp.where(((quad + 1) & 2) != 0, -cos_v, cos_v)
    return sin_v, cos_v


def multiple(x, m):
    return x if isinstance(x, int) else pl.multiple_of(x, m)


def interleave(dots, pieces):
    for i, one in enumerate(dots):
        one()
        for piece in pieces[i * len(pieces) // len(dots) : (i + 1) * len(pieces) // len(dots)]:
            piece()


def spots_kernel(n, nb, pupil, field, me_ref, pos_hbm, fwd_hbm, bwd_hbm, *refs):
    in_refs, grad_refs, aux_ref, stat_ref = refs[:n], refs[n : 2 * n], refs[2 * n], refs[2 * n + 1]
    phase_s, amp_s, cot_s, pg_s, part_s, pos_ref, fwd_ref, bwd_ref, sems, *per_tile = refs[2 * n + 2 :]
    e_s, x_s, p_s, y_s, g_s = (per_tile[k * nb : (k + 1) * nb] for k in range(5))
    copies = [
        pltpu.make_async_copy(pos_hbm, pos_ref, sems.at[0]),
        pltpu.make_async_copy(fwd_hbm, fwd_ref, sems.at[1]),
        pltpu.make_async_copy(bwd_hbm, bwd_ref, sems.at[2]),
    ]
    for copy in copies:
        copy.start()
    width = LANES // n
    nbins = n * nb
    qp = pupil * pupil // (n * n)
    qc = field * field // (n * n)
    half, fhalf = pupil // 2, field // 2
    me = me_ref[0]
    group1 = lane_group((1, LANES), width)
    owner = [lax.rem(me + n - j, n) for j in range(n)]

    for j in range(n):
        for q in range(0, qp, 16):
            hi = in_refs[j][q : q + 16, :].astype(F32)
            lo = in_refs[j][qp + q : qp + q + 16, :].astype(F32)
            am = in_refs[j][2 * qp + q : 2 * qp + q + 16, :].astype(F32)
            turned = [(a * qp + q) % pupil >= half for a in range(n)]
            for src, dst in ((hi + lo, phase_s), (am, amp_s)):
                ways = {
                    way: spread_groups(reverse_rows(src) if way else src, n, width)
                    for way in set(turned)
                }
                for a in range(n):
                    line = (a * qp + q) // pupil * pupil + (half if turned[a] else 0)
                    part = (a * qp + q) % half
                    part = half - 16 - part if turned[a] else part
                    at = pl.multiple_of(owner[j] * (n * qp) + line + part, 16)
                    dst[pl.ds(at, 16), :] = ways[turned[a]][a]

    per = qc // field
    low = [owner[j] < n // 2 for j in range(n)]
    sign = [jnp.where(low[j], 0, 1) for j in range(n)]

    def place(j, i, q):
        at = 3 * qp + i * field + q
        raw = in_refs[j][at : at + 16, :].astype(F32)
        raw = reverse_rows(raw) if q >= fhalf else raw
        col = field - 16 - q if q >= fhalf else q
        for a, cot in enumerate(spread_groups(raw, n, width)):
            k1 = (owner[j] * n + a) * per + i
            line = jnp.where(low[j], k1, field - 1 - k1)
            at = pl.multiple_of(line * fhalf + col, 16)
            cot_s[sign[j], int(q >= fhalf), pl.ds(at, 16), :] = cot

    prof, wgt = [], []
    for t in range(nb):
        p_row, w_row = jnp.zeros((1, LANES), F32), jnp.zeros((1, LANES), F32)
        for j in range(n):
            extra = in_refs[j][3 * qp + qc :, :].astype(F32)
            rows = [extra[6 * t + i : 6 * t + i + 1, :] for i in range(6)]
            p_row = jnp.where(group1 == owner[j], rows[0] + rows[1] + rows[2], p_row)
            w_row = jnp.where(group1 == owner[j], rows[3] + rows[4] + rows[5], w_row)
        prof.append(p_row)
        wgt.append(w_row)
    total = sum(prof)
    step = n // 2
    while step >= 1:
        total = total + roll(total, step * width)
        step //= 2
    coef = [2.0 / (pupil * pupil) * prof[t] * wgt[t] / total for t in range(nb)]
    aux = jnp.zeros(aux_ref.shape, F32)
    row = lax.broadcasted_iota(jnp.int32, aux_ref.shape, 0)
    for t in range(nb):
        aux = jnp.where(row == nb + t, prof[t], aux)
        aux = jnp.where(row == 2 * nb + t, wgt[t], aux)
    aux_ref[...] = jnp.where(row == 3 * nb, total, aux)

    copies[0].wait()
    pos = pos_ref[...]
    near = jnp.zeros_like(pos)
    for d, one in enumerate(spread_groups(pos, n, width)):
        near = jnp.where(me == d, one, near)
    shift = math.pi / field
    tilt_x, tilt_y = [], []
    for t in range(nb):
        kappa = ELONG * (2.0 * (group1 * nb + t).astype(F32) / (nbins - 1) - 1.0)
        tilt_x.append(kappa * near[0:1, :] + shift)
        tilt_y.append(kappa * near[1:2, :] + shift)

    row = lax.broadcasted_iota(jnp.int32, (pupil, LANES), 0)
    u_rows = jnp.where(row < half, row, pupil + half - 1 - row).astype(F32) - (pupil - 1) / 2.0
    lean = [u_rows * tilt_x[t] for t in range(nb)]

    def fields(t, i):
        at16 = multiple(i * half, half)
        found = []
        for r in (i, pupil - 1 - i):
            at = multiple(r * pupil, pupil)
            v = (float(r) if isinstance(r, int) else r.astype(F32)) - (pupil - 1) / 2.0
            am = amp_s[pl.ds(at, pupil), :]
            sin_v, cos_v = sincos(phase_s[pl.ds(at, pupil), :] + (lean[t] + v * tilt_y[t]))
            one = (am * cos_v, am * sin_v)
            for k in range(2):
                e_s[t][k, pl.ds(at, pupil), :] = one[k]
            found.append(one)
        for k in range(2):
            even, odd = found[1][k] + found[0][k], found[1][k] - found[0][k]
            classes = (
                even[half:] + even[:half],
                odd[half:] + odd[:half],
                even[half:] - even[:half],
                odd[half:] - odd[:half],
            )
            lanes = pl.ds(k * LANES, LANES)
            for c, x in enumerate(classes):
                hi, lo = split(x)
                x_s[t][c, 0, pl.ds(at16, half), lanes] = hi
                x_s[t][c, 1, pl.ds(at16, half), lanes] = lo

    depth = half * half
    rows_all = fhalf * fhalf
    chunk = min(CHUNK, rows_all)

    def forward(t, c, m):
        rows = pl.ds(m * chunk, chunk)
        p_s[t][c, rows, :] = dot_three(fwd_ref[c, rows, :], depth, x_s[t][c, 0], x_s[t][c, 1])

    def weigh(t, i):
        rows = pl.ds(i * 16, 16)
        cot = [cot_s[a, b, rows, :] for a in range(2) for b in range(2)]
        re = [p_s[t][c, rows, pl.ds(0, LANES)] for c in range(4)]
        im = [p_s[t][c, rows, pl.ds(LANES, LANES)] for c in range(4)]
        s0, s1, s2, s3 = re[0] + im[1], re[0] - im[1], im[2] - re[3], im[2] + re[3]
        y = [cot[0] * (s0 + s2), cot[1] * (s0 - s2), cot[2] * (s1 + s3), cot[3] * (s1 - s3)]
        s0, s1, s2, s3 = im[0] - re[1], im[0] + re[1], re[2] + im[3], re[2] - im[3]
        z = [cot[0] * (s0 - s2), cot[1] * (s0 + s2), cot[2] * (s1 - s3), cot[3] * (s1 + s3)]
        yp, ym, yd, ye = y[0] + y[1], y[2] + y[3], y[0] - y[1], y[2] - y[3]
        zp, zm, zd, ze = z[0] + z[1], z[2] + z[3], z[0] - z[1], z[2] - z[3]
        back = (
            (yp + ym, zp + zm),
            (zm - zp, yp - ym),
            (-ze - zd, yd + ye),
            (ye - yd, ze - zd),
        )
        for c in range(4):
            for k in range(2):
                hi, lo = split(back[c][k])
                lanes = pl.ds(k * LANES, LANES)
                y_s[t][c, 0, rows, lanes] = hi
                y_s[t][c, 1, rows, lanes] = lo

    def backward(t, c):
        high = jnp.dot(bwd_ref[c], y_s[t][c, 0], preferred_element_type=F32)
        low = jnp.dot(bwd_ref[c, :depth, :], y_s[t][c, 1], preferred_element_type=F32)
        g_s[t][c] = high[:depth] + (high[depth:] + low)

    def products(t, i, stat):
        at16 = multiple(i * half, half)
        found = []
        for k in range(2):
            g = [g_s[t][c, pl.ds(at16, half), pl.ds(k * LANES, LANES)] for c in range(4)]
            even = jnp.concatenate([g[0] - g[2], g[0] + g[2]], axis=0)
            odd = jnp.concatenate([g[1] - g[3], g[1] + g[3]], axis=0)
            found.append((even - odd, even + odd))
        for which, r in enumerate((i, pupil - 1 - i)):
            rows = pl.ds(multiple(r * pupil, pupil), pupil)
            e_re, e_im = e_s[t][0, rows, :], e_s[t][1, rows, :]
            g_re, g_im = found[0][which], found[1][which]
            stat = stat + (e_re * g_re + e_im * g_im)
            grad = coef[t] * (e_re * g_im - e_im * g_re)
            if t:
                grad = grad + part_s[rows, :]
            if t < nb - 1:
                part_s[rows, :] = grad
                continue
            step = n // 2
            while step >= 1:
                grad = grad + roll(grad, step * width)
                step //= 2
            pg_s[rows, :] = jnp.concatenate([grad[:half], reverse_rows(grad[half:])], axis=0)
        return stat

    stats = [jnp.zeros((pupil, LANES), F32) for _ in range(nb)]

    def early_products(t, i):
        stats[t] = products(t, i, stats[t])

    work = functools.partial
    places = [
        work(place, j, i, q) for j in range(n) for i in range(per) for q in range(0, field, 16)
    ]
    lax.fori_loop(0, half, lambda i, carry: fields(0, i) or carry, 0)
    copies[1].wait()
    for t in range(nb):
        pieces = places if t == 0 else []
        if t < nb - 1:
            pieces = [work(fields, t + 1, i) for i in range(half)] + pieces
        elif nb > 1:
            pieces = [work(weigh, 0, i) for i in range(rows_all // 16)] + pieces
        interleave(
            [work(forward, t, c, m) for c in range(4) for m in range(rows_all // chunk)], pieces
        )
    if nb == 1:
        for i in range(rows_all // 16):
            weigh(0, i)
    copies[2].wait()
    for t in range(nb):
        if t < nb - 1:
            pieces = [work(weigh, t + 1, i) for i in range(rows_all // 16)]
        else:
            pieces = [work(early_products, b, i) for b in range(nb - 1) for i in range(half)]
        interleave([work(backward, t, c) for c in range(4)], pieces)
    stats[-1] = lax.fori_loop(0, half, lambda i, stat: products(nb - 1, i, stat), stats[-1])

    lane = lax.broadcasted_iota(jnp.int32, (1, LANES), 1)
    sums = jnp.zeros((1, LANES), F32)
    for t in range(nb):
        stat = jnp.sum(stats[t], axis=0, keepdims=True) * (1.0 / (pupil * pupil))
        step = 1
        while step < width:
            stat = stat + roll(stat, step)
            step *= 2
        sums = jnp.where(lane % width == width - 1 - t, roll(stat, -t), sums)
    stat_ref[...] = jnp.broadcast_to(sums, stat_ref.shape)
    group = lane_group((8, LANES), width)
    for k, ref in enumerate(grad_refs):
        d = lax.rem(me + k, n)
        for q in range(0, qp, 8):
            out = jnp.zeros((8, LANES), F32)
            for a in range(n):
                at = pl.multiple_of((d * n + a) * qp + q, 8)
                out = jnp.where(group == a, pg_s[pl.ds(at, 8), :], out)
            ref[q : q + 8, :] = out


def gradient_kernel(n, me_ref, *refs):
    width = LANES // n
    out_ref = refs[n]
    qp = out_ref.shape[0] // n
    turn = me_ref[0] * width
    for q in range(0, qp, 8):
        parts = [refs[(n - i) % n][q : q + 8, :] for i in range(n)]
        for a, block in enumerate(swap_groups(parts, width)):
            out_ref[a * qp + q : a * qp + q + 8, :] = pltpu.roll(block, turn, 1)


def profile_kernel(n, nb, nsub_all, me_ref, aux_ref, stat_ref, prof_ref):
    width = LANES // n
    lane = lax.broadcasted_iota(jnp.int32, (1, LANES), 1)
    stat = jnp.sum(stat_ref[...], axis=0, keepdims=True)
    aux = aux_ref[...]
    total = jnp.max(aux[3 * nb : 3 * nb + 1, :])
    centre = jnp.zeros((1, LANES), F32)
    own = []
    for t in range(nb):
        prof, wgt = aux[nb + t : nb + t + 1], aux[2 * nb + t : 2 * nb + t + 1]
        term = stat * wgt
        centre += jnp.where(lane % width == width - 1 - t, term * prof, 0.0)
        own.append(jnp.sum(jnp.where(lane == (me_ref[0] + 1) * width - 1 - t, term, 0.0)))
    centre = jnp.sum(centre)
    for t in range(nb):
        prof_ref[t] = (own[t] / total - centre / (total * total)) / nsub_all


def local(cotangent, amplitude, phase, position, profile, alt_weight):
    n = lax.axis_size("alt")
    n_sub = lax.axis_size("sub")
    nsub_all = n_sub * phase.shape[1]
    nb = profile.shape[0]
    pupil = math.isqrt(n * phase.shape[0])
    field = math.isqrt(n * cotangent.shape[0])
    qp = phase.shape[0] // n
    qc = cotangent.shape[0] // n
    extra = -(-6 * nb // 16) * 16
    me = lax.axis_index("alt").astype(jnp.int32).reshape(1)
    smem = pl.BlockSpec(memory_space=pltpu.SMEM)
    vmem = pl.BlockSpec(memory_space=pltpu.VMEM)
    hbm = pl.BlockSpec(memory_space=pltpu.HBM)
    params = pltpu.CompilerParams(vmem_limit_bytes=VMEM_LIMIT)

    def keep(*arrays):
        return [pltpu.with_memory_space_constraint(x, pltpu.HBM) for x in arrays]

    def exchange(blocks):
        return [blocks[0]] + [
            lax.ppermute(blocks[j], "alt", [(i, (i + j) % n) for i in range(n)])
            for j in range(1, n)
        ]

    blocks = pl.pallas_call(
        functools.partial(pack_kernel, n, nb),
        out_shape=[jax.ShapeDtypeStruct((3 * qp + qc + extra, LANES), BF16)] * n,
        in_specs=[smem] + [hbm] * 5,
        out_specs=[vmem] * n,
        scratch_shapes=[
            pltpu.SMEM(profile.shape, F32),
            pltpu.SMEM(alt_weight.shape, F32),
            pltpu.VMEM(amplitude.shape, BF16),
            pltpu.VMEM(phase.shape, F32),
            pltpu.VMEM(cotangent.shape, BF16),
            pltpu.SemaphoreType.DMA((5,)),
        ],
        compiler_params=params,
        name="pack",
    )(me, *keep(profile, alt_weight, amplitude, phase, cotangent))
    blocks = exchange(blocks)

    fwd, bwd = (jnp.asarray(x) for x in tables(pupil, field))
    depth = pupil * pupil // 4
    rows_all = field * field // 4
    aux_rows = -(-(3 * nb + 1) // 8) * 8
    *grads, aux, stat = pl.pallas_call(
        functools.partial(spots_kernel, n, nb, pupil, field),
        out_shape=[jax.ShapeDtypeStruct((qp, LANES), F32)] * n
        + [jax.ShapeDtypeStruct((rows, LANES), F32) for rows in (aux_rows, n_sub * n)],
        in_specs=[smem] + [hbm] * 3 + [vmem] * n,
        out_specs=[vmem] * (n + 2),
        scratch_shapes=[
            pltpu.VMEM((pupil * pupil, LANES), F32),
            pltpu.VMEM((pupil * pupil, LANES), F32),
            pltpu.VMEM((2, 2, rows_all, LANES), F32),
            pltpu.VMEM((pupil * pupil, LANES), F32),
            pltpu.VMEM((pupil * pupil, LANES), F32),
            pltpu.VMEM(position.shape, F32),
            pltpu.VMEM(fwd.shape, BF16),
            pltpu.VMEM(bwd.shape, BF16),
            pltpu.SemaphoreType.DMA((3,)),
        ]
        + [pltpu.VMEM((2, pupil * pupil, LANES), F32)] * nb
        + [pltpu.VMEM((4, 2, depth, 2 * LANES), BF16)] * nb
        + [pltpu.VMEM((4, rows_all, 2 * LANES), F32)] * nb
        + [pltpu.VMEM((4, 2, rows_all, 2 * LANES), BF16)] * nb
        + [pltpu.VMEM((4, depth, 2 * LANES), F32)] * nb,
        compiler_params=params,
        name="spots",
    )(me, *keep(position, fwd, bwd), *blocks)
    stat = lax.all_to_all(stat, ("sub", "alt"), 0, 0, tiled=True)
    grads = exchange(grads)
    phase_grad = pl.pallas_call(
        functools.partial(gradient_kernel, n),
        out_shape=jax.ShapeDtypeStruct(phase.shape, F32),
        in_specs=[smem] + [vmem] * n,
        out_specs=vmem,
        compiler_params=params,
        name="gradient",
    )(me, *grads)
    profile_grad = pl.pallas_call(
        functools.partial(profile_kernel, n, nb, nsub_all),
        out_shape=jax.ShapeDtypeStruct(profile.shape, F32),
        in_specs=[smem, vmem, vmem],
        out_specs=smem,
        compiler_params=params,
        name="profile",
    )(me, aux, stat)
    return phase_grad, profile_grad


def solution(mesh):
    placed = (P("alt", "sub"), P("alt", "sub"), P("alt", "sub"), P(None, "sub"), P("alt"), P("alt"))
    return jax.shard_map(
        local, mesh=mesh, in_specs=placed, out_specs=(P("alt", "sub"), P("alt")), check_vma=False
    )
```

```python
import functools
import math

import jax
import jax.numpy as jnp
import ml_dtypes
import numpy as np
from jax import lax
from jax.experimental import pallas as pl
from jax.experimental.pallas import tpu as pltpu
from jax.sharding import PartitionSpec as P

ELONG = 0.75
LANES = 128
VMEM_LIMIT = 52 * 1024 * 1024
F32 = jnp.float32
BF16 = jnp.bfloat16


CHUNK = 1024


def halves(pupil, field, fun):
    freq = np.arange(field // 2) + 0.5
    place = (pupil - 1) / 2.0 - np.arange(pupil // 2)
    return fun(2.0 * np.pi / field * np.outer(freq, place))


def hi_lo(matrix):
    hi = matrix.astype(np.float32).astype(ml_dtypes.bfloat16)
    lo = (matrix - hi.astype(np.float64)).astype(np.float32).astype(ml_dtypes.bfloat16)
    return np.concatenate([hi, lo], axis=1)


def tables(pupil, field):
    fun = (np.cos, np.sin)
    fwd, bwd = [], []
    for b in range(2):
        for a in range(2):
            t = np.kron(halves(pupil, field, fun[a]), halves(pupil, field, fun[b]))
            fwd.append(hi_lo(t))
            bwd.append(np.concatenate(np.split(hi_lo(t.T), 2, axis=1), axis=0))
    return np.stack(fwd), np.stack(bwd)


def split(x):
    hi = x.astype(BF16)
    return hi, (x - hi.astype(F32)).astype(BF16)


def dot_three(table, depth, hi, lo):
    wide = jnp.concatenate([table, table[:, :depth]], axis=1)
    return jnp.dot(wide, jnp.concatenate([hi, hi, lo], axis=0), preferred_element_type=F32)


def lane_group(shape, width):
    return lax.broadcasted_iota(jnp.int32, shape, len(shape) - 1) // width


def roll(x, shift):
    return pltpu.roll(x, shift % LANES, x.ndim - 1)


def swap_groups(blocks, width):
    n = len(blocks)
    blocks = list(blocks)
    group = lane_group(blocks[0].shape, width)
    step = 1
    while step < n:
        low = (group & step) == 0
        for i in range(n):
            if i & step:
                continue
            j = i + step
            a, b = blocks[i], blocks[j]
            blocks[i] = jnp.where(low, a, roll(b, step * width))
            blocks[j] = jnp.where(low, roll(a, -step * width), b)
        step *= 2
    return blocks


def spread_groups(x, n, width):
    group = lane_group(x.shape, width)
    out = [x]
    step = n // 2
    while step >= 1:
        low = (group & step) == 0
        made = []
        for y in out:
            up, down = roll(y, step * width), roll(y, -step * width)
            made.append(jnp.where(low, y, up))
            made.append(jnp.where(low, down, y))
        out = made
        step //= 2
    return out


def reverse_rows(x):
    row = lax.broadcasted_iota(jnp.int32, (8, LANES), 0)
    parts = []
    for i in range(x.shape[0] - 8, -1, -8):
        y = pltpu.roll(x[i : i + 8], 4, 0)
        y = jnp.where((row & 2) == 0, pltpu.roll(y, 6, 0), pltpu.roll(y, 2, 0))
        y = jnp.where((row & 1) == 0, pltpu.roll(y, 7, 0), pltpu.roll(y, 1, 0))
        parts.append(y)
    return jnp.concatenate(parts, axis=0)


def pack_kernel(n, nb, me_ref, profile_hbm, weight_hbm, amp_hbm, phase_hbm, cot_hbm, *refs):
    out_refs = refs[:n]
    profile_ref, weight_ref, amp_ref, phase_ref, cot_ref, sems = refs[n:]
    pairs = (
        (phase_hbm, phase_ref),
        (amp_hbm, amp_ref),
        (profile_hbm, profile_ref),
        (weight_hbm, weight_ref),
        (cot_hbm, cot_ref),
    )
    copies = [pltpu.make_async_copy(src, dst, sems.at[i]) for i, (src, dst) in enumerate(pairs)]
    for copy in copies:
        copy.start()
    width = LANES // n
    qp = phase_ref.shape[0] // n
    qc = cot_ref.shape[0] // n
    turn = lax.rem(n - me_ref[0], n) * width
    for copy in copies:
        copy.wait()
    for q in range(0, qp, 16):
        parts = [pltpu.roll(phase_ref[a * qp + q : a * qp + q + 16, :], turn, 1) for a in range(n)]
        for j, block in enumerate(swap_groups(parts, width)):
            hi, lo = split(block)
            out_refs[j][q : q + 16, :] = hi
            out_refs[j][qp + q : qp + q + 16, :] = lo
    for q in range(0, qp, 16):
        parts = [
            pltpu.roll(amp_ref[a * qp + q : a * qp + q + 16, :].astype(F32), turn, 1)
            for a in range(n)
        ]
        for j, block in enumerate(swap_groups(parts, width)):
            out_refs[j][2 * qp + q : 2 * qp + q + 16, :] = block.astype(BF16)

    def step(i, carry):
        at = pl.multiple_of(i * 16, 16)
        parts = [
            pltpu.roll(cot_ref[pl.ds(a * qc + at, 16), :].astype(F32), turn, 1) for a in range(n)
        ]
        for j, block in enumerate(swap_groups(parts, width)):
            out_refs[j][pl.ds(3 * qp + at, 16), :] = block.astype(BF16)
        return carry

    lax.fori_loop(0, qc // 16, step, 0, unroll=4)
    base = 3 * qp + qc
    rows = out_refs[0].shape[0] - base
    row = lax.broadcasted_iota(jnp.int32, (rows, LANES), 0)
    extra = jnp.zeros((rows, LANES), F32)
    for j in range(nb):
        for k, ref in enumerate((profile_ref, weight_ref)):
            value = jnp.full((rows, LANES), ref[j], F32)
            for part in range(3):
                piece = value.astype(BF16).astype(F32)
                extra = jnp.where(row == (2 * j + k) * 3 + part, piece, extra)
                value = value - piece
    for j in range(n):
        out_refs[j][base:, :] = extra.astype(BF16)


def sincos(x):
    turns = jnp.round(x * (2.0 / math.pi))
    r = x - turns * 1.5703125
    r = r - turns * 4.838267948966e-4
    r2 = r * r
    s = r + r * r2 * (-1.6666654611e-1 + r2 * (8.3321608736e-3 + r2 * -1.9515295891e-4))
    c = (1.0 - 0.5 * r2) + r2 * r2 * (
        4.166664568298827e-2 + r2 * (-1.388731625493765e-3 + r2 * 2.443315711809948e-5)
    )
    quad = turns.astype(jnp.int32)
    odd = (quad & 1) != 0
    sin_v = jnp.where(odd, c, s)
    cos_v = jnp.where(odd, s, c)
    sin_v = jnp.where((quad & 2) != 0, -sin_v, sin_v)
    cos_v = jnp.where(((quad + 1) & 2) != 0, -cos_v, cos_v)
    return sin_v, cos_v


def multiple(x, m):
    return x if isinstance(x, int) else pl.multiple_of(x, m)


def interleave(dots, pieces):
    for i, one in enumerate(dots):
        one()
        for piece in pieces[i * len(pieces) // len(dots) : (i + 1) * len(pieces) // len(dots)]:
            piece()


def spots_kernel(n, nb, pupil, field, me_ref, pos_hbm, fwd_hbm, bwd_hbm, *refs):
    in_refs, grad_refs, aux_ref, stat_ref = refs[:n], refs[n : 2 * n], refs[2 * n], refs[2 * n + 1]
    phase_s, amp_s, cot_s, pg_s, part_s, pos_ref, fwd_ref, bwd_ref, sems, *per_tile = refs[2 * n + 2 :]
    e_s, x_s, p_s, y_s, g_s = (per_tile[k * nb : (k + 1) * nb] for k in range(5))
    copies = [
        pltpu.make_async_copy(pos_hbm, pos_ref, sems.at[0]),
        pltpu.make_async_copy(fwd_hbm, fwd_ref, sems.at[1]),
        pltpu.make_async_copy(bwd_hbm, bwd_ref, sems.at[2]),
    ]
    for copy in copies:
        copy.start()
    width = LANES // n
    nbins = n * nb
    qp = pupil * pupil // (n * n)
    qc = field * field // (n * n)
    half, fhalf = pupil // 2, field // 2
    me = me_ref[0]
    group1 = lane_group((1, LANES), width)
    owner = [lax.rem(me + n - j, n) for j in range(n)]

    for j in range(n):
        for q in range(0, qp, 16):
            hi = in_refs[j][q : q + 16, :].astype(F32)
            lo = in_refs[j][qp + q : qp + q + 16, :].astype(F32)
            am = in_refs[j][2 * qp + q : 2 * qp + q + 16, :].astype(F32)
            turned = [(a * qp + q) % pupil >= half for a in range(n)]
            for src, dst in ((hi + lo, phase_s), (am, amp_s)):
                ways = {
                    way: spread_groups(reverse_rows(src) if way else src, n, width)
                    for way in set(turned)
                }
                for a in range(n):
                    line = (a * qp + q) // pupil * pupil + (half if turned[a] else 0)
                    part = (a * qp + q) % half
                    part = half - 16 - part if turned[a] else part
                    at = pl.multiple_of(owner[j] * (n * qp) + line + part, 16)
                    dst[pl.ds(at, 16), :] = ways[turned[a]][a]

    per = qc // field
    low = [owner[j] < n // 2 for j in range(n)]
    sign = [jnp.where(low[j], 0, 1) for j in range(n)]

    def place(j, i, q):
        at = 3 * qp + i * field + q
        raw = in_refs[j][at : at + 16, :].astype(F32)
        raw = reverse_rows(raw) if q >= fhalf else raw
        col = field - 16 - q if q >= fhalf else q
        for a, cot in enumerate(spread_groups(raw, n, width)):
            k1 = (owner[j] * n + a) * per + i
            line = jnp.where(low[j], k1, field - 1 - k1)
            at = pl.multiple_of(line * fhalf + col, 16)
            cot_s[sign[j], int(q >= fhalf), pl.ds(at, 16), :] = cot

    prof, wgt = [], []
    for t in range(nb):
        p_row, w_row = jnp.zeros((1, LANES), F32), jnp.zeros((1, LANES), F32)
        for j in range(n):
            extra = in_refs[j][3 * qp + qc :, :].astype(F32)
            rows = [extra[6 * t + i : 6 * t + i + 1, :] for i in range(6)]
            p_row = jnp.where(group1 == owner[j], rows[0] + rows[1] + rows[2], p_row)
            w_row = jnp.where(group1 == owner[j], rows[3] + rows[4] + rows[5], w_row)
        prof.append(p_row)
        wgt.append(w_row)
    total = sum(prof)
    step = n // 2
    while step >= 1:
        total = total + roll(total, step * width)
        step //= 2
    coef = [2.0 / (pupil * pupil) * prof[t] * wgt[t] / total for t in range(nb)]
    aux = jnp.zeros(aux_ref.shape, F32)
    row = lax.broadcasted_iota(jnp.int32, aux_ref.shape, 0)
    for t in range(nb):
        aux = jnp.where(row == nb + t, prof[t], aux)
        aux = jnp.where(row == 2 * nb + t, wgt[t], aux)
    aux_ref[...] = jnp.where(row == 3 * nb, total, aux)

    copies[0].wait()
    pos = pos_ref[...]
    near = jnp.zeros_like(pos)
    for d, one in enumerate(spread_groups(pos, n, width)):
        near = jnp.where(me == d, one, near)
    shift = math.pi / field
    tilt_x, tilt_y = [], []
    for t in range(nb):
        kappa = ELONG * (2.0 * (group1 * nb + t).astype(F32) / (nbins - 1) - 1.0)
        tilt_x.append(kappa * near[0:1, :] + shift)
        tilt_y.append(kappa * near[1:2, :] + shift)

    row = lax.broadcasted_iota(jnp.int32, (pupil, LANES), 0)
    u_rows = jnp.where(row < half, row, pupil + half - 1 - row).astype(F32) - (pupil - 1) / 2.0
    lean = [u_rows * tilt_x[t] for t in range(nb)]

    def fields(t, i):
        at16 = multiple(i * half, half)
        found = []
        for r in (i, pupil - 1 - i):
            at = multiple(r * pupil, pupil)
            v = (float(r) if isinstance(r, int) else r.astype(F32)) - (pupil - 1) / 2.0
            am = amp_s[pl.ds(at, pupil), :]
            sin_v, cos_v = sincos(phase_s[pl.ds(at, pupil), :] + (lean[t] + v * tilt_y[t]))
            one = (am * cos_v, am * sin_v)
            for k in range(2):
                e_s[t][k, pl.ds(at, pupil), :] = one[k]
            found.append(one)
        for k in range(2):
            even, odd = found[1][k] + found[0][k], found[1][k] - found[0][k]
            classes = (
                even[half:] + even[:half],
                odd[half:] + odd[:half],
                even[half:] - even[:half],
                odd[half:] - odd[:half],
            )
            lanes = pl.ds(k * LANES, LANES)
            for c, x in enumerate(classes):
                hi, lo = split(x)
                x_s[t][c, 0, pl.ds(at16, half), lanes] = hi
                x_s[t][c, 1, pl.ds(at16, half), lanes] = lo

    depth = half * half
    rows_all = fhalf * fhalf
    chunk = min(CHUNK, rows_all)

    def forward(t, c, m):
        rows = pl.ds(m * chunk, chunk)
        p_s[t][c, rows, :] = dot_three(fwd_ref[c, rows, :], depth, x_s[t][c, 0], x_s[t][c, 1])

    def weigh(t, i):
        rows = pl.ds(i * 16, 16)
        cot = [cot_s[a, b, rows, :] for a in range(2) for b in range(2)]
        re = [p_s[t][c, rows, pl.ds(0, LANES)] for c in range(4)]
        im = [p_s[t][c, rows, pl.ds(LANES, LANES)] for c in range(4)]
        s0, s1, s2, s3 = re[0] + im[1], re[0] - im[1], im[2] - re[3], im[2] + re[3]
        y = [cot[0] * (s0 + s2), cot[1] * (s0 - s2), cot[2] * (s1 + s3), cot[3] * (s1 - s3)]
        s0, s1, s2, s3 = im[0] - re[1], im[0] + re[1], re[2] + im[3], re[2] - im[3]
        z = [cot[0] * (s0 - s2), cot[1] * (s0 + s2), cot[2] * (s1 - s3), cot[3] * (s1 + s3)]
        yp, ym, yd, ye = y[0] + y[1], y[2] + y[3], y[0] - y[1], y[2] - y[3]
        zp, zm, zd, ze = z[0] + z[1], z[2] + z[3], z[0] - z[1], z[2] - z[3]
        back = (
            (yp + ym, zp + zm),
            (zm - zp, yp - ym),
            (-ze - zd, yd + ye),
            (ye - yd, ze - zd),
        )
        for c in range(4):
            for k in range(2):
                hi, lo = split(back[c][k])
                lanes = pl.ds(k * LANES, LANES)
                y_s[t][c, 0, rows, lanes] = hi
                y_s[t][c, 1, rows, lanes] = lo

    def backward(t, c):
        high = jnp.dot(bwd_ref[c], y_s[t][c, 0], preferred_element_type=F32)
        low = jnp.dot(bwd_ref[c, :depth, :], y_s[t][c, 1], preferred_element_type=F32)
        g_s[t][c] = high[:depth] + (high[depth:] + low)

    def products(t, i, stat):
        at16 = multiple(i * half, half)
        found = []
        for k in range(2):
            g = [g_s[t][c, pl.ds(at16, half), pl.ds(k * LANES, LANES)] for c in range(4)]
            even = jnp.concatenate([g[0] - g[2], g[0] + g[2]], axis=0)
            odd = jnp.concatenate([g[1] - g[3], g[1] + g[3]], axis=0)
            found.append((even - odd, even + odd))
        for which, r in enumerate((i, pupil - 1 - i)):
            rows = pl.ds(multiple(r * pupil, pupil), pupil)
            e_re, e_im = e_s[t][0, rows, :], e_s[t][1, rows, :]
            g_re, g_im = found[0][which], found[1][which]
            stat = stat + (e_re * g_re + e_im * g_im)
            grad = coef[t] * (e_re * g_im - e_im * g_re)
            if t:
                grad = grad + part_s[rows, :]
            if t < nb - 1:
                part_s[rows, :] = grad
                continue
            step = n // 2
            while step >= 1:
                grad = grad + roll(grad, step * width)
                step //= 2
            pg_s[rows, :] = jnp.concatenate([grad[:half], reverse_rows(grad[half:])], axis=0)
        return stat

    stats = [jnp.zeros((pupil, LANES), F32) for _ in range(nb)]

    def early_products(t, i):
        stats[t] = products(t, i, stats[t])

    work = functools.partial
    places = [
        work(place, j, i, q) for j in range(n) for i in range(per) for q in range(0, field, 16)
    ]
    lax.fori_loop(0, half, lambda i, carry: fields(0, i) or carry, 0, unroll=2)
    copies[1].wait()
    for t in range(nb):
        pieces = places if t == 0 else []
        if t < nb - 1:
            pieces = [work(fields, t + 1, i) for i in range(half)] + pieces
        elif nb > 1:
            pieces = [work(weigh, 0, i) for i in range(rows_all // 16)] + pieces
        interleave(
            [work(forward, t, c, m) for c in range(4) for m in range(rows_all // chunk)], pieces
        )
    if nb == 1:
        for i in range(rows_all // 16):
            weigh(0, i)
    copies[2].wait()
    for t in range(nb):
        if t < nb - 1:
            pieces = [work(weigh, t + 1, i) for i in range(rows_all // 16)]
        else:
            pieces = [work(early_products, b, i) for b in range(nb - 1) for i in range(half)]
        interleave([work(backward, t, c) for c in range(4)], pieces)
    stats[-1] = lax.fori_loop(
        0, half, lambda i, stat: products(nb - 1, i, stat), stats[-1], unroll=2
    )

    lane = lax.broadcasted_iota(jnp.int32, (1, LANES), 1)
    sums = jnp.zeros((1, LANES), F32)
    for t in range(nb):
        stat = jnp.sum(stats[t], axis=0, keepdims=True) * (1.0 / (pupil * pupil))
        step = 1
        while step < width:
            stat = stat + roll(stat, step)
            step *= 2
        sums = jnp.where(lane % width == width - 1 - t, roll(stat, -t), sums)
    stat_ref[...] = jnp.broadcast_to(sums, stat_ref.shape)
    group = lane_group((8, LANES), width)
    for k, ref in enumerate(grad_refs):
        d = lax.rem(me + k, n)
        for q in range(0, qp, 8):
            out = jnp.zeros((8, LANES), F32)
            for a in range(n):
                at = pl.multiple_of((d * n + a) * qp + q, 8)
                out = jnp.where(group == a, pg_s[pl.ds(at, 8), :], out)
            ref[q : q + 8, :] = out


def final_kernel(n, nb, nsub_all, me_ref, aux_ref, stat_ref, *refs):
    width = LANES // n
    out_ref, prof_ref = refs[n:]
    qp = out_ref.shape[0] // n
    turn = me_ref[0] * width
    for q in range(0, qp, 8):
        parts = [refs[(n - i) % n][q : q + 8, :] for i in range(n)]
        for a, block in enumerate(swap_groups(parts, width)):
            out_ref[a * qp + q : a * qp + q + 8, :] = pltpu.roll(block, turn, 1)
    lane = lax.broadcasted_iota(jnp.int32, (1, LANES), 1)
    stat = jnp.sum(stat_ref[...], axis=0, keepdims=True)
    aux = aux_ref[...]
    total = jnp.max(aux[3 * nb : 3 * nb + 1, :])
    centre = jnp.zeros((1, LANES), F32)
    own = []
    for t in range(nb):
        prof, wgt = aux[nb + t : nb + t + 1], aux[2 * nb + t : 2 * nb + t + 1]
        term = stat * wgt
        centre += jnp.where(lane % width == width - 1 - t, term * prof, 0.0)
        own.append(jnp.sum(jnp.where(lane == (me_ref[0] + 1) * width - 1 - t, term, 0.0)))
    centre = jnp.sum(centre)
    for t in range(nb):
        prof_ref[t] = (own[t] / total - centre / (total * total)) / nsub_all


def local(cotangent, amplitude, phase, position, profile, alt_weight):
    n = lax.axis_size("alt")
    n_sub = lax.axis_size("sub")
    nsub_all = n_sub * phase.shape[1]
    nb = profile.shape[0]
    pupil = math.isqrt(n * phase.shape[0])
    field = math.isqrt(n * cotangent.shape[0])
    qp = phase.shape[0] // n
    qc = cotangent.shape[0] // n
    extra = -(-6 * nb // 16) * 16
    me = lax.axis_index("alt").astype(jnp.int32).reshape(1)
    smem = pl.BlockSpec(memory_space=pltpu.SMEM)
    vmem = pl.BlockSpec(memory_space=pltpu.VMEM)
    hbm = pl.BlockSpec(memory_space=pltpu.HBM)
    params = pltpu.CompilerParams(vmem_limit_bytes=VMEM_LIMIT)

    def keep(*arrays):
        return [pltpu.with_memory_space_constraint(x, pltpu.HBM) for x in arrays]

    def exchange(blocks):
        return [blocks[0]] + [
            lax.ppermute(blocks[j], "alt", [(i, (i + j) % n) for i in range(n)])
            for j in range(1, n)
        ]

    blocks = pl.pallas_call(
        functools.partial(pack_kernel, n, nb),
        out_shape=[jax.ShapeDtypeStruct((3 * qp + qc + extra, LANES), BF16)] * n,
        in_specs=[smem] + [hbm] * 5,
        out_specs=[vmem] * n,
        scratch_shapes=[
            pltpu.SMEM(profile.shape, F32),
            pltpu.SMEM(alt_weight.shape, F32),
            pltpu.VMEM(amplitude.shape, BF16),
            pltpu.VMEM(phase.shape, F32),
            pltpu.VMEM(cotangent.shape, BF16),
            pltpu.SemaphoreType.DMA((5,)),
        ],
        compiler_params=params,
        name="pack",
    )(me, *keep(profile, alt_weight, amplitude, phase, cotangent))
    blocks = exchange(blocks)

    fwd, bwd = (jnp.asarray(x) for x in tables(pupil, field))
    depth = pupil * pupil // 4
    rows_all = field * field // 4
    aux_rows = -(-(3 * nb + 1) // 8) * 8
    *grads, aux, stat = pl.pallas_call(
        functools.partial(spots_kernel, n, nb, pupil, field),
        out_shape=[jax.ShapeDtypeStruct((qp, LANES), F32)] * n
        + [jax.ShapeDtypeStruct((rows, LANES), F32) for rows in (aux_rows, n_sub * n)],
        in_specs=[smem] + [hbm] * 3 + [vmem] * n,
        out_specs=[vmem] * (n + 2),
        scratch_shapes=[
            pltpu.VMEM((pupil * pupil, LANES), F32),
            pltpu.VMEM((pupil * pupil, LANES), F32),
            pltpu.VMEM((2, 2, rows_all, LANES), F32),
            pltpu.VMEM((pupil * pupil, LANES), F32),
            pltpu.VMEM((pupil * pupil, LANES), F32),
            pltpu.VMEM(position.shape, F32),
            pltpu.VMEM(fwd.shape, BF16),
            pltpu.VMEM(bwd.shape, BF16),
            pltpu.SemaphoreType.DMA((3,)),
        ]
        + [pltpu.VMEM((2, pupil * pupil, LANES), F32)] * nb
        + [pltpu.VMEM((4, 2, depth, 2 * LANES), BF16)] * nb
        + [pltpu.VMEM((4, rows_all, 2 * LANES), F32)] * nb
        + [pltpu.VMEM((4, 2, rows_all, 2 * LANES), BF16)] * nb
        + [pltpu.VMEM((4, depth, 2 * LANES), F32)] * nb,
        compiler_params=params,
        name="spots",
    )(me, *keep(position, fwd, bwd), *blocks)
    stat = lax.all_to_all(stat, ("sub", "alt"), 0, 0, tiled=True)
    grads = exchange(grads)
    return pl.pallas_call(
        functools.partial(final_kernel, n, nb, nsub_all),
        out_shape=(
            jax.ShapeDtypeStruct(phase.shape, F32),
            jax.ShapeDtypeStruct(profile.shape, F32),
        ),
        in_specs=[smem, vmem, vmem] + [vmem] * n,
        out_specs=(vmem, smem),
        compiler_params=params,
        name="finish",
    )(me, aux, stat, *grads)


def solution(mesh):
    placed = (P("alt", "sub"), P("alt", "sub"), P("alt", "sub"), P(None, "sub"), P("alt"), P("alt"))
    return jax.shard_map(
        local, mesh=mesh, in_specs=placed, out_specs=(P("alt", "sub"), P("alt")), check_vma=False
    )
```
